512 devices in a mesh: gz: 8 (over x, core), xy: 64 (over y, z).
Axes of the slice: x: 4, y: 4, z: 16, core: 2. Of those that a mesh axis runs over, the one named last changes fastest.
Arguments:
- pressure_rhs: float32 [64, 2048, 512], P('gz', 'xy'), may hold values from -6 to 6
- inv_density: float32 [64, 2048, 512], P('gz', 'xy'), may hold values from 0.5 to 8
Outputs:
- pressure: float32 [64, 2048, 512], P('gz', 'xy')
- residual: float32 [64, 2048, 512], P('gz', 'xy')
The draws below stay inside these ranges and needn't reach their ends.
All inputs are finite; a program needn't handle non-finite values.
Results may differ from the reference program's by a relative error of at most 0.0002.
Values sent between devices are 32-bit elements; how exact they have to be, the bound alone decides.
A program may use at most 128 MiB of HBM per device.

```python
import math
import jax
import jax.numpy as jnp

NX = 512
LEVELS = 3
SWEEPS = 2
COARSE_SWEEPS = 8
NZ = 64
NY = 2048


def steps_of(own_key, dims, split, least, largest):
    def one(dim, blocks):
        steps = jax.random.uniform(jax.random.fold_in(jax.random.fold_in(own_key, 6), dim), (blocks,), jnp.float32, least / len(split), largest / len(split))
        return jnp.repeat(jnp.exp(steps), dims[dim] // blocks).reshape((-1,) + (1,) * (len(dims) - dim - 1))

    factor_of = one(*split[0])
    for cut in split[1:]:
        factor_of = factor_of * one(*cut)
    return factor_of


def noise(key, extent, width, most, shards=(), held_as=jnp.bfloat16):
    factor_of = steps_of(key, extent, shards, -0.22, 0.18) if shards else 1.0
    drawn = jax.random.normal(key, extent, jnp.float32) * width * factor_of
    return jnp.minimum(jnp.maximum(drawn, -most), most).astype(held_as)


def setup_inputs(seed: int = 0) -> dict:
    seeds = jax.random.split(jax.random.key(seed), 3)
    pressure_rhs = noise(seeds[0], (NZ, NY, NX), 1.0, 6.0, ((0, 8), (1, 64)), jnp.float32)
    inv_density = jnp.clip(jnp.exp(math.log(8.0) - 2.7725887 * jax.random.uniform(seeds[1], (NZ, NY, NX), jnp.float32) ** steps_of(seeds[1], (NZ, NY, NX), ((0, 8), (1, 64)), -0.2, 0.2)), 0.5, 8.0)
    return {"pressure_rhs": pressure_rhs, "inv_density": inv_density}


OMEGA = 0.8


def neighbours(padded):
    return [padded[:-2, 1:-1, 1:-1], padded[2:, 1:-1, 1:-1], padded[1:-1, :-2, 1:-1], padded[1:-1, 2:, 1:-1], padded[1:-1, 1:-1, :-2], padded[1:-1, 1:-1, 2:]]


def face_weights(padded_beta, factor):
    middle = padded_beta[1:-1, 1:-1, 1:-1]
    weights = [0.5 * (middle + beside) for beside in neighbours(padded_beta)]
    diagonal = factor * (weights[0] + weights[1] + weights[2] + weights[3] + weights[4] + weights[5])
    return weights, diagonal


def apply_operator(values, padded, weights, factor):
    summed = jnp.zeros_like(values)
    for weight, beside in zip(weights, neighbours(padded)):
        summed = summed + weight * (values - beside)
    return factor * summed


def restrict(field):
    z_cells, y_cells, x_cells = field.shape
    return field.reshape(z_cells // 2, 2, y_cells // 2, 2, x_cells // 2, 2).mean(axis=(1, 3, 5))


def prolong(field):
    return jnp.repeat(jnp.repeat(jnp.repeat(field, 2, 0), 2, 1), 2, 2)


def local_pad(values):
    return jnp.pad(values, 1)


def smooth(iterate, source, weights, diagonal, factor, repeats):
    for repeat in range(repeats):
        iterate = iterate + OMEGA * (source - apply_operator(iterate, local_pad(iterate), weights, factor)) / diagonal
    return iterate


def reference(pressure_rhs, inv_density):
    coefficients = [inv_density]
    for depth_index in range(LEVELS):
        coefficients.append(restrict(coefficients[-1]))
    operators = []
    for depth_index in range(LEVELS + 1):
        factor = 0.25 ** depth_index
        weights, diagonal = face_weights(local_pad(coefficients[depth_index]), factor)
        operators.append((weights, diagonal, factor))
    sources = [pressure_rhs]
    smoothed = []
    for depth_index in range(LEVELS):
        weights, diagonal, factor = operators[depth_index]
        source = sources[depth_index]
        iterate = smooth(jnp.zeros_like(source), source, weights, diagonal, factor, SWEEPS)
        defect = source - apply_operator(iterate, local_pad(iterate), weights, factor)
        smoothed.append(iterate)
        sources.append(restrict(defect))
    weights, diagonal, factor = operators[LEVELS]
    iterate = smooth(jnp.zeros_like(sources[LEVELS]), sources[LEVELS], weights, diagonal, factor, COARSE_SWEEPS)
    for depth_index in reversed(range(LEVELS)):
        weights, diagonal, factor = operators[depth_index]
        iterate = smoothed[depth_index] + prolong(iterate)
        iterate = smooth(iterate, sources[depth_index], weights, diagonal, factor, SWEEPS)
    weights, diagonal, factor = operators[0]
    residual = pressure_rhs - apply_operator(iterate, local_pad(iterate), weights, factor)
    return iterate, residual
```

```python
import functools

import jax
import jax.numpy as jnp
from jax import lax
from jax.experimental import pallas as pl
from jax.experimental.pallas import tpu as pltpu
from jax.sharding import PartitionSpec as P

MESH = pl.DeviceIdType.MESH
F32 = jnp.float32
LN = 128


def windows(lo, hi, rows=8):
    starts = list(range(lo, hi - rows + 1, rows))
    if starts[-1] + rows < hi:
        starts.append(hi - rows)
    return starts


def lane_of(v):
    return lax.broadcasted_iota(jnp.int32, v.shape, v.ndim - 1)


def next_x(v):
    r = pltpu.roll(v, LN - 1, axis=2)
    if v.shape[0] == 1:
        return r
    carry = jnp.concatenate([r[1:], r[:1]], axis=0)
    return jnp.where(lane_of(v) == LN - 1, carry, r)


def prev_x(v):
    r = pltpu.roll(v, 1, axis=2)
    if v.shape[0] == 1:
        return r
    carry = jnp.concatenate([r[-1:], r[:-1]], axis=0)
    return jnp.where(lane_of(v) == 0, carry, r)


def x_index(v):
    tile = lax.broadcasted_iota(jnp.int32, v.shape, 0)
    return tile * LN + lane_of(v)


def neighbour_sum(a, w, z, y, n):
    wx, wy, wz = w[0], w[1], w[2]
    ys = pl.ds(y, n)
    v = a[z, :, ys, :]
    wxc = wx[z, :, ys, :]
    acc = wxc * next_x(v) + prev_x(wxc * v)
    acc += wy[z, :, ys, :] * a[z, :, pl.ds(y + 1, n), :]
    acc += wy[z, :, pl.ds(y - 1, n), :] * a[z, :, pl.ds(y - 1, n), :]
    acc += wz[z, :, ys, :] * a[z + 1, :, ys, :]
    acc += wz[z - 1, :, ys, :] * a[z - 1, :, ys, :]
    return v, acc


def sweep(a, out, w, s, zs, yr):
    def step(z, c):
        for y in windows(*yr):
            v, acc = neighbour_sum(a, w, z, y, 8)
            ys = pl.ds(y, 8)
            out[z, :, ys, :] = 0.2 * v + w[3][z, :, ys, :] * (s[z, :, ys, :] + acc)
        return c

    lax.fori_loop(zs[0], zs[1], step, 0)


def defect(a, out, w, s, zs, yr):
    def step(z, c):
        for y in windows(*yr):
            v, acc = neighbour_sum(a, w, z, y, 8)
            ys = pl.ds(y, 8)
            out[z, :, ys, :] = s[z, :, ys, :] + (acc - w[4][z, :, ys, :] * v)
        return c

    lax.fori_loop(zs[0], zs[1], step, 0)


def weights(b, w, zs, yr, nx):
    wx, wy, wz, d, tot = w

    def step(z, c):
        for y in windows(yr[0] - 1, yr[1]):
            ys = pl.ds(y, 8)
            wy[z, :, ys, :] = 0.5 * (b[z, :, ys, :] + b[z, :, pl.ds(y + 1, 8), :])
        for y in windows(*yr):
            ys = pl.ds(y, 8)
            v = b[z, :, ys, :]
            x = x_index(v)
            up = jnp.where(x >= nx - 1, 0.0, next_x(v))
            down = jnp.where(x == 0, 0.0, prev_x(v))
            above = b[z + 1, :, ys, :]
            wx[z, :, ys, :] = jnp.where(x >= nx - 1, 0.0, 0.5 * (v + up))
            wz[z, :, ys, :] = 0.5 * (v + above)
            beside = b[z, :, pl.ds(y + 1, 8), :] + b[z, :, pl.ds(y - 1, 8), :]
            total = 3.0 * v + 0.5 * ((up + down) + beside + (above + b[z - 1, :, ys, :]))
            tot[z, :, ys, :] = total
            d[z, :, ys, :] = jnp.where(v > 0.0, 0.8 / total, 0.0)
        return c

    lax.fori_loop(zs[0], zs[1], step, 0)
    z = zs[0] - 1
    for y in windows(*yr):
        ys = pl.ds(y, 8)
        wz[z, :, ys, :] = 0.5 * (b[z, :, ys, :] + b[z + 1, :, ys, :])


def first_sweep(s, out, w, zs, yr):
    def step(z, c):
        for y in windows(*yr):
            ys = pl.ds(y, 8)
            out[z, :, ys, :] = w[3][z, :, ys, :] * s[z, :, ys, :]
        return c

    lax.fori_loop(zs[0], zs[1], step, 0)


def take(v, index):
    flat = v.reshape(-1, LN)
    return jnp.take_along_axis(flat, index(lax.broadcasted_iota(jnp.int32, flat.shape, 1)), axis=1).reshape(v.shape)


def coarsen(f, out, z_f, y_f, z_c, y_c, nz, ny, scale):
    rows = min(ny, 8)

    def step(k, c):
        for y in windows(0, ny, rows):
            even = pl.ds(y_f + 2 * y, rows, stride=2)
            odd = pl.ds(y_f + 2 * y + 1, rows, stride=2)
            z = z_f + 2 * k
            v = (f[z, :, even, :] + f[z, :, odd, :]) + (f[z + 1, :, even, :] + f[z + 1, :, odd, :])
            if scale != 1.0:
                v = v * scale
            v = v + pltpu.roll(v, LN - 1, axis=2)
            g = take(v, lambda j: lax.rem(2 * j, LN))
            low = lax.broadcasted_iota(jnp.int32, (rows, LN), 1) < LN // 2
            tiles = v.shape[0]
            for t in range(max(1, tiles // 2)):
                high = g[2 * t + 1] if tiles > 1 else jnp.zeros((rows, LN), F32)
                out[z_c + k, t, pl.ds(y_c + y, rows), :] = jnp.where(low, g[2 * t], high)
        return c

    lax.fori_loop(0, nz, step, 0)


def spread(e, out, z_c, y_c, z_o, y_o, nz, ny, tiles):
    def step(k, c):
        for y in windows(0, ny):
            v = e[z_c + k, :, pl.ds(y_c + y, 8), :]
            parts = [take(v, lambda j: j // 2)]
            if tiles > 1:
                parts.append(take(v, lambda j: LN // 2 + j // 2))
            for t in range(tiles):
                g = parts[t % 2][t // 2]
                out[z_o + k, t, pl.ds(y_o + 2 * y, 8, stride=2), :] = g
                out[z_o + k, t, pl.ds(y_o + 2 * y + 1, 8, stride=2), :] = g
        return c

    lax.fori_loop(0, nz, step, 0)


def add_spread(u, pe, out, z0, nz, yr):
    def step(k, c):
        for y in windows(*yr):
            ys = pl.ds(y, 8)
            p = pe[k, :, ys, :]
            out[z0 + 2 * k, :, ys, :] = u[z0 + 2 * k, :, ys, :] + p
            out[z0 + 2 * k + 1, :, ys, :] = u[z0 + 2 * k + 1, :, ys, :] + p
        return c

    lax.fori_loop(0, nz // 2, step, 0)


def kernel(ng, nw, nx, rhs, den, p_out, r_out,
           sb0, w0a, w0b, w0c, w0d, w0e, va, vb, vc, pe0,
           b1, s1, w1a, w1b, w1c, w1d, w1e, v1a, v1b, v1c, pe1,
           sub2, b2, s2, w2a, w2b, w2c, w2d, w2e, v2a, v2b, v2c, pe2,
           own3, b3, s3, w3a, w3b, w3c, w3d, w3e, e3a, e3b,
           in_sem, out_sem, ssem, rsem, gsem, grsem):
    gz, xy = lax.axis_index("gz"), lax.axis_index("xy")
    w0 = (w0a, w0b, w0c, w0d, w0e)
    w1 = (w1a, w1b, w1c, w1d, w1e)
    w2 = (w2a, w2b, w2c, w2d, w2e)
    w3 = (w3a, w3b, w3c, w3d, w3e)
    b0, s0 = sb0.at[1], sb0.at[0]
    H0, H1, H2, Y3 = 3, 7, 4, 12

    loads = []
    for t in range(4):
        for i, (src, dst) in enumerate(((den, b0), (rhs, s0))):
            cp = pltpu.make_async_copy(
                src.at[:, :, pl.ds(LN * t, LN)], dst.at[pl.ds(H0, 8), t, pl.ds(H0, 32), :], in_sem.at[i, t]
            )
            cp.start()
            loads.append(cp)

    def clear(ref, zs, ys):
        shape = (zs[1] - zs[0], ref.shape[-3], ys[1] - ys[0], LN)
        if len(ref.shape) == 5:
            for k in range(ref.shape[0]):
                ref[k, zs[0]:zs[1], :, ys[0]:ys[1], :] = jnp.zeros(shape, F32)
        else:
            ref[zs[0]:zs[1], :, ys[0]:ys[1], :] = jnp.zeros(shape, F32)

    for ref, h, z, y, reach in ((sb0, H0, 8, 32, 1), (vb, H0, 8, 32, 1), (b1, H1, 4, 16, 2), (s1, H1, 4, 16, 2),
                                (sub2, H2, 2, 8, 2)):
        top, rows = 2 * h + z, 2 * h + y

        @pl.when(gz < reach)
        def _(ref=ref, h=h, rows=rows):
            clear(ref, (0, h), (0, rows))

        @pl.when(gz >= ng - reach)
        def _(ref=ref, h=h, z=z, top=top, rows=rows):
            clear(ref, (h + z, top), (0, rows))

        @pl.when(xy == 0)
        def _(ref=ref, h=h, top=top):
            clear(ref, (0, top), (0, h))

        @pl.when(xy == nw - 1)
        def _(ref=ref, h=h, y=y, top=top, rows=rows):
            clear(ref, (0, top), (h + y, rows))

    for ref in (b3, s3):
        @pl.when(xy < 3)
        def _(ref=ref):
            clear(ref, (0, ng), (0, Y3))

        @pl.when(xy >= nw - 3)
        def _(ref=ref):
            clear(ref, (0, ng), (Y3 + 4, 32))

    for ref in (e3a, e3b):
        clear(ref, (0, 3), (0, 32))
        clear(ref, (3 + ng, 6 + ng), (0, 32))

    def inside(a, b):
        conds = []
        if a:
            conds += [gz + a >= 0, gz + a < ng]
        if b:
            conds += [xy + b >= 0, xy + b < nw]
        return functools.reduce(jnp.logical_and, conds)

    barrier = pltpu.get_barrier_semaphore()

    def greet(to_other):
        def body(k, c):
            for b in range(-3, 4):
                ok = jnp.logical_and(xy + b >= 0, xy + b < nw)
                if b == 0:
                    ok = jnp.logical_and(ok, k != gz)

                @pl.when(ok)
                def _(b=b):
                    to_other(k, b)
            return c

        lax.fori_loop(0, ng, body, 0)

    greet(lambda k, b: pl.semaphore_signal(barrier, inc=1, device_id=(k, xy + b), device_id_type=MESH))
    columns = 1 + jnp.minimum(xy, 3) + jnp.minimum(nw - 1 - xy, 3)
    pl.semaphore_wait(barrier, ng * columns - 1)
    for cp in loads:
        cp.wait()

    used = [0]

    def exchange(moves):
        copies = []
        for a, b, ref, src, dst in moves:
            i = used[0]
            used[0] += 1
            cp = pltpu.make_async_remote_copy(
                src_ref=ref.at[src], dst_ref=ref.at[dst], send_sem=ssem.at[i], recv_sem=rsem.at[i],
                device_id=(gz + a, xy + b), device_id_type=MESH,
            )

            @pl.when(inside(a, b))
            def _(cp=cp):
                cp.start()

            copies.append((a, b, cp))

        def wait_recv():
            for a, b, cp in copies:
                @pl.when(inside(-a, -b))
                def _(cp=cp):
                    cp.wait_recv()

        def wait_send():
            for a, b, cp in copies:
                @pl.when(inside(a, b))
                def _(cp=cp):
                    cp.wait_send()

        return wait_recv, wait_send

    def span(shift, own, h, lo_skip, width):
        if shift == 0:
            return h, h + own
        if shift > 0:
            return max(h - width, h - shift * own), min(h - lo_skip, h - (shift - 1) * own)
        return max(h + own + lo_skip, h - shift * own), min(h + own + width, h + (1 - shift) * own)

    def move(ref, a, b, own, h, wz, wy, lead=(), skip=0):
        z0, z1 = span(a, own[0], h, skip if b == 0 else 0, wz)
        y0, y1 = span(b, own[1], h, skip if a == 0 else 0, wy)
        dst = lead + (pl.ds(z0, z1 - z0), slice(None), pl.ds(y0, y1 - y0), slice(None))
        src = lead + (pl.ds(z0 + a * own[0], z1 - z0), slice(None), pl.ds(y0 + b * own[1], y1 - y0), slice(None))
        return (a, b, ref, src, dst)

    all2 = (slice(None),)
    o0, o1, o2 = (8, 32), (4, 16), (2, 8)
    signs = (-1, 1)
    moves = [move(sb0, a, 0, o0, H0, 3, 0, (1,)) for a in signs]
    moves += [move(sb0, a, 0, o0, H0, 2, 0, (0,)) for a in signs]
    moves += [move(sb0, 0, b, o0, H0, 0, 3, all2) for b in signs]
    moves += [move(sb0, a, b, o0, H0, 2, 2, all2) for a in signs for b in signs]
    got0, sent0 = exchange(moves)

    coarsen(b0, b1, H0, H0, H1, H1, 4, 16, 1.0)
    moves = [move(b1, a, 0, o1, H1, 7, 0) for a in (-1, 1, -2, 2)]
    moves += [move(b1, 0, b, o1, H1, 0, 7) for b in signs]
    moves += [move(b1, a, b, o1, H1, 7, 6) for a in signs for b in signs]
    moves += [move(b1, a, b, o1, H1, 6, 2) for a in (-2, 2) for b in signs]
    gotb1, sentb1 = exchange(moves)
    coarsen(b1, b2, H1, H1, H2, H2, 2, 8, 1.0)
    coarsen(b2, own3.at[0], H2, H2, 0, 0, 1, 4, 1.0)

    got0()
    weights(b0, w0, (1, 13), (1, 37), nx)
    first_sweep(s0, va, w0, (1, 13), (1, 37))
    sweep(va, vb, w0, s0, (3, 11), (2, 36))
    sweep(va, vb, w0, s0, (2, 3), (3, 35))
    sweep(va, vb, w0, s0, (11, 12), (3, 35))
    defect(vb, vc, w0, s0, (3, 11), (3, 35))
    coarsen(vc, s1, H0, H0, H1, H1, 4, 16, 4.0)

    moves = [move(s1, a, 0, o1, H1, 6, 0) for a in (-1, 1, -2, 2)]
    moves += [move(s1, 0, b, o1, H1, 0, 6) for b in signs]
    moves += [move(s1, a, b, o1, H1, 6, 5) for a in signs for b in signs]
    moves += [move(s1, a, b, o1, H1, 5, 1) for a in (-2, 2) for b in signs]
    gots1, sents1 = exchange(moves)

    moves = [move(vb, a, 0, o0, H0, 3, 0, skip=1) for a in signs]
    moves += [move(vb, 0, b, o0, H0, 0, 3, skip=1) for b in signs]
    moves += [move(vb, a, b, o0, H0, 2, 2) for a in signs for b in signs]
    gotu0, sentu0 = exchange(moves)

    def gather(own, ref, g):
        for b in (0, 1, -1, 2, -2, 3, -3):
            rows = pl.ds(Y3 - 4 * b, 4)

            @pl.when(jnp.logical_and(xy + b >= 0, xy + b < nw))
            def _(b=b, rows=rows):
                def body(k, c):
                    def go():
                        pltpu.make_async_remote_copy(
                            src_ref=own.at[0], dst_ref=ref.at[gz, :, rows, :], send_sem=gsem.at[g, b + 3],
                            recv_sem=grsem.at[g, b + 3], device_id=(k, xy + b), device_id_type=MESH,
                        ).start()

                    if b == 0:
                        pl.when(k != gz)(go)
                    else:
                        go()
                    return c

                lax.fori_loop(0, ng, body, 0)

        def wait(sems, sign):
            for b in (0, 1, -1, 2, -2, 3, -3):
                planes = ng - 1 if b == 0 else ng
                part = ref.at[pl.ds(0, planes), :, pl.ds(Y3 - 4 * b, 4), :]

                @pl.when(jnp.logical_and(xy + sign * b >= 0, xy + sign * b < nw))
                def _(b=b, part=part):
                    pltpu.make_async_copy(part, part, sems.at[g, b + 3]).wait()

        return lambda: wait(grsem, -1), lambda: wait(gsem, 1)

    b3[gz, :, pl.ds(Y3, 4), :] = own3[0, 0]
    gotb3, sentb3 = gather(own3.at[0], b3, 0)
    gotb1()
    weights(b1, w1, (1, 17), (1, 29), nx // 2)
    coarsen(b1, b2, 1, 1, 1, 1, 8, 14, 1.0)
    weights(b2, w2, (2, 8), (2, 14), nx // 4)

    gots1()
    first_sweep(s1, v1a, w1, (1, 17), (1, 29))
    sweep(v1a, v1b, w1, s1, (2, 16), (2, 28))
    defect(v1b, v1c, w1, s1, (3, 15), (3, 27))
    coarsen(v1c, s2, 3, 3, 2, 2, 6, 12, 4.0)
    first_sweep(s2, v2a, w2, (2, 8), (2, 14))
    sweep(v2a, v2b, w2, s2, (3, 7), (3, 13))
    defect(v2b, v2c, w2, s2, (4, 6), (4, 12))
    coarsen(v2c, own3.at[1], H2, H2, 0, 0, 1, 4, 4.0)

    s3[gz, :, pl.ds(Y3, 4), :] = own3[1, 0]
    gots3, sents3 = gather(own3.at[1], s3, 1)

    for i, ref in enumerate((b2, s2, v2b)):
        sub2[i, pl.ds(H2, 2), :, pl.ds(H2, 8), :] = ref[pl.ds(H2, 2), :, pl.ds(H2, 8), :]
    moves = [move(sub2, a, b, o2, H2, 4, 4, all2) for a in range(-2, 3) for b in (-1, 0, 1) if (a, b) != (0, 0)]
    gotsub, sentsub = exchange(moves)

    gotb3()
    R = (2, 26)
    n = R[1] - R[0]
    v = b3[:, 0, pl.ds(R[0], n), :]
    x = lane_of(v)
    zero = jnp.zeros((1, n, LN), F32)
    up = jnp.where(x >= nx // 8 - 1, 0.0, pltpu.roll(v, LN - 1, axis=2))
    down = jnp.where(x == 0, 0.0, pltpu.roll(v, 1, axis=2))
    above = jnp.concatenate([v[1:], zero], axis=0)
    below = jnp.concatenate([zero, v[:-1]], axis=0)
    north, south = b3[:, 0, pl.ds(R[0] + 1, n), :], b3[:, 0, pl.ds(R[0] - 1, n), :]
    w3a[:, pl.ds(R[0], n), :] = jnp.where(x >= nx // 8 - 1, 0.0, 0.5 * (v + up))
    w3b[:, pl.ds(R[0], n), :] = 0.5 * (v + north)
    w3e[:, pl.ds(R[0], n), :] = 0.5 * (v + south)
    w3c[pl.ds(1, ng), pl.ds(R[0], n), :] = 0.5 * (v + above)
    w3c[pl.ds(0, 1), pl.ds(R[0], n), :] = zero
    total = 3.0 * v + 0.5 * ((up + down) + (north + south) + (above + below))
    w3d[:, pl.ds(R[0], n), :] = jnp.where(v > 0.0, 0.8 / total, 0.0)
    gots3()
    e3a[pl.ds(3, ng), 0, pl.ds(R[0], n), :] = w3d[:, pl.ds(R[0], n), :] * s3[:, 0, pl.ds(R[0], n), :]
    a, out = e3a, e3b
    for lo, n in ((3, 22), (3, 22), (6, 16), (6, 16), (6, 16), (6, 16), (10, 8)):
        rows = pl.ds(lo, n)
        v = a[pl.ds(3, ng), 0, rows, :]
        wx = w3a[:, rows, :]
        acc = wx * pltpu.roll(v, LN - 1, axis=2) + pltpu.roll(wx * v, 1, axis=2)
        acc += w3b[:, rows, :] * a[pl.ds(3, ng), 0, pl.ds(lo + 1, n), :]
        acc += w3e[:, rows, :] * a[pl.ds(3, ng), 0, pl.ds(lo - 1, n), :]
        acc += w3c[pl.ds(1, ng), rows, :] * a[pl.ds(4, ng), 0, rows, :]
        acc += w3c[pl.ds(0, ng), rows, :] * a[pl.ds(2, ng), 0, rows, :]
        out[pl.ds(3, ng), 0, rows, :] = 0.2 * v + w3d[:, rows, :] * (s3[:, 0, rows, :] + acc)
        a, out = out, a

    gotsub()
    weights(sub2.at[0], w2, (1, 9), (1, 15), nx // 4)
    spread(a, pe2, gz + 1, 10, 0, 0, 5, 8, 1)
    add_spread(sub2.at[2], pe2, v2a, 0, 10, (0, 16))
    sweep(v2a, v2b, w2, sub2.at[1], (1, 9), (1, 15))
    sweep(v2b, v2a, w2, sub2.at[1], (2, 8), (2, 14))

    spread(v2a, pe1, 2, 2, 0, 3, 6, 12, 2)
    add_spread(v1b, pe1, v1a, 3, 12, (3, 27))
    sweep(v1a, v1c, w1, s1, (4, 14), (4, 26))
    sweep(v1c, v1a, w1, s1, (5, 13), (5, 25))

    spread(v1a, pe0, 5, 5, 0, 0, 8, 20, 4)
    gotu0()

    def add0(k, c):
        for y in windows(0, 38):
            va[k, :, pl.ds(y, 8), :] = vb[k, :, pl.ds(y, 8), :] + pe0[(k + 1) // 2, :, pl.ds(y + 1, 8), :]
        return c

    lax.fori_loop(0, 14, add0, 0)
    sweep(va, vc, w0, s0, (1, 13), (1, 37))
    sweep(vc, va, w0, s0, (2, 12), (2, 36))
    stores = []

    def store(src, dst, i):
        for t in range(4):
            cp = pltpu.make_async_copy(
                src.at[pl.ds(H0, 8), t, pl.ds(H0, 32), :], dst.at[:, :, pl.ds(LN * t, LN)], out_sem.at[i, t]
            )
            cp.start()
            stores.append(cp)

    store(va, p_out, 0)
    defect(va, vc, w0, s0, (3, 11), (3, 35))
    store(vc, r_out, 1)
    for wait in (sent0, sentb1, sents1, sentu0, sentb3, sents3, sentsub):
        wait()
    for cp in stores:
        cp.wait()


def solution(mesh):
    ng, nw = mesh.shape["gz"], mesh.shape["xy"]

    def block(rhs, den):
        nx = rhs.shape[2]
        f0 = pltpu.VMEM((14, 4, 40, LN), F32)
        f1 = pltpu.VMEM((18, 2, 32, LN), F32)
        f2 = pltpu.VMEM((10, 1, 16, LN), F32)
        g3 = pltpu.VMEM((ng, 1, 32, LN), F32)
        w3 = pltpu.VMEM((ng, 32, LN), F32)
        return pl.pallas_call(
            functools.partial(kernel, ng, nw, nx),
            out_shape=[jax.ShapeDtypeStruct(rhs.shape, F32)] * 2,
            in_specs=[pl.BlockSpec(memory_space=pl.ANY)] * 2,
            out_specs=[pl.BlockSpec(memory_space=pl.ANY)] * 2,
            scratch_shapes=[pltpu.VMEM((2, 14, 4, 40, LN), F32)] + [f0] * 8 + [pltpu.VMEM((8, 4, 40, LN), F32)]
            + [f1] * 10 + [pltpu.VMEM((6, 2, 32, LN), F32)]
            + [pltpu.VMEM((3, 10, 1, 16, LN), F32)] + [f2] * 10 + [pltpu.VMEM((5, 1, 16, LN), F32)]
            + [pltpu.VMEM((2, 1, 1, 4, LN), F32), g3, g3, w3, w3, pltpu.VMEM((ng + 1, 32, LN), F32), w3, w3]
            + [pltpu.VMEM((ng + 6, 1, 32, LN), F32)] * 2
            + [pltpu.SemaphoreType.DMA((2, 4))] * 2
            + [pltpu.SemaphoreType.DMA((64,))] * 2
            + [pltpu.SemaphoreType.DMA((2, 7))] * 2,
            compiler_params=pltpu.CompilerParams(
                collective_id=0, has_side_effects=True, vmem_limit_bytes=50 * 2**20
            ),
        )(rhs, den)

    spec = P("gz", "xy", None)
    return jax.shard_map(block, mesh=mesh, in_specs=(spec, spec), out_specs=(spec, spec), check_vma=False)
```

```python
import functools

import jax
import jax.numpy as jnp
from jax import lax
from jax.experimental import pallas as pl
from jax.experimental.pallas import tpu as pltpu
from jax.sharding import PartitionSpec as P

MESH = pl.DeviceIdType.MESH
F32 = jnp.float32
LN = 128


def windows(lo, hi, rows=8):
    starts = list(range(lo, hi - rows + 1, rows))
    if starts[-1] + rows < hi:
        starts.append(hi - rows)
    return starts


def lane_of(v):
    return lax.broadcasted_iota(jnp.int32, v.shape, v.ndim - 1)


def next_x(v):
    r = pltpu.roll(v, LN - 1, axis=2)
    if v.shape[0] == 1:
        return r
    carry = jnp.concatenate([r[1:], r[:1]], axis=0)
    return jnp.where(lane_of(v) == LN - 1, carry, r)


def prev_x(v):
    r = pltpu.roll(v, 1, axis=2)
    if v.shape[0] == 1:
        return r
    carry = jnp.concatenate([r[-1:], r[:-1]], axis=0)
    return jnp.where(lane_of(v) == 0, carry, r)


def x_index(v):
    tile = lax.broadcasted_iota(jnp.int32, v.shape, 0)
    return tile * LN + lane_of(v)


def neighbour_sum(a, w, z, y, n):
    wx, wy, wz = w[0], w[1], w[2]
    ys = pl.ds(y, n)
    v = a[z, :, ys, :]
    wxc = wx[z, :, ys, :]
    acc = wxc * next_x(v) + prev_x(wxc * v)
    acc += wy[z, :, ys, :] * a[z, :, pl.ds(y + 1, n), :]
    acc += wy[z, :, pl.ds(y - 1, n), :] * a[z, :, pl.ds(y - 1, n), :]
    acc += wz[z, :, ys, :] * a[z + 1, :, ys, :]
    acc += wz[z - 1, :, ys, :] * a[z - 1, :, ys, :]
    return v, acc


PLANES = {4: 4, 2: 4, 1: 16}


def planes(zs, body, tiles):
    n, u = zs[1] - zs[0], min(PLANES[tiles], zs[1] - zs[0])

    def run(z0, k):
        todo = []
        for i in range(k):
            todo += body(z0 + i)
        for ref, index, value in todo:
            ref[index] = value

    if n // u > 1:
        def step(k, c):
            run(zs[0] + k * u, u)
            return c

        lax.fori_loop(0, n // u, step, 0)
    else:
        run(zs[0], u)
    if n % u:
        run(zs[1] - n % u, n % u)


def sweep(a, out, w, s, zs, yr):
    def body(z):
        todo = []
        for y in windows(*yr):
            v, acc = neighbour_sum(a, w, z, y, 8)
            at = (z, slice(None), pl.ds(y, 8), slice(None))
            todo.append((out, at, 0.2 * v + w[3][at] * (s[at] + acc)))
        return todo

    planes(zs, body, a.shape[1])


def defect(a, out, w, s, zs, yr):
    def body(z):
        todo = []
        for y in windows(*yr):
            v, acc = neighbour_sum(a, w, z, y, 8)
            at = (z, slice(None), pl.ds(y, 8), slice(None))
            todo.append((out, at, s[at] + (acc - w[4][at] * v)))
        return todo

    planes(zs, body, a.shape[1])


def weights(b, w, zs, yr, nx):
    wx, wy, wz, d, tot = w

    def body(z):
        todo = []
        for y in windows(yr[0] - 1, yr[1]):
            at = (z, slice(None), pl.ds(y, 8), slice(None))
            todo.append((wy, at, 0.5 * (b[at] + b[z, :, pl.ds(y + 1, 8), :])))
        for y in windows(*yr):
            ys = pl.ds(y, 8)
            at = (z, slice(None), ys, slice(None))
            v = b[at]
            x = x_index(v)
            up = jnp.where(x >= nx - 1, 0.0, next_x(v))
            down = jnp.where(x == 0, 0.0, prev_x(v))
            above = b[z + 1, :, ys, :]
            todo.append((wx, at, jnp.where(x >= nx - 1, 0.0, 0.5 * (v + up))))
            todo.append((wz, at, 0.5 * (v + above)))
            beside = b[z, :, pl.ds(y + 1, 8), :] + b[z, :, pl.ds(y - 1, 8), :]
            total = 3.0 * v + 0.5 * ((up + down) + beside + (above + b[z - 1, :, ys, :]))
            todo.append((tot, at, total))
            todo.append((d, at, jnp.where(v > 0.0, 0.8 / total, 0.0)))
        return todo

    planes(zs, body, b.shape[1])
    z = zs[0] - 1
    for y in windows(*yr):
        ys = pl.ds(y, 8)
        wz[z, :, ys, :] = 0.5 * (b[z, :, ys, :] + b[z + 1, :, ys, :])


def first_sweep(s, out, w, zs, yr):
    def body(z):
        todo = []
        for y in windows(*yr):
            at = (z, slice(None), pl.ds(y, 8), slice(None))
            todo.append((out, at, w[3][at] * s[at]))
        return todo

    planes(zs, body, s.shape[1])


def take(v, index):
    flat = v.reshape(-1, LN)
    return jnp.take_along_axis(flat, index(lax.broadcasted_iota(jnp.int32, flat.shape, 1)), axis=1).reshape(v.shape)


def coarsen(f, out, z_f, y_f, z_c, y_c, nz, ny, scale):
    rows = min(ny, 8)

    def body(k):
        todo = []
        for y in windows(0, ny, rows):
            even = pl.ds(y_f + 2 * y, rows, stride=2)
            odd = pl.ds(y_f + 2 * y + 1, rows, stride=2)
            z = z_f + 2 * k
            v = (f[z, :, even, :] + f[z, :, odd, :]) + (f[z + 1, :, even, :] + f[z + 1, :, odd, :])
            if scale != 1.0:
                v = v * scale
            v = v + pltpu.roll(v, LN - 1, axis=2)
            g = take(v, lambda j: lax.rem(2 * j, LN))
            low = lax.broadcasted_iota(jnp.int32, (rows, LN), 1) < LN // 2
            tiles = v.shape[0]
            for t in range(max(1, tiles // 2)):
                high = g[2 * t + 1] if tiles > 1 else jnp.zeros((rows, LN), F32)
                todo.append((out, (z_c + k, t, pl.ds(y_c + y, rows), slice(None)), jnp.where(low, g[2 * t], high)))
        return todo

    planes((0, nz), body, max(1, f.shape[1] // 2))


def spread(e, out, z_c, y_c, z_o, y_o, nz, ny, tiles):
    def body(k):
        todo = []
        for y in windows(0, ny):
            v = e[z_c + k, :, pl.ds(y_c + y, 8), :]
            parts = [take(v, lambda j: j // 2)]
            if tiles > 1:
                parts.append(take(v, lambda j: LN // 2 + j // 2))
            for t in range(tiles):
                for i in range(2):
                    at = (z_o + k, t, pl.ds(y_o + 2 * y + i, 8, stride=2), slice(None))
                    todo.append((out, at, parts[t % 2][t // 2]))
        return todo

    planes((0, nz), body, max(1, tiles // 2))


def add_spread(u, pe, out, z0, nz, yr):
    def body(k):
        todo = []
        for y in windows(*yr):
            ys = pl.ds(y, 8)
            p = pe[k, :, ys, :]
            for i in range(2):
                at = (z0 + 2 * k + i, slice(None), ys, slice(None))
                todo.append((out, at, u[at] + p))
        return todo

    planes((0, nz // 2), body, u.shape[1])


def kernel(ng, nw, nx, rhs, den, p_out, r_out,
           sb0, w0a, w0b, w0c, w0d, w0e, va, vb, vc, pe0,
           b1, s1, w1a, w1b, w1c, w1d, w1e, v1a, v1b, v1c, pe1,
           sub2, b2, s2, w2a, w2b, w2c, w2d, w2e, v2a, v2b, v2c, pe2,
           own3, b3, s3, w3a, w3b, w3c, w3d, w3e, e3a, e3b,
           in_sem, out_sem, ssem, rsem, gsem, grsem):
    gz, xy = lax.axis_index("gz"), lax.axis_index("xy")
    w0 = (w0a, w0b, w0c, w0d, w0e)
    w1 = (w1a, w1b, w1c, w1d, w1e)
    w2 = (w2a, w2b, w2c, w2d, w2e)
    w3 = (w3a, w3b, w3c, w3d, w3e)
    b0, s0 = sb0.at[1], sb0.at[0]
    H0, H1, H2, Y3 = 3, 7, 4, 12

    loads = []
    for t in range(4):
        for i, (src, dst) in enumerate(((den, b0), (rhs, s0))):
            cp = pltpu.make_async_copy(
                src.at[:, :, pl.ds(LN * t, LN)], dst.at[pl.ds(H0, 8), t, pl.ds(H0, 32), :], in_sem.at[i, t]
            )
            cp.start()
            loads.append(cp)

    def clear(ref, zs, ys):
        shape = (zs[1] - zs[0], ref.shape[-3], ys[1] - ys[0], LN)
        if len(ref.shape) == 5:
            for k in range(ref.shape[0]):
                ref[k, zs[0]:zs[1], :, ys[0]:ys[1], :] = jnp.zeros(shape, F32)
        else:
            ref[zs[0]:zs[1], :, ys[0]:ys[1], :] = jnp.zeros(shape, F32)

    for ref, h, z, y, reach in ((sb0, H0, 8, 32, 1), (vb, H0, 8, 32, 1), (b1, H1, 4, 16, 2), (s1, H1, 4, 16, 2),
                                (sub2, H2, 2, 8, 2)):
        top, rows = 2 * h + z, 2 * h + y

        @pl.when(gz < reach)
        def _(ref=ref, h=h, rows=rows):
            clear(ref, (0, h), (0, rows))

        @pl.when(gz >= ng - reach)
        def _(ref=ref, h=h, z=z, top=top, rows=rows):
            clear(ref, (h + z, top), (0, rows))

        @pl.when(xy == 0)
        def _(ref=ref, h=h, top=top):
            clear(ref, (0, top), (0, h))

        @pl.when(xy == nw - 1)
        def _(ref=ref, h=h, y=y, top=top, rows=rows):
            clear(ref, (0, top), (h + y, rows))

    for ref in (b3, s3):
        @pl.when(xy < 3)
        def _(ref=ref):
            clear(ref, (0, ng), (0, Y3))

        @pl.when(xy >= nw - 3)
        def _(ref=ref):
            clear(ref, (0, ng), (Y3 + 4, 32))

    for ref in (e3a, e3b):
        clear(ref, (0, 3), (0, 32))
        clear(ref, (3 + ng, 6 + ng), (0, 32))

    def inside(a, b):
        conds = []
        if a:
            conds += [gz + a >= 0, gz + a < ng]
        if b:
            conds += [xy + b >= 0, xy + b < nw]
        return functools.reduce(jnp.logical_and, conds)

    barrier = pltpu.get_barrier_semaphore()

    def greet(to_other):
        def body(k, c):
            for b in range(-3, 4):
                ok = jnp.logical_and(xy + b >= 0, xy + b < nw)
                if b == 0:
                    ok = jnp.logical_and(ok, k != gz)

                @pl.when(ok)
                def _(b=b):
                    to_other(k, b)
            return c

        lax.fori_loop(0, ng, body, 0)

    greet(lambda k, b: pl.semaphore_signal(barrier, inc=1, device_id=(k, xy + b), device_id_type=MESH))
    columns = 1 + jnp.minimum(xy, 3) + jnp.minimum(nw - 1 - xy, 3)
    pl.semaphore_wait(barrier, ng * columns - 1)
    for cp in loads:
        cp.wait()

    used = [0]

    def exchange(moves):
        copies = []
        for a, b, ref, src, dst in moves:
            i = used[0]
            used[0] += 1
            cp = pltpu.make_async_remote_copy(
                src_ref=ref.at[src], dst_ref=ref.at[dst], send_sem=ssem.at[i], recv_sem=rsem.at[i],
                device_id=(gz + a, xy + b), device_id_type=MESH,
            )

            @pl.when(inside(a, b))
            def _(cp=cp):
                cp.start()

            copies.append((a, b, cp))

        def wait_recv():
            for a, b, cp in copies:
                @pl.when(inside(-a, -b))
                def _(cp=cp):
                    cp.wait_recv()

        def wait_send():
            for a, b, cp in copies:
                @pl.when(inside(a, b))
                def _(cp=cp):
                    cp.wait_send()

        return wait_recv, wait_send

    def span(shift, own, h, lo_skip, width):
        if shift == 0:
            return h, h + own
        if shift > 0:
            return max(h - width, h - shift * own), min(h - lo_skip, h - (shift - 1) * own)
        return max(h + own + lo_skip, h - shift * own), min(h + own + width, h + (1 - shift) * own)

    def move(ref, a, b, own, h, wz, wy, lead=(), skip=0):
        z0, z1 = span(a, own[0], h, skip if b == 0 else 0, wz)
        y0, y1 = span(b, own[1], h, skip if a == 0 else 0, wy)
        dst = lead + (pl.ds(z0, z1 - z0), slice(None), pl.ds(y0, y1 - y0), slice(None))
        src = lead + (pl.ds(z0 + a * own[0], z1 - z0), slice(None), pl.ds(y0 + b * own[1], y1 - y0), slice(None))
        return (a, b, ref, src, dst)

    all2 = (slice(None),)
    o0, o1, o2 = (8, 32), (4, 16), (2, 8)
    signs = (-1, 1)
    moves = [move(sb0, a, 0, o0, H0, 3, 0, (1,)) for a in signs]
    moves += [move(sb0, a, 0, o0, H0, 2, 0, (0,)) for a in signs]
    moves += [move(sb0, 0, b, o0, H0, 0, 3, all2) for b in signs]
    moves += [move(sb0, a, b, o0, H0, 2, 2, all2) for a in signs for b in signs]
    got0, sent0 = exchange(moves)

    coarsen(b0, b1, H0, H0, H1, H1, 4, 16, 1.0)
    moves = [move(b1, a, 0, o1, H1, 7, 0) for a in (-1, 1, -2, 2)]
    moves += [move(b1, 0, b, o1, H1, 0, 7) for b in signs]
    moves += [move(b1, a, b, o1, H1, 7, 6) for a in signs for b in signs]
    moves += [move(b1, a, b, o1, H1, 6, 2) for a in (-2, 2) for b in signs]
    gotb1, sentb1 = exchange(moves)
    coarsen(b1, b2, H1, H1, H2, H2, 2, 8, 1.0)
    coarsen(b2, own3.at[0], H2, H2, 0, 0, 1, 4, 1.0)

    got0()
    weights(b0, w0, (1, 13), (1, 37), nx)
    first_sweep(s0, va, w0, (1, 13), (1, 37))
    sweep(va, vb, w0, s0, (3, 11), (2, 36))
    sweep(va, vb, w0, s0, (2, 3), (3, 35))
    sweep(va, vb, w0, s0, (11, 12), (3, 35))
    defect(vb, vc, w0, s0, (3, 11), (3, 35))
    coarsen(vc, s1, H0, H0, H1, H1, 4, 16, 4.0)

    moves = [move(s1, a, 0, o1, H1, 6, 0) for a in (-1, 1, -2, 2)]
    moves += [move(s1, 0, b, o1, H1, 0, 6) for b in signs]
    moves += [move(s1, a, b, o1, H1, 6, 5) for a in signs for b in signs]
    moves += [move(s1, a, b, o1, H1, 5, 1) for a in (-2, 2) for b in signs]
    gots1, sents1 = exchange(moves)

    moves = [move(vb, a, 0, o0, H0, 3, 0, skip=1) for a in signs]
    moves += [move(vb, 0, b, o0, H0, 0, 3, skip=1) for b in signs]
    moves += [move(vb, a, b, o0, H0, 2, 2) for a in signs for b in signs]
    gotu0, sentu0 = exchange(moves)

    def gather(own, ref, g):
        for b in (0, 1, -1, 2, -2, 3, -3):
            rows = pl.ds(Y3 - 4 * b, 4)

            @pl.when(jnp.logical_and(xy + b >= 0, xy + b < nw))
            def _(b=b, rows=rows):
                def body(k, c):
                    def go():
                        pltpu.make_async_remote_copy(
                            src_ref=own.at[0], dst_ref=ref.at[gz, :, rows, :], send_sem=gsem.at[g, b + 3],
                            recv_sem=grsem.at[g, b + 3], device_id=(k, xy + b), device_id_type=MESH,
                        ).start()

                    if b == 0:
                        pl.when(k != gz)(go)
                    else:
                        go()
                    return c

                lax.fori_loop(0, ng, body, 0)

        def wait(sems, sign):
            for b in (0, 1, -1, 2, -2, 3, -3):
                planes = ng - 1 if b == 0 else ng
                part = ref.at[pl.ds(0, planes), :, pl.ds(Y3 - 4 * b, 4), :]

                @pl.when(jnp.logical_and(xy + sign * b >= 0, xy + sign * b < nw))
                def _(b=b, part=part):
                    pltpu.make_async_copy(part, part, sems.at[g, b + 3]).wait()

        return lambda: wait(grsem, -1), lambda: wait(gsem, 1)

    b3[gz, :, pl.ds(Y3, 4), :] = own3[0, 0]
    gotb3, sentb3 = gather(own3.at[0], b3, 0)
    gotb1()
    weights(b1, w1, (1, 17), (1, 29), nx // 2)
    coarsen(b1, b2, 1, 1, 1, 1, 8, 14, 1.0)
    weights(b2, w2, (2, 8), (2, 14), nx // 4)

    gots1()
    first_sweep(s1, v1a, w1, (1, 17), (1, 29))
    sweep(v1a, v1b, w1, s1, (2, 16), (2, 28))
    defect(v1b, v1c, w1, s1, (3, 15), (3, 27))
    coarsen(v1c, s2, 3, 3, 2, 2, 6, 12, 4.0)
    first_sweep(s2, v2a, w2, (2, 8), (2, 14))
    sweep(v2a, v2b, w2, s2, (3, 7), (3, 13))
    defect(v2b, v2c, w2, s2, (4, 6), (4, 12))
    coarsen(v2c, own3.at[1], H2, H2, 0, 0, 1, 4, 4.0)

    s3[gz, :, pl.ds(Y3, 4), :] = own3[1, 0]
    gots3, sents3 = gather(own3.at[1], s3, 1)

    for i, ref in enumerate((b2, s2, v2b)):
        sub2[i, pl.ds(H2, 2), :, pl.ds(H2, 8), :] = ref[pl.ds(H2, 2), :, pl.ds(H2, 8), :]
    moves = [move(sub2, a, b, o2, H2, 4, 4, all2) for a in range(-2, 3) for b in (-1, 0, 1) if (a, b) != (0, 0)]
    gotsub, sentsub = exchange(moves)

    gotb3()
    R = (2, 26)
    n = R[1] - R[0]
    v = b3[:, 0, pl.ds(R[0], n), :]
    x = lane_of(v)
    zero = jnp.zeros((1, n, LN), F32)
    up = jnp.where(x >= nx // 8 - 1, 0.0, pltpu.roll(v, LN - 1, axis=2))
    down = jnp.where(x == 0, 0.0, pltpu.roll(v, 1, axis=2))
    above = jnp.concatenate([v[1:], zero], axis=0)
    below = jnp.concatenate([zero, v[:-1]], axis=0)
    north, south = b3[:, 0, pl.ds(R[0] + 1, n), :], b3[:, 0, pl.ds(R[0] - 1, n), :]
    w3a[:, pl.ds(R[0], n), :] = jnp.where(x >= nx // 8 - 1, 0.0, 0.5 * (v + up))
    w3b[:, pl.ds(R[0], n), :] = 0.5 * (v + north)
    w3e[:, pl.ds(R[0], n), :] = 0.5 * (v + south)
    w3c[pl.ds(1, ng), pl.ds(R[0], n), :] = 0.5 * (v + above)
    w3c[pl.ds(0, 1), pl.ds(R[0], n), :] = zero
    total = 3.0 * v + 0.5 * ((up + down) + (north + south) + (above + below))
    w3d[:, pl.ds(R[0], n), :] = jnp.where(v > 0.0, 0.8 / total, 0.0)
    gots3()
    e3a[pl.ds(3, ng), 0, pl.ds(R[0], n), :] = w3d[:, pl.ds(R[0], n), :] * s3[:, 0, pl.ds(R[0], n), :]
    a, out = e3a, e3b
    for lo, n in ((3, 22), (3, 22), (6, 16), (6, 16), (6, 16), (6, 16), (10, 8)):
        rows = pl.ds(lo, n)
        v = a[pl.ds(3, ng), 0, rows, :]
        wx = w3a[:, rows, :]
        acc = wx * pltpu.roll(v, LN - 1, axis=2) + pltpu.roll(wx * v, 1, axis=2)
        acc += w3b[:, rows, :] * a[pl.ds(3, ng), 0, pl.ds(lo + 1, n), :]
        acc += w3e[:, rows, :] * a[pl.ds(3, ng), 0, pl.ds(lo - 1, n), :]
        acc += w3c[pl.ds(1, ng), rows, :] * a[pl.ds(4, ng), 0, rows, :]
        acc += w3c[pl.ds(0, ng), rows, :] * a[pl.ds(2, ng), 0, rows, :]
        out[pl.ds(3, ng), 0, rows, :] = 0.2 * v + w3d[:, rows, :] * (s3[:, 0, rows, :] + acc)
        a, out = out, a

    gotsub()
    weights(sub2.at[0], w2, (1, 9), (1, 15), nx // 4)
    spread(a, pe2, gz + 1, 10, 0, 0, 5, 8, 1)
    add_spread(sub2.at[2], pe2, v2a, 0, 10, (0, 16))
    sweep(v2a, v2b, w2, sub2.at[1], (1, 9), (1, 15))
    sweep(v2b, v2a, w2, sub2.at[1], (2, 8), (2, 14))

    spread(v2a, pe1, 2, 2, 0, 3, 6, 12, 2)
    add_spread(v1b, pe1, v1a, 3, 12, (3, 27))
    sweep(v1a, v1c, w1, s1, (4, 14), (4, 26))
    sweep(v1c, v1a, w1, s1, (5, 13), (5, 25))

    spread(v1a, pe0, 5, 5, 0, 0, 8, 20, 4)
    gotu0()

    def add0(k, c):
        for y in windows(0, 38):
            va[k, :, pl.ds(y, 8), :] = vb[k, :, pl.ds(y, 8), :] + pe0[(k + 1) // 2, :, pl.ds(y + 1, 8), :]
        return c

    lax.fori_loop(0, 14, add0, 0)
    sweep(va, vc, w0, s0, (1, 13), (1, 37))
    sweep(vc, va, w0, s0, (2, 12), (2, 36))
    stores = []

    def store(src, dst, i):
        for t in range(4):
            cp = pltpu.make_async_copy(
                src.at[pl.ds(H0, 8), t, pl.ds(H0, 32), :], dst.at[:, :, pl.ds(LN * t, LN)], out_sem.at[i, t]
            )
            cp.start()
            stores.append(cp)

    store(va, p_out, 0)
    defect(va, vc, w0, s0, (3, 11), (3, 35))
    store(vc, r_out, 1)
    for wait in (sent0, sentb1, sents1, sentu0, sentb3, sents3, sentsub):
        wait()
    for cp in stores:
        cp.wait()


def solution(mesh):
    ng, nw = mesh.shape["gz"], mesh.shape["xy"]

    def block(rhs, den):
        nx = rhs.shape[2]
        f0 = pltpu.VMEM((14, 4, 40, LN), F32)
        f1 = pltpu.VMEM((18, 2, 32, LN), F32)
        f2 = pltpu.VMEM((10, 1, 16, LN), F32)
        g3 = pltpu.VMEM((ng, 1, 32, LN), F32)
        w3 = pltpu.VMEM((ng, 32, LN), F32)
        return pl.pallas_call(
            functools.partial(kernel, ng, nw, nx),
            out_shape=[jax.ShapeDtypeStruct(rhs.shape, F32)] * 2,
            in_specs=[pl.BlockSpec(memory_space=pl.ANY)] * 2,
            out_specs=[pl.BlockSpec(memory_space=pl.ANY)] * 2,
            scratch_shapes=[pltpu.VMEM((2, 14, 4, 40, LN), F32)] + [f0] * 8 + [pltpu.VMEM((8, 4, 40, LN), F32)]
            + [f1] * 10 + [pltpu.VMEM((6, 2, 32, LN), F32)]
            + [pltpu.VMEM((3, 10, 1, 16, LN), F32)] + [f2] * 10 + [pltpu.VMEM((5, 1, 16, LN), F32)]
            + [pltpu.VMEM((2, 1, 1, 4, LN), F32), g3, g3, w3, w3, pltpu.VMEM((ng + 1, 32, LN), F32), w3, w3]
            + [pltpu.VMEM((ng + 6, 1, 32, LN), F32)] * 2
            + [pltpu.SemaphoreType.DMA((2, 4))] * 2
            + [pltpu.SemaphoreType.DMA((64,))] * 2
            + [pltpu.SemaphoreType.DMA((2, 7))] * 2,
            compiler_params=pltpu.CompilerParams(
                collective_id=0, has_side_effects=True, vmem_limit_bytes=50 * 2**20
            ),
        )(rhs, den)

    spec = P("gz", "xy", None)
    return jax.shard_map(block, mesh=mesh, in_specs=(spec, spec), out_specs=(spec, spec), check_vma=False)
```

```python
import functools

import jax
import jax.numpy as jnp
from jax import lax
from jax.experimental import pallas as pl
from jax.experimental.pallas import tpu as pltpu
from jax.sharding import PartitionSpec as P

MESH = pl.DeviceIdType.MESH
F32 = jnp.float32
LN = 128


def windows(lo, hi, rows=8):
    starts = list(range(lo, hi - rows + 1, rows))
    if starts[-1] + rows < hi:
        starts.append(hi - rows)
    return starts


def lane_of(v):
    return lax.broadcasted_iota(jnp.int32, v.shape, v.ndim - 1)


def next_x(v):
    r = pltpu.roll(v, LN - 1, axis=2)
    if v.shape[0] == 1:
        return r
    carry = jnp.concatenate([r[1:], r[:1]], axis=0)
    return jnp.where(lane_of(v) == LN - 1, carry, r)


def prev_x(v):
    r = pltpu.roll(v, 1, axis=2)
    if v.shape[0] == 1:
        return r
    carry = jnp.concatenate([r[-1:], r[:-1]], axis=0)
    return jnp.where(lane_of(v) == 0, carry, r)


def x_index(v):
    tile = lax.broadcasted_iota(jnp.int32, v.shape, 0)
    return tile * LN + lane_of(v)


def neighbour_sum(a, w, z, y, n):
    wx, wy, wz = w[0], w[1], w[2]
    ys = pl.ds(y, n)
    v = a[z, :, ys, :]
    wxc = wx[z, :, ys, :]
    acc = wxc * next_x(v) + prev_x(wxc * v)
    acc += wy[z, :, ys, :] * a[z, :, pl.ds(y + 1, n), :]
    acc += wy[z, :, pl.ds(y - 1, n), :] * a[z, :, pl.ds(y - 1, n), :]
    acc += wz[z, :, ys, :] * a[z + 1, :, ys, :]
    acc += wz[z - 1, :, ys, :] * a[z - 1, :, ys, :]
    return v, acc


PLANES = {4: 4, 2: 4, 1: 16}


def planes(zs, body, tiles):
    n, u = zs[1] - zs[0], min(PLANES[tiles], zs[1] - zs[0])

    def run(z0, k):
        todo = []
        for i in range(k):
            todo += body(z0 + i)
        for ref, index, value in todo:
            ref[index] = value

    if n // u > 1:
        def step(k, c):
            run(zs[0] + k * u, u)
            return c

        lax.fori_loop(0, n // u, step, 0)
    else:
        run(zs[0], u)
    if n % u:
        run(zs[1] - n % u, n % u)


def sweep(a, out, w, s, zs, yr):
    def body(z):
        todo = []
        for y in windows(*yr):
            v, acc = neighbour_sum(a, w, z, y, 8)
            at = (z, slice(None), pl.ds(y, 8), slice(None))
            todo.append((out, at, 0.2 * v + w[3][at] * (s[at] + acc)))
        return todo

    planes(zs, body, a.shape[1])


def defect(a, out, w, s, zs, yr):
    def body(z):
        todo = []
        for y in windows(*yr):
            v, acc = neighbour_sum(a, w, z, y, 8)
            at = (z, slice(None), pl.ds(y, 8), slice(None))
            todo.append((out, at, s[at] + (acc - w[4][at] * v)))
        return todo

    planes(zs, body, a.shape[1])


def weights(b, w, zs, yr, nx):
    wx, wy, wz, d, tot = w

    def body(z):
        todo = []
        for y in windows(yr[0] - 1, yr[1]):
            at = (z, slice(None), pl.ds(y, 8), slice(None))
            todo.append((wy, at, 0.5 * (b[at] + b[z, :, pl.ds(y + 1, 8), :])))
        for y in windows(*yr):
            ys = pl.ds(y, 8)
            at = (z, slice(None), ys, slice(None))
            v = b[at]
            x = x_index(v)
            up = jnp.where(x >= nx - 1, 0.0, next_x(v))
            down = jnp.where(x == 0, 0.0, prev_x(v))
            above = b[z + 1, :, ys, :]
            todo.append((wx, at, jnp.where(x >= nx - 1, 0.0, 0.5 * (v + up))))
            todo.append((wz, at, 0.5 * (v + above)))
            beside = b[z, :, pl.ds(y + 1, 8), :] + b[z, :, pl.ds(y - 1, 8), :]
            total = 3.0 * v + 0.5 * ((up + down) + beside + (above + b[z - 1, :, ys, :]))
            todo.append((tot, at, total))
            todo.append((d, at, jnp.where(v > 0.0, 0.8 / total, 0.0)))
        return todo

    planes(zs, body, b.shape[1])
    z = zs[0] - 1
    for y in windows(*yr):
        ys = pl.ds(y, 8)
        wz[z, :, ys, :] = 0.5 * (b[z, :, ys, :] + b[z + 1, :, ys, :])


def first_sweep(s, out, w, zs, yr):
    def body(z):
        todo = []
        for y in windows(*yr):
            at = (z, slice(None), pl.ds(y, 8), slice(None))
            todo.append((out, at, w[3][at] * s[at]))
        return todo

    planes(zs, body, s.shape[1])


def take(v, index):
    flat = v.reshape(-1, LN)
    return jnp.take_along_axis(flat, index(lax.broadcasted_iota(jnp.int32, flat.shape, 1)), axis=1).reshape(v.shape)


def coarsen(f, out, z_f, y_f, z_c, y_c, nz, ny, scale):
    rows = min(ny, 8)

    def body(k):
        todo = []
        for y in windows(0, ny, rows):
            even = pl.ds(y_f + 2 * y, rows, stride=2)
            odd = pl.ds(y_f + 2 * y + 1, rows, stride=2)
            z = z_f + 2 * k
            v = (f[z, :, even, :] + f[z, :, odd, :]) + (f[z + 1, :, even, :] + f[z + 1, :, odd, :])
            if scale != 1.0:
                v = v * scale
            v = v + pltpu.roll(v, LN - 1, axis=2)
            g = take(v, lambda j: lax.rem(2 * j, LN))
            low = lax.broadcasted_iota(jnp.int32, (rows, LN), 1) < LN // 2
            tiles = v.shape[0]
            for t in range(max(1, tiles // 2)):
                high = g[2 * t + 1] if tiles > 1 else jnp.zeros((rows, LN), F32)
                todo.append((out, (z_c + k, t, pl.ds(y_c + y, rows), slice(None)), jnp.where(low, g[2 * t], high)))
        return todo

    planes((0, nz), body, max(1, f.shape[1] // 2))


def spread(e, out, z_c, y_c, z_o, y_o, nz, ny, tiles):
    def body(k):
        todo = []
        for y in windows(0, ny):
            v = e[z_c + k, :, pl.ds(y_c + y, 8), :]
            parts = [take(v, lambda j: j // 2)]
            if tiles > 1:
                parts.append(take(v, lambda j: LN // 2 + j // 2))
            for t in range(tiles):
                for i in range(2):
                    at = (z_o + k, t, pl.ds(y_o + 2 * y + i, 8, stride=2), slice(None))
                    todo.append((out, at, parts[t % 2][t // 2]))
        return todo

    planes((0, nz), body, max(1, tiles // 2))


def add_spread(u, pe, out, z0, nz, yr):
    def body(k):
        todo = []
        for y in windows(*yr):
            ys = pl.ds(y, 8)
            p = pe[k, :, ys, :]
            for i in range(2):
                at = (z0 + 2 * k + i, slice(None), ys, slice(None))
                todo.append((out, at, u[at] + p))
        return todo

    planes((0, nz // 2), body, u.shape[1])


def kernel(ng, nw, nx, rhs, den, p_out, r_out,
           sb0, w0a, w0b, w0c, w0d, w0e, va, vb, vc, pe0,
           b1, s1, w1a, w1b, w1c, w1d, w1e, v1a, v1b, v1c, pe1,
           sub2, b2, s2, w2a, w2b, w2c, w2d, w2e, v2a, v2b, v2c, pe2,
           own3, b3, s3, w3a, w3b, w3c, w3d, w3e, e3a, e3b,
           in_sem, out_sem, ssem, rsem, gsem, grsem):
    gz, xy = lax.axis_index("gz"), lax.axis_index("xy")
    w0 = (w0a, w0b, w0c, w0d, w0e)
    w1 = (w1a, w1b, w1c, w1d, w1e)
    w2 = (w2a, w2b, w2c, w2d, w2e)
    w3 = (w3a, w3b, w3c, w3d, w3e)
    b0, s0 = sb0.at[1], sb0.at[0]
    H0, H1, H2, Y3 = 3, 7, 4, 12

    loads = []
    for t in range(4):
        for i, (src, dst) in enumerate(((den, b0), (rhs, s0))):
            cp = pltpu.make_async_copy(
                src.at[:, :, pl.ds(LN * t, LN)], dst.at[pl.ds(H0, 8), t, pl.ds(H0, 32), :], in_sem.at[i, t]
            )
            cp.start()
            loads.append(cp)

    def clear(ref, zs, ys):
        shape = (zs[1] - zs[0], ref.shape[-3], ys[1] - ys[0], LN)
        if len(ref.shape) == 5:
            for k in range(ref.shape[0]):
                ref[k, zs[0]:zs[1], :, ys[0]:ys[1], :] = jnp.zeros(shape, F32)
        else:
            ref[zs[0]:zs[1], :, ys[0]:ys[1], :] = jnp.zeros(shape, F32)

    for ref, h, z, y, reach in ((sb0, H0, 8, 32, 1), (vb, H0, 8, 32, 1), (b1, H1, 4, 16, 2), (s1, H1, 4, 16, 2),
                                (sub2, H2, 2, 8, 2)):
        top, rows = 2 * h + z, 2 * h + y

        @pl.when(gz < reach)
        def _(ref=ref, h=h, rows=rows):
            clear(ref, (0, h), (0, rows))

        @pl.when(gz >= ng - reach)
        def _(ref=ref, h=h, z=z, top=top, rows=rows):
            clear(ref, (h + z, top), (0, rows))

        @pl.when(xy == 0)
        def _(ref=ref, h=h, top=top):
            clear(ref, (0, top), (0, h))

        @pl.when(xy == nw - 1)
        def _(ref=ref, h=h, y=y, top=top, rows=rows):
            clear(ref, (0, top), (h + y, rows))

    @pl.when(xy < 3)
    def _():
        clear(s3, (0, ng), (0, Y3))

    @pl.when(xy >= nw - 3)
    def _():
        clear(s3, (0, ng), (Y3 + 4, 32))

    for ref in (e3a, e3b):
        clear(ref, (0, 3), (0, 32))
        clear(ref, (3 + ng, 6 + ng), (0, 32))

    def inside(a, b):
        conds = []
        if a:
            conds += [gz + a >= 0, gz + a < ng]
        if b:
            conds += [xy + b >= 0, xy + b < nw]
        return functools.reduce(jnp.logical_and, conds)

    barrier = pltpu.get_barrier_semaphore()

    def reach(start):
        def body(k, c):
            for b in range(-3, 4):
                ok = jnp.logical_and(xy + b >= 0, xy + b < nw)
                if b == 0:
                    ok = jnp.logical_and(ok, k != gz)
                pl.when(ok)(functools.partial(start, k, b))
            return c

        lax.fori_loop(0, ng, body, 0)

    reach(lambda k, b: pl.semaphore_signal(barrier, inc=1, device_id=(k, xy + b), device_id_type=MESH))
    columns = 1 + jnp.minimum(xy, 3) + jnp.minimum(nw - 1 - xy, 3)
    pl.semaphore_wait(barrier, ng * columns - 1)
    for cp in loads:
        cp.wait()

    used = [0]

    def exchange(moves):
        copies = []
        for a, b, ref, src, dst in moves:
            i = used[0]
            used[0] += 1
            cp = pltpu.make_async_remote_copy(
                src_ref=ref.at[src], dst_ref=ref.at[dst], send_sem=ssem.at[i], recv_sem=rsem.at[i],
                device_id=(gz + a, xy + b), device_id_type=MESH,
            )

            @pl.when(inside(a, b))
            def _(cp=cp):
                cp.start()

            copies.append((a, b, cp))

        def wait_recv():
            for a, b, cp in copies:
                @pl.when(inside(-a, -b))
                def _(cp=cp):
                    cp.wait_recv()

        def wait_send():
            for a, b, cp in copies:
                @pl.when(inside(a, b))
                def _(cp=cp):
                    cp.wait_send()

        return wait_recv, wait_send

    def span(shift, own, h, lo_skip, width):
        if shift == 0:
            return h, h + own
        if shift > 0:
            return max(h - width, h - shift * own), min(h - lo_skip, h - (shift - 1) * own)
        return max(h + own + lo_skip, h - shift * own), min(h + own + width, h + (1 - shift) * own)

    def move(ref, a, b, own, h, wz, wy, lead=(), skip=0):
        z0, z1 = span(a, own[0], h, skip if b == 0 else 0, wz)
        y0, y1 = span(b, own[1], h, skip if a == 0 else 0, wy)
        dst = lead + (pl.ds(z0, z1 - z0), slice(None), pl.ds(y0, y1 - y0), slice(None))
        src = lead + (pl.ds(z0 + a * own[0], z1 - z0), slice(None), pl.ds(y0 + b * own[1], y1 - y0), slice(None))
        return (a, b, ref, src, dst)

    all2 = (slice(None),)
    o0, o1, o2 = (8, 32), (4, 16), (2, 8)
    signs = (-1, 1)
    moves = [move(sb0, a, 0, o0, H0, 3, 0, (1,)) for a in signs]
    moves += [move(sb0, a, 0, o0, H0, 2, 0, (0,)) for a in signs]
    moves += [move(sb0, 0, b, o0, H0, 0, 3, all2) for b in signs]
    moves += [move(sb0, a, b, o0, H0, 2, 2, all2) for a in signs for b in signs]
    got0, sent0 = exchange(moves)

    coarsen(b0, b1, H0, H0, H1, H1, 4, 16, 1.0)
    moves = [move(b1, a, 0, o1, H1, 7, 0) for a in (-1, 1, -2, 2)]
    moves += [move(b1, 0, b, o1, H1, 0, 7) for b in signs]
    moves += [move(b1, a, b, o1, H1, 7, 6) for a in signs for b in signs]
    moves += [move(b1, a, b, o1, H1, 6, 2) for a in (-2, 2) for b in signs]
    gotb1, sentb1 = exchange(moves)
    coarsen(b1, b2, H1, H1, H2, H2, 2, 8, 1.0)
    coarsen(b2, own3.at[1], H2, H2, 0, 0, 1, 4, 1.0)

    got0()
    weights(b0, w0, (1, 13), (1, 37), nx)
    first_sweep(s0, va, w0, (1, 13), (1, 37))
    sweep(va, vb, w0, s0, (3, 11), (2, 36))
    sweep(va, vb, w0, s0, (2, 3), (3, 35))
    sweep(va, vb, w0, s0, (11, 12), (3, 35))
    defect(vb, vc, w0, s0, (3, 11), (3, 35))
    coarsen(vc, s1, H0, H0, H1, H1, 4, 16, 4.0)

    moves = [move(s1, a, 0, o1, H1, 6, 0) for a in (-1, 1, -2, 2)]
    moves += [move(s1, 0, b, o1, H1, 0, 6) for b in signs]
    moves += [move(s1, a, b, o1, H1, 6, 5) for a in signs for b in signs]
    moves += [move(s1, a, b, o1, H1, 5, 1) for a in (-2, 2) for b in signs]
    gots1, sents1 = exchange(moves)

    gotb1()
    weights(b1, w1, (1, 17), (1, 29), nx // 2)
    coarsen(b1, b2, 1, 1, 1, 1, 8, 14, 1.0)
    weights(b2, w2, (2, 8), (2, 14), nx // 4)

    gots1()

    moves = [move(vb, a, 0, o0, H0, 3, 0, skip=1) for a in signs]
    moves += [move(vb, 0, b, o0, H0, 0, 3, skip=1) for b in signs]
    moves += [move(vb, a, b, o0, H0, 2, 2) for a in signs for b in signs]
    gotu0, sentu0 = exchange(moves)

    first_sweep(s1, v1a, w1, (1, 17), (1, 29))
    sweep(v1a, v1b, w1, s1, (2, 16), (2, 28))
    defect(v1b, v1c, w1, s1, (3, 15), (3, 27))
    coarsen(v1c, s2, 3, 3, 2, 2, 6, 12, 4.0)
    first_sweep(s2, v2a, w2, (2, 8), (2, 14))
    sweep(v2a, v2b, w2, s2, (3, 7), (3, 13))
    defect(v2b, v2c, w2, s2, (4, 6), (4, 12))
    coarsen(v2c, own3.at[0], H2, H2, 0, 0, 1, 4, 4.0)

    mine = own3[0, 0, 0]
    own3[2, 0, 0] = jnp.where(lane_of(mine) < LN // 2, mine, pltpu.roll(own3[1, 0, 0], LN // 2, axis=1))
    s3[gz, :, pl.ds(Y3, 4), :] = own3[2, 0]
    sides = (0, 1, -1, 2, -2, 3, -3)

    def send3(k, b):
        pltpu.make_async_remote_copy(
            src_ref=own3.at[2, 0], dst_ref=s3.at[gz, :, pl.ds(Y3 - 4 * b, 4), :], send_sem=gsem.at[b + 3],
            recv_sem=grsem.at[b + 3], device_id=(k, xy + b), device_id_type=MESH,
        ).start()

    reach(send3)

    def wait3(sems, sign):
        for b in sides:
            part = s3.at[pl.ds(0, ng - 1 if b == 0 else ng), :, pl.ds(Y3 - 4 * b, 4), :]

            @pl.when(jnp.logical_and(xy + sign * b >= 0, xy + sign * b < nw))
            def _(b=b, part=part):
                pltpu.make_async_copy(part, part, sems.at[b + 3]).wait()

    gots3, sents3 = lambda: wait3(grsem, -1), lambda: wait3(gsem, 1)

    for i, ref in enumerate((b2, s2, v2b)):
        sub2[i, pl.ds(H2, 2), :, pl.ds(H2, 8), :] = ref[pl.ds(H2, 2), :, pl.ds(H2, 8), :]
    moves = [move(sub2, a, b, o2, H2, 4, 4, all2) for a in range(-2, 3) for b in (-1, 0, 1) if (a, b) != (0, 0)]
    gotsub, sentsub = exchange(moves)

    gots3()
    v = s3[:, 0, pl.ds(0, 28), :]
    low = lane_of(v) < LN // 2
    b3[:, 0, pl.ds(0, 28), :] = jnp.where(low, pltpu.roll(v, LN // 2, axis=2), 0.0)
    s3[:, 0, pl.ds(0, 28), :] = jnp.where(low, v, 0.0)
    R = (2, 26)
    n = R[1] - R[0]
    v = b3[:, 0, pl.ds(R[0], n), :]
    x = lane_of(v)
    zero = jnp.zeros((1, n, LN), F32)
    up = jnp.where(x >= nx // 8 - 1, 0.0, pltpu.roll(v, LN - 1, axis=2))
    down = jnp.where(x == 0, 0.0, pltpu.roll(v, 1, axis=2))
    above = jnp.concatenate([v[1:], zero], axis=0)
    below = jnp.concatenate([zero, v[:-1]], axis=0)
    north, south = b3[:, 0, pl.ds(R[0] + 1, n), :], b3[:, 0, pl.ds(R[0] - 1, n), :]
    w3a[:, pl.ds(R[0], n), :] = jnp.where(x >= nx // 8 - 1, 0.0, 0.5 * (v + up))
    w3b[:, pl.ds(R[0], n), :] = 0.5 * (v + north)
    w3e[:, pl.ds(R[0], n), :] = 0.5 * (v + south)
    w3c[pl.ds(1, ng), pl.ds(R[0], n), :] = 0.5 * (v + above)
    w3c[pl.ds(0, 1), pl.ds(R[0], n), :] = zero
    total = 3.0 * v + 0.5 * ((up + down) + (north + south) + (above + below))
    w3d[:, pl.ds(R[0], n), :] = jnp.where(v > 0.0, 0.8 / total, 0.0)
    e3a[pl.ds(3, ng), 0, pl.ds(R[0], n), :] = w3d[:, pl.ds(R[0], n), :] * s3[:, 0, pl.ds(R[0], n), :]
    a, out = e3a, e3b
    for lo, n in ((3, 22), (3, 22), (6, 16), (6, 16), (6, 16), (6, 16), (10, 8)):
        rows = pl.ds(lo, n)
        v = a[pl.ds(3, ng), 0, rows, :]
        wx = w3a[:, rows, :]
        acc = wx * pltpu.roll(v, LN - 1, axis=2) + pltpu.roll(wx * v, 1, axis=2)
        acc += w3b[:, rows, :] * a[pl.ds(3, ng), 0, pl.ds(lo + 1, n), :]
        acc += w3e[:, rows, :] * a[pl.ds(3, ng), 0, pl.ds(lo - 1, n), :]
        acc += w3c[pl.ds(1, ng), rows, :] * a[pl.ds(4, ng), 0, rows, :]
        acc += w3c[pl.ds(0, ng), rows, :] * a[pl.ds(2, ng), 0, rows, :]
        out[pl.ds(3, ng), 0, rows, :] = 0.2 * v + w3d[:, rows, :] * (s3[:, 0, rows, :] + acc)
        a, out = out, a

    gotsub()
    weights(sub2.at[0], w2, (1, 9), (1, 15), nx // 4)
    spread(a, pe2, gz + 1, 10, 0, 0, 5, 8, 1)
    add_spread(sub2.at[2], pe2, v2a, 0, 10, (0, 16))
    sweep(v2a, v2b, w2, sub2.at[1], (1, 9), (1, 15))
    sweep(v2b, v2a, w2, sub2.at[1], (2, 8), (2, 14))

    spread(v2a, pe1, 2, 2, 0, 3, 6, 12, 2)
    add_spread(v1b, pe1, v1a, 3, 12, (3, 27))
    sweep(v1a, v1c, w1, s1, (4, 14), (4, 26))
    sweep(v1c, v1a, w1, s1, (5, 13), (5, 25))

    spread(v1a, pe0, 5, 5, 0, 0, 8, 20, 4)
    gotu0()

    def add0(fine):
        def body(k):
            todo = []
            for y in windows(0, 38):
                p = pe0[k, :, pl.ds(y + 1, 8), :]
                for i in fine:
                    at = (2 * k + i, slice(None), pl.ds(y, 8), slice(None))
                    todo.append((va, at, vb[at] + p))
            return todo

        return body

    planes((0, 1), add0((0,)), 4)
    planes((1, 7), add0((-1, 0)), 4)
    planes((7, 8), add0((-1,)), 4)
    sweep(va, vc, w0, s0, (1, 13), (1, 37))
    sweep(vc, va, w0, s0, (2, 12), (2, 36))
    stores = []

    def store(src, dst, i):
        for t in range(4):
            cp = pltpu.make_async_copy(
                src.at[pl.ds(H0, 8), t, pl.ds(H0, 32), :], dst.at[:, :, pl.ds(LN * t, LN)], out_sem.at[i, t]
            )
            cp.start()
            stores.append(cp)

    store(va, p_out, 0)
    defect(va, vc, w0, s0, (3, 11), (3, 35))
    store(vc, r_out, 1)
    for wait in (sent0, sentb1, sents1, sentu0, sents3, sentsub):
        wait()
    for cp in stores:
        cp.wait()


def solution(mesh):
    ng, nw = mesh.shape["gz"], mesh.shape["xy"]

    def block(rhs, den):
        nx = rhs.shape[2]
        f0 = pltpu.VMEM((14, 4, 40, LN), F32)
        f1 = pltpu.VMEM((18, 2, 32, LN), F32)
        f2 = pltpu.VMEM((10, 1, 16, LN), F32)
        g3 = pltpu.VMEM((ng, 1, 32, LN), F32)
        w3 = pltpu.VMEM((ng, 32, LN), F32)
        return pl.pallas_call(
            functools.partial(kernel, ng, nw, nx),
            out_shape=[jax.ShapeDtypeStruct(rhs.shape, F32)] * 2,
            in_specs=[pl.BlockSpec(memory_space=pl.ANY)] * 2,
            out_specs=[pl.BlockSpec(memory_space=pl.ANY)] * 2,
            scratch_shapes=[pltpu.VMEM((2, 14, 4, 40, LN), F32)] + [f0] * 8 + [pltpu.VMEM((8, 4, 48, LN), F32)]
            + [f1] * 10 + [pltpu.VMEM((6, 2, 32, LN), F32)]
            + [pltpu.VMEM((3, 10, 1, 16, LN), F32)] + [f2] * 10 + [pltpu.VMEM((5, 1, 24, LN), F32)]
            + [pltpu.VMEM((3, 1, 1, 4, LN), F32), g3, g3, w3, w3, pltpu.VMEM((ng + 1, 32, LN), F32), w3, w3]
            + [pltpu.VMEM((ng + 6, 1, 32, LN), F32)] * 2
            + [pltpu.SemaphoreType.DMA((2, 4))] * 2
            + [pltpu.SemaphoreType.DMA((64,))] * 2
            + [pltpu.SemaphoreType.DMA((7,))] * 2,
            compiler_params=pltpu.CompilerParams(
                collective_id=0, has_side_effects=True, vmem_limit_bytes=50 * 2**20
            ),
        )(rhs, den)

    spec = P("gz", "xy", None)
    return jax.shard_map(block, mesh=mesh, in_specs=(spec, spec), out_specs=(spec, spec), check_vma=False)
```

```python
import functools

import jax
import jax.numpy as jnp
from jax import lax
from jax.experimental import pallas as pl
from jax.experimental.pallas import tpu as pltpu
from jax.sharding import PartitionSpec as P

MESH = pl.DeviceIdType.MESH
F32 = jnp.float32
LN = 128


def windows(lo, hi, rows=8):
    starts = list(range(lo, hi - rows + 1, rows))
    if starts[-1] + rows < hi:
        starts.append(hi - rows)
    return starts


def lane_of(v):
    return lax.broadcasted_iota(jnp.int32, v.shape, v.ndim - 1)


def next_x(v):
    r = pltpu.roll(v, LN - 1, axis=2)
    if v.shape[0] == 1:
        return r
    carry = jnp.concatenate([r[1:], r[:1]], axis=0)
    return jnp.where(lane_of(v) == LN - 1, carry, r)


def prev_x(v):
    r = pltpu.roll(v, 1, axis=2)
    if v.shape[0] == 1:
        return r
    carry = jnp.concatenate([r[-1:], r[:-1]], axis=0)
    return jnp.where(lane_of(v) == 0, carry, r)


def x_index(v):
    tile = lax.broadcasted_iota(jnp.int32, v.shape, 0)
    return tile * LN + lane_of(v)


def neighbour_sum(a, w, z, y, n):
    wx, wy, wz = w[0], w[1], w[2]
    ys = pl.ds(y, n)
    v = a[z, :, ys, :]
    wxc = wx[z, :, ys, :]
    acc = wxc * next_x(v) + prev_x(wxc * v)
    acc += wy[z, :, ys, :] * a[z, :, pl.ds(y + 1, n), :]
    acc += wy[z, :, pl.ds(y - 1, n), :] * a[z, :, pl.ds(y - 1, n), :]
    acc += wz[z, :, ys, :] * a[z + 1, :, ys, :]
    acc += wz[z - 1, :, ys, :] * a[z - 1, :, ys, :]
    return v, acc


PLANES = {4: 4, 2: 4, 1: 16}


def planes(zs, body, tiles):
    n, u = zs[1] - zs[0], min(PLANES[tiles], zs[1] - zs[0])

    def run(z0, k):
        todo = []
        for i in range(k):
            todo += body(z0 + i)
        for ref, index, value in todo:
            ref[index] = value

    if n // u > 1:
        def step(k, c):
            run(zs[0] + k * u, u)
            return c

        lax.fori_loop(0, n // u, step, 0)
    else:
        run(zs[0], u)
    if n % u:
        run(zs[1] - n % u, n % u)


def sweep(a, out, w, s, zs, yr):
    def body(z):
        todo = []
        for y in windows(*yr):
            v, acc = neighbour_sum(a, w, z, y, 8)
            at = (z, slice(None), pl.ds(y, 8), slice(None))
            todo.append((out, at, 0.2 * v + w[3][at] * (s[at] + acc)))
        return todo

    planes(zs, body, a.shape[1])


def defect(a, out, w, s, zs, yr):
    def body(z):
        todo = []
        for y in windows(*yr):
            v, acc = neighbour_sum(a, w, z, y, 8)
            at = (z, slice(None), pl.ds(y, 8), slice(None))
            todo.append((out, at, s[at] + (acc - w[4][at] * v)))
        return todo

    planes(zs, body, a.shape[1])


def weights(b, w, zs, yr, nx):
    wx, wy, wz, d, tot = w

    def body(z):
        todo = []
        for y in windows(yr[0] - 1, yr[1]):
            at = (z, slice(None), pl.ds(y, 8), slice(None))
            todo.append((wy, at, 0.5 * (b[at] + b[z, :, pl.ds(y + 1, 8), :])))
        for y in windows(*yr):
            ys = pl.ds(y, 8)
            at = (z, slice(None), ys, slice(None))
            v = b[at]
            x = x_index(v)
            up = jnp.where(x >= nx - 1, 0.0, next_x(v))
            down = jnp.where(x == 0, 0.0, prev_x(v))
            above = b[z + 1, :, ys, :]
            todo.append((wx, at, jnp.where(x >= nx - 1, 0.0, 0.5 * (v + up))))
            todo.append((wz, at, 0.5 * (v + above)))
            beside = b[z, :, pl.ds(y + 1, 8), :] + b[z, :, pl.ds(y - 1, 8), :]
            total = 3.0 * v + 0.5 * ((up + down) + beside + (above + b[z - 1, :, ys, :]))
            todo.append((tot, at, total))
            todo.append((d, at, jnp.where(v > 0.0, 0.8 / total, 0.0)))
        return todo

    planes(zs, body, b.shape[1])
    z = zs[0] - 1
    for y in windows(*yr):
        ys = pl.ds(y, 8)
        wz[z, :, ys, :] = 0.5 * (b[z, :, ys, :] + b[z + 1, :, ys, :])


def first_sweep(s, out, w, zs, yr):
    def body(z):
        todo = []
        for y in windows(*yr):
            at = (z, slice(None), pl.ds(y, 8), slice(None))
            todo.append((out, at, w[3][at] * s[at]))
        return todo

    planes(zs, body, s.shape[1])


def take(v, index):
    flat = v.reshape(-1, LN)
    return jnp.take_along_axis(flat, index(lax.broadcasted_iota(jnp.int32, flat.shape, 1)), axis=1).reshape(v.shape)


def coarsen(f, out, z_f, y_f, z_c, y_c, nz, ny, scale):
    rows = min(ny, 8)

    def body(k):
        todo = []
        for y in windows(0, ny, rows):
            even = pl.ds(y_f + 2 * y, rows, stride=2)
            odd = pl.ds(y_f + 2 * y + 1, rows, stride=2)
            z = z_f + 2 * k
            v = (f[z, :, even, :] + f[z, :, odd, :]) + (f[z + 1, :, even, :] + f[z + 1, :, odd, :])
            if scale != 1.0:
                v = v * scale
            v = v + pltpu.roll(v, LN - 1, axis=2)
            g = take(v, lambda j: lax.rem(2 * j, LN))
            low = lax.broadcasted_iota(jnp.int32, (rows, LN), 1) < LN // 2
            tiles = v.shape[0]
            for t in range(max(1, tiles // 2)):
                high = g[2 * t + 1] if tiles > 1 else jnp.zeros((rows, LN), F32)
                todo.append((out, (z_c + k, t, pl.ds(y_c + y, rows), slice(None)), jnp.where(low, g[2 * t], high)))
        return todo

    planes((0, nz), body, max(1, f.shape[1] // 2))


def spread(e, out, z_c, y_c, z_o, y_o, nz, ny, tiles):
    def body(k):
        todo = []
        for y in windows(0, ny):
            v = e[z_c + k, :, pl.ds(y_c + y, 8), :]
            parts = [take(v, lambda j: j // 2)]
            if tiles > 1:
                parts.append(take(v, lambda j: LN // 2 + j // 2))
            for t in range(tiles):
                for i in range(2):
                    at = (z_o + k, t, pl.ds(y_o + 2 * y + i, 8, stride=2), slice(None))
                    todo.append((out, at, parts[t % 2][t // 2]))
        return todo

    planes((0, nz), body, max(1, tiles // 2))


def add_spread(u, pe, out, z0, nz, yr):
    def body(k):
        todo = []
        for y in windows(*yr):
            ys = pl.ds(y, 8)
            p = pe[k, :, ys, :]
            for i in range(2):
                at = (z0 + 2 * k + i, slice(None), ys, slice(None))
                todo.append((out, at, u[at] + p))
        return todo

    planes((0, nz // 2), body, u.shape[1])


def kernel(ng, nw, nx, rhs, den, p_out, r_out,
           sb0, w0a, w0b, w0c, w0d, w0e, va, vb, vc, pe0,
           b1, s1, w1a, w1b, w1c, w1d, w1e, v1a, v1b, v1c, pe1,
           sub2, b2, s2, w2a, w2b, w2c, w2d, w2e, v2a, v2b, v2c, pe2,
           own3, b3, s3, w3a, w3b, w3c, w3d, w3e, e3a, e3b,
           in_sem, out_sem, ssem, rsem, gsem, grsem):
    gz, xy = lax.axis_index("gz"), lax.axis_index("xy")
    w0 = (w0a, w0b, w0c, w0d, w0e)
    w1 = (w1a, w1b, w1c, w1d, w1e)
    w2 = (w2a, w2b, w2c, w2d, w2e)
    w3 = (w3a, w3b, w3c, w3d, w3e)
    b0, s0 = sb0.at[1], sb0.at[0]
    H0, H1, H2, Y3 = 3, 7, 4, 12

    loads = []
    for t in range(4):
        for i, (src, dst) in enumerate(((den, b0), (rhs, s0))):
            cp = pltpu.make_async_copy(
                src.at[:, :, pl.ds(LN * t, LN)], dst.at[pl.ds(H0, 8), t, pl.ds(H0, 32), :], in_sem.at[i, t]
            )
            cp.start()
            loads.append(cp)

    def clear(ref, zs, ys):
        shape = (zs[1] - zs[0], ref.shape[-3], ys[1] - ys[0], LN)
        if len(ref.shape) == 5:
            for k in range(ref.shape[0]):
                ref[k, zs[0]:zs[1], :, ys[0]:ys[1], :] = jnp.zeros(shape, F32)
        else:
            ref[zs[0]:zs[1], :, ys[0]:ys[1], :] = jnp.zeros(shape, F32)

    for ref, h, z, y, reach in ((sb0, H0, 8, 32, 1), (vb, H0, 8, 32, 1), (b1, H1, 4, 16, 2), (s1, H1, 4, 16, 2),
                                (sub2, H2, 2, 8, 2)):
        top, rows = 2 * h + z, 2 * h + y

        @pl.when(gz < reach)
        def _(ref=ref, h=h, rows=rows):
            clear(ref, (0, h), (0, rows))

        @pl.when(gz >= ng - reach)
        def _(ref=ref, h=h, z=z, top=top, rows=rows):
            clear(ref, (h + z, top), (0, rows))

        @pl.when(xy == 0)
        def _(ref=ref, h=h, top=top):
            clear(ref, (0, top), (0, h))

        @pl.when(xy == nw - 1)
        def _(ref=ref, h=h, y=y, top=top, rows=rows):
            clear(ref, (0, top), (h + y, rows))

    @pl.when(xy < 3)
    def _():
        clear(s3, (0, ng), (0, Y3))

    @pl.when(xy >= nw - 3)
    def _():
        clear(s3, (0, ng), (Y3 + 4, 32))

    for ref in (e3a, e3b):
        clear(ref, (0, 3), (0, 32))
        clear(ref, (3 + ng, 6 + ng), (0, 32))

    def inside(a, b):
        conds = []
        if a:
            conds += [gz + a >= 0, gz + a < ng]
        if b:
            conds += [xy + b >= 0, xy + b < nw]
        return functools.reduce(jnp.logical_and, conds)

    barrier = pltpu.get_barrier_semaphore()

    def reach(start, far=3):
        def body(k, c):
            for b in range(-far, far + 1):
                ok = jnp.logical_and(xy + b >= 0, xy + b < nw)
                if b == 0:
                    ok = jnp.logical_and(ok, k != gz)
                pl.when(ok)(functools.partial(start, k, b))
            return c

        lax.fori_loop(0, ng, body, 0)

    reach(lambda k, b: pl.semaphore_signal(barrier, inc=1, device_id=(k, xy + b), device_id_type=MESH), 1)
    columns = 1 + jnp.minimum(xy, 1) + jnp.minimum(nw - 1 - xy, 1)
    pl.semaphore_wait(barrier, ng * columns - 1)
    for cp in loads:
        cp.wait()

    used = [0]

    def exchange(moves):
        copies = []
        for a, b, ref, src, dst in moves:
            i = used[0]
            used[0] += 1
            cp = pltpu.make_async_remote_copy(
                src_ref=ref.at[src], dst_ref=ref.at[dst], send_sem=ssem.at[i], recv_sem=rsem.at[i],
                device_id=(gz + a, xy + b), device_id_type=MESH,
            )

            @pl.when(inside(a, b))
            def _(cp=cp):
                cp.start()

            copies.append((a, b, cp))

        def wait_recv():
            for a, b, cp in copies:
                @pl.when(inside(-a, -b))
                def _(cp=cp):
                    cp.wait_recv()

        def wait_send():
            for a, b, cp in copies:
                @pl.when(inside(a, b))
                def _(cp=cp):
                    cp.wait_send()

        return wait_recv, wait_send

    def span(shift, own, h, lo_skip, width):
        if shift == 0:
            return h, h + own
        if shift > 0:
            return max(h - width, h - shift * own), min(h - lo_skip, h - (shift - 1) * own)
        return max(h + own + lo_skip, h - shift * own), min(h + own + width, h + (1 - shift) * own)

    def move(ref, a, b, own, h, wz, wy, lead=(), skip=0):
        z0, z1 = span(a, own[0], h, skip if b == 0 else 0, wz)
        y0, y1 = span(b, own[1], h, skip if a == 0 else 0, wy)
        dst = lead + (pl.ds(z0, z1 - z0), slice(None), pl.ds(y0, y1 - y0), slice(None))
        src = lead + (pl.ds(z0 + a * own[0], z1 - z0), slice(None), pl.ds(y0 + b * own[1], y1 - y0), slice(None))
        return (a, b, ref, src, dst)

    all2 = (slice(None),)
    o0, o1, o2 = (8, 32), (4, 16), (2, 8)
    signs = (-1, 1)
    moves = [move(sb0, a, 0, o0, H0, 3, 0, (1,)) for a in signs]
    moves += [move(sb0, a, 0, o0, H0, 2, 0, (0,)) for a in signs]
    moves += [move(sb0, 0, b, o0, H0, 0, 3, all2) for b in signs]
    moves += [move(sb0, a, b, o0, H0, 2, 2, all2) for a in signs for b in signs]
    got0, sent0 = exchange(moves)

    coarsen(b0, b1, H0, H0, H1, H1, 4, 16, 1.0)
    moves = [move(b1, a, 0, o1, H1, 7, 0) for a in (-1, 1, -2, 2)]
    moves += [move(b1, 0, b, o1, H1, 0, 7) for b in signs]
    moves += [move(b1, a, b, o1, H1, 7, 6) for a in signs for b in signs]
    moves += [move(b1, a, b, o1, H1, 6, 2) for a in (-2, 2) for b in signs]
    gotb1, sentb1 = exchange(moves)
    coarsen(b1, b2, H1, H1, H2, H2, 2, 8, 1.0)
    coarsen(b2, own3.at[1], H2, H2, 0, 0, 1, 4, 1.0)

    got0()
    weights(b0, w0, (1, 13), (1, 37), nx)
    first_sweep(s0, va, w0, (1, 13), (1, 37))
    sweep(va, vb, w0, s0, (3, 11), (2, 36))
    sweep(va, vb, w0, s0, (2, 3), (3, 35))
    sweep(va, vb, w0, s0, (11, 12), (3, 35))
    defect(vb, vc, w0, s0, (3, 11), (3, 35))
    coarsen(vc, s1, H0, H0, H1, H1, 4, 16, 4.0)

    moves = [move(s1, a, 0, o1, H1, 6, 0) for a in (-1, 1, -2, 2)]
    moves += [move(s1, 0, b, o1, H1, 0, 6) for b in signs]
    moves += [move(s1, a, b, o1, H1, 6, 5) for a in signs for b in signs]
    moves += [move(s1, a, b, o1, H1, 5, 1) for a in (-2, 2) for b in signs]
    gots1, sents1 = exchange(moves)

    moves = [move(vb, a, 0, o0, H0, 3, 0, skip=1) for a in signs]
    moves += [move(vb, 0, b, o0, H0, 0, 3, skip=1) for b in signs]
    moves += [move(vb, a, b, o0, H0, 2, 2) for a in signs for b in signs]
    gotu0, sentu0 = exchange(moves)
    sent0()
    sentb1()
    gotb1()
    weights(b1, w1, (1, 17), (1, 29), nx // 2)
    coarsen(b1, b2, 1, 1, 1, 1, 8, 14, 1.0)
    weights(b2, w2, (2, 8), (2, 14), nx // 4)

    gots1()

    first_sweep(s1, v1a, w1, (1, 17), (1, 29))
    sweep(v1a, v1b, w1, s1, (2, 16), (2, 28))
    defect(v1b, v1c, w1, s1, (3, 15), (3, 27))
    coarsen(v1c, s2, 3, 3, 2, 2, 6, 12, 4.0)
    first_sweep(s2, v2a, w2, (2, 8), (2, 14))
    sweep(v2a, v2b, w2, s2, (3, 7), (3, 13))
    defect(v2b, v2c, w2, s2, (4, 6), (4, 12))
    coarsen(v2c, own3.at[0], H2, H2, 0, 0, 1, 4, 4.0)

    mine = own3[0, 0, 0]
    own3[2, 0, 0] = jnp.where(lane_of(mine) < LN // 2, mine, pltpu.roll(own3[1, 0, 0], LN // 2, axis=1))
    s3[gz, :, pl.ds(Y3, 4), :] = own3[2, 0]
    sides = (0, 1, -1, 2, -2, 3, -3)

    def send3(k, b):
        pltpu.make_async_remote_copy(
            src_ref=own3.at[2, 0], dst_ref=s3.at[gz, :, pl.ds(Y3 - 4 * b, 4), :], send_sem=gsem.at[b + 3],
            recv_sem=grsem.at[b + 3], device_id=(k, xy + b), device_id_type=MESH,
        ).start()

    reach(send3)

    def wait3(sems, sign):
        for b in sides:
            part = s3.at[pl.ds(0, ng - 1 if b == 0 else ng), :, pl.ds(Y3 - 4 * b, 4), :]

            @pl.when(jnp.logical_and(xy + sign * b >= 0, xy + sign * b < nw))
            def _(b=b, part=part):
                pltpu.make_async_copy(part, part, sems.at[b + 3]).wait()

    gots3, sents3 = lambda: wait3(grsem, -1), lambda: wait3(gsem, 1)

    for i, ref in enumerate((b2, s2, v2b)):
        sub2[i, pl.ds(H2, 2), :, pl.ds(H2, 8), :] = ref[pl.ds(H2, 2), :, pl.ds(H2, 8), :]
    moves = [move(sub2, a, b, o2, H2, 4, 4, all2) for a in range(-2, 3) for b in (-1, 0, 1) if (a, b) != (0, 0)]
    gotsub, sentsub = exchange(moves)

    sents1()
    sentu0()
    sents3()
    gots3()
    v = s3[:, 0, pl.ds(0, 28), :]
    low = lane_of(v) < LN // 2
    b3[:, 0, pl.ds(0, 28), :] = jnp.where(low, pltpu.roll(v, LN // 2, axis=2), 0.0)
    s3[:, 0, pl.ds(0, 28), :] = jnp.where(low, v, 0.0)
    R = (2, 26)
    n = R[1] - R[0]
    v = b3[:, 0, pl.ds(R[0], n), :]
    x = lane_of(v)
    zero = jnp.zeros((1, n, LN), F32)
    up = jnp.where(x >= nx // 8 - 1, 0.0, pltpu.roll(v, LN - 1, axis=2))
    down = jnp.where(x == 0, 0.0, pltpu.roll(v, 1, axis=2))
    above = jnp.concatenate([v[1:], zero], axis=0)
    below = jnp.concatenate([zero, v[:-1]], axis=0)
    north, south = b3[:, 0, pl.ds(R[0] + 1, n), :], b3[:, 0, pl.ds(R[0] - 1, n), :]
    w3a[:, pl.ds(R[0], n), :] = jnp.where(x >= nx // 8 - 1, 0.0, 0.5 * (v + up))
    w3b[:, pl.ds(R[0], n), :] = 0.5 * (v + north)
    w3e[:, pl.ds(R[0], n), :] = 0.5 * (v + south)
    w3c[pl.ds(1, ng), pl.ds(R[0], n), :] = 0.5 * (v + above)
    w3c[pl.ds(0, 1), pl.ds(R[0], n), :] = zero
    total = 3.0 * v + 0.5 * ((up + down) + (north + south) + (above + below))
    w3d[:, pl.ds(R[0], n), :] = jnp.where(v > 0.0, 0.8 / total, 0.0)
    e3a[pl.ds(3, ng), 0, pl.ds(R[0], n), :] = w3d[:, pl.ds(R[0], n), :] * s3[:, 0, pl.ds(R[0], n), :]
    a, out = e3a, e3b
    for lo, n in ((3, 22), (3, 22), (6, 16), (6, 16), (6, 16), (6, 16), (10, 8)):
        rows = pl.ds(lo, n)
        v = a[pl.ds(3, ng), 0, rows, :]
        wx = w3a[:, rows, :]
        acc = wx * pltpu.roll(v, LN - 1, axis=2) + pltpu.roll(wx * v, 1, axis=2)
        acc += w3b[:, rows, :] * a[pl.ds(3, ng), 0, pl.ds(lo + 1, n), :]
        acc += w3e[:, rows, :] * a[pl.ds(3, ng), 0, pl.ds(lo - 1, n), :]
        acc += w3c[pl.ds(1, ng), rows, :] * a[pl.ds(4, ng), 0, rows, :]
        acc += w3c[pl.ds(0, ng), rows, :] * a[pl.ds(2, ng), 0, rows, :]
        out[pl.ds(3, ng), 0, rows, :] = 0.2 * v + w3d[:, rows, :] * (s3[:, 0, rows, :] + acc)
        a, out = out, a

    gotsub()
    weights(sub2.at[0], w2, (1, 9), (1, 15), nx // 4)
    spread(a, pe2, gz + 1, 10, 0, 0, 5, 8, 1)
    add_spread(sub2.at[2], pe2, v2a, 0, 10, (0, 16))
    sweep(v2a, v2b, w2, sub2.at[1], (1, 9), (1, 15))
    sweep(v2b, v2a, w2, sub2.at[1], (2, 8), (2, 14))

    spread(v2a, pe1, 2, 2, 0, 3, 6, 12, 2)
    add_spread(v1b, pe1, v1a, 3, 12, (3, 27))
    sweep(v1a, v1c, w1, s1, (4, 14), (4, 26))
    sweep(v1c, v1a, w1, s1, (5, 13), (5, 25))

    spread(v1a, pe0, 5, 5, 0, 0, 8, 20, 4)
    gotu0()

    def add0(fine):
        def body(k):
            todo = []
            for y in windows(0, 38):
                p = pe0[k, :, pl.ds(y + 1, 8), :]
                for i in fine:
                    at = (2 * k + i, slice(None), pl.ds(y, 8), slice(None))
                    todo.append((va, at, vb[at] + p))
            return todo

        return body

    planes((0, 1), add0((0,)), 4)
    planes((1, 7), add0((-1, 0)), 4)
    planes((7, 8), add0((-1,)), 4)
    sweep(va, vc, w0, s0, (1, 13), (1, 37))
    sweep(vc, va, w0, s0, (2, 12), (2, 36))
    stores = []

    def store(src, dst, i):
        for t in range(4):
            cp = pltpu.make_async_copy(
                src.at[pl.ds(H0, 8), t, pl.ds(H0, 32), :], dst.at[:, :, pl.ds(LN * t, LN)], out_sem.at[i, t]
            )
            cp.start()
            stores.append(cp)

    store(va, p_out, 0)
    defect(va, vc, w0, s0, (3, 11), (3, 35))
    store(vc, r_out, 1)
    sentsub()
    for cp in stores:
        cp.wait()


def solution(mesh):
    ng, nw = mesh.shape["gz"], mesh.shape["xy"]

    def block(rhs, den):
        nx = rhs.shape[2]
        f0 = pltpu.VMEM((14, 4, 40, LN), F32)
        f1 = pltpu.VMEM((18, 2, 32, LN), F32)
        f2 = pltpu.VMEM((10, 1, 16, LN), F32)
        g3 = pltpu.VMEM((ng, 1, 32, LN), F32)
        w3 = pltpu.VMEM((ng, 32, LN), F32)
        return pl.pallas_call(
            functools.partial(kernel, ng, nw, nx),
            out_shape=[jax.ShapeDtypeStruct(rhs.shape, F32)] * 2,
            in_specs=[pl.BlockSpec(memory_space=pl.ANY)] * 2,
            out_specs=[pl.BlockSpec(memory_space=pl.ANY)] * 2,
            scratch_shapes=[pltpu.VMEM((2, 14, 4, 40, LN), F32)] + [f0] * 8 + [pltpu.VMEM((8, 4, 48, LN), F32)]
            + [f1] * 10 + [pltpu.VMEM((6, 2, 32, LN), F32)]
            + [pltpu.VMEM((3, 10, 1, 16, LN), F32)] + [f2] * 10 + [pltpu.VMEM((5, 1, 24, LN), F32)]
            + [pltpu.VMEM((3, 1, 1, 4, LN), F32), g3, g3, w3, w3, pltpu.VMEM((ng + 1, 32, LN), F32), w3, w3]
            + [pltpu.VMEM((ng + 6, 1, 32, LN), F32)] * 2
            + [pltpu.SemaphoreType.DMA((2, 4))] * 2
            + [pltpu.SemaphoreType.DMA((64,))] * 2
            + [pltpu.SemaphoreType.DMA((7,))] * 2,
            compiler_params=pltpu.CompilerParams(
                collective_id=0, has_side_effects=True, vmem_limit_bytes=50 * 2**20
            ),
        )(*(pltpu.with_memory_space_constraint(x, pltpu.HBM) for x in (rhs, den)))

    spec = P("gz", "xy", None)
    return jax.shard_map(block, mesh=mesh, in_specs=(spec, spec), out_specs=(spec, spec), check_vma=False)
```

```python
import functools

import jax
import jax.numpy as jnp
from jax import lax
from jax.experimental import pallas as pl
from jax.experimental.pallas import tpu as pltpu
from jax.sharding import PartitionSpec as P

MESH = pl.DeviceIdType.MESH
F32 = jnp.float32
LN = 128


def windows(lo, hi, rows=8):
    starts = list(range(lo, hi - rows + 1, rows))
    if starts[-1] + rows < hi:
        starts.append(hi - rows)
    return starts


def lane_of(v):
    return lax.broadcasted_iota(jnp.int32, v.shape, v.ndim - 1)


def next_x(v):
    r = pltpu.roll(v, LN - 1, axis=2)
    if v.shape[0] == 1:
        return r
    carry = jnp.concatenate([r[1:], r[:1]], axis=0)
    return jnp.where(lane_of(v) == LN - 1, carry, r)


def prev_x(v):
    r = pltpu.roll(v, 1, axis=2)
    if v.shape[0] == 1:
        return r
    carry = jnp.concatenate([r[-1:], r[:-1]], axis=0)
    return jnp.where(lane_of(v) == 0, carry, r)


def x_index(v):
    tile = lax.broadcasted_iota(jnp.int32, v.shape, 0)
    return tile * LN + lane_of(v)


def neighbour_sum(a, w, z, y, n):
    wx, wy, wz = w[0], w[1], w[2]
    ys = pl.ds(y, n)
    v = a[z, :, ys, :]
    wxc = wx[z, :, ys, :]
    acc = wxc * next_x(v) + prev_x(wxc * v)
    acc += wy[z, :, ys, :] * a[z, :, pl.ds(y + 1, n), :]
    acc += wy[z, :, pl.ds(y - 1, n), :] * a[z, :, pl.ds(y - 1, n), :]
    acc += wz[z, :, ys, :] * a[z + 1, :, ys, :]
    acc += wz[z - 1, :, ys, :] * a[z - 1, :, ys, :]
    return v, acc


PLANES = {4: 6, 2: 8, 1: 16}


def planes(zs, body, tiles):
    n = zs[1] - zs[0]
    u = max(u for u in range(1, PLANES[tiles] + 1) if n % u == 0)

    def run(z0, k):
        todo = []
        for i in range(k):
            todo += body(z0 + i)
        for ref, index, value in todo:
            ref[index] = value

    if n // u > 1:
        def step(k, c):
            run(zs[0] + k * u, u)
            return c

        lax.fori_loop(0, n // u, step, 0)
    else:
        run(zs[0], u)


def sweep(a, out, w, s, zs, yr):
    def body(z):
        todo = []
        for y in windows(*yr):
            v, acc = neighbour_sum(a, w, z, y, 8)
            at = (z, slice(None), pl.ds(y, 8), slice(None))
            todo.append((out, at, 0.2 * v + w[3][at] * (s[at] + acc)))
        return todo

    planes(zs, body, a.shape[1])


def defect(a, out, w, s, zs, yr, shift=0):
    def body(z):
        todo = []
        for y in windows(*yr):
            v, acc = neighbour_sum(a, w, z, y, 8)
            at = (z, slice(None), pl.ds(y, 8), slice(None))
            to = (z - shift, slice(None), pl.ds(y - shift, 8), slice(None))
            todo.append((out, to, s[at] + (acc - w[4][at] * v)))
        return todo

    planes(zs, body, a.shape[1])


def weights(b, w, zs, yr, nx):
    wx, wy, wz, d, tot = w

    def body(z):
        todo = []
        for y in windows(yr[0] - 1, yr[1]):
            at = (z, slice(None), pl.ds(y, 8), slice(None))
            todo.append((wy, at, 0.5 * (b[at] + b[z, :, pl.ds(y + 1, 8), :])))
        for y in windows(*yr):
            ys = pl.ds(y, 8)
            at = (z, slice(None), ys, slice(None))
            v = b[at]
            x = x_index(v)
            up = jnp.where(x >= nx - 1, 0.0, next_x(v))
            down = jnp.where(x == 0, 0.0, prev_x(v))
            above = b[z + 1, :, ys, :]
            todo.append((wx, at, jnp.where(x >= nx - 1, 0.0, 0.5 * (v + up))))
            todo.append((wz, at, 0.5 * (v + above)))
            beside = b[z, :, pl.ds(y + 1, 8), :] + b[z, :, pl.ds(y - 1, 8), :]
            total = 3.0 * v + 0.5 * ((up + down) + beside + (above + b[z - 1, :, ys, :]))
            todo.append((tot, at, total))
            todo.append((d, at, jnp.where(v > 0.0, 0.8 / total, 0.0)))
        return todo

    planes(zs, body, b.shape[1])
    z = zs[0] - 1
    for y in windows(*yr):
        ys = pl.ds(y, 8)
        wz[z, :, ys, :] = 0.5 * (b[z, :, ys, :] + b[z + 1, :, ys, :])


def first_sweep(s, out, w, zs, yr):
    def body(z):
        todo = []
        for y in windows(*yr):
            at = (z, slice(None), pl.ds(y, 8), slice(None))
            todo.append((out, at, w[3][at] * s[at]))
        return todo

    planes(zs, body, s.shape[1])


def take(v, index):
    flat = v.reshape(-1, LN)
    return jnp.take_along_axis(flat, index(lax.broadcasted_iota(jnp.int32, flat.shape, 1)), axis=1).reshape(v.shape)


def coarsen(f, out, z_f, y_f, z_c, y_c, nz, ny, scale):
    rows = min(ny, 8)

    def body(k):
        todo = []
        for y in windows(0, ny, rows):
            even = pl.ds(y_f + 2 * y, rows, stride=2)
            odd = pl.ds(y_f + 2 * y + 1, rows, stride=2)
            z = z_f + 2 * k
            v = (f[z, :, even, :] + f[z, :, odd, :]) + (f[z + 1, :, even, :] + f[z + 1, :, odd, :])
            if scale != 1.0:
                v = v * scale
            v = v + pltpu.roll(v, LN - 1, axis=2)
            g = take(v, lambda j: lax.rem(2 * j, LN))
            low = lax.broadcasted_iota(jnp.int32, (rows, LN), 1) < LN // 2
            tiles = v.shape[0]
            for t in range(max(1, tiles // 2)):
                high = g[2 * t + 1] if tiles > 1 else jnp.zeros((rows, LN), F32)
                todo.append((out, (z_c + k, t, pl.ds(y_c + y, rows), slice(None)), jnp.where(low, g[2 * t], high)))
        return todo

    planes((0, nz), body, max(1, f.shape[1] // 2))


def spread(e, out, z_c, y_c, z_o, y_o, nz, ny, tiles):
    def body(k):
        todo = []
        for y in windows(0, ny):
            v = e[z_c + k, :, pl.ds(y_c + y, 8), :]
            parts = [take(v, lambda j: j // 2)]
            if tiles > 1:
                parts.append(take(v, lambda j: LN // 2 + j // 2))
            for t in range(tiles):
                for i in range(2):
                    at = (z_o + k, t, pl.ds(y_o + 2 * y + i, 8, stride=2), slice(None))
                    todo.append((out, at, parts[t % 2][t // 2]))
        return todo

    planes((0, nz), body, max(1, tiles // 2))


def add_spread(u, pe, out, z0, nz, yr):
    def body(k):
        todo = []
        for y in windows(*yr):
            ys = pl.ds(y, 8)
            p = pe[k, :, ys, :]
            for i in range(2):
                at = (z0 + 2 * k + i, slice(None), ys, slice(None))
                todo.append((out, at, u[at] + p))
        return todo

    planes((0, nz // 2), body, u.shape[1])


def kernel(ng, nw, nx, rhs, den, p_out, r_out,
           sb0, w0a, w0b, w0c, w0d, w0e, va, vb, vc, pe0,
           b1, s1, w1a, w1b, w1c, w1d, w1e, v1a, v1b, v1c, pe1,
           sub2, b2, s2, w2a, w2b, w2c, w2d, w2e, v2a, v2b, v2c, pe2,
           own3, b3, s3, w3a, w3b, w3c, w3d, w3e, e3a, e3b,
           in_sem, ssem, rsem, gsem, grsem):
    gz, xy = lax.axis_index("gz"), lax.axis_index("xy")
    w0 = (w0a, w0b, w0c, w0d, w0e)
    w1 = (w1a, w1b, w1c, w1d, w1e)
    w2 = (w2a, w2b, w2c, w2d, w2e)
    w3 = (w3a, w3b, w3c, w3d, w3e)
    b0, s0 = sb0.at[1], sb0.at[0]
    H0, H1, H2, Y3 = 3, 7, 4, 12

    loads = []
    for t in range(4):
        for i, (src, dst) in enumerate(((den, b0), (rhs, s0))):
            cp = pltpu.make_async_copy(
                src.at[:, :, pl.ds(LN * t, LN)], dst.at[pl.ds(H0, 8), t, pl.ds(H0, 32), :], in_sem.at[i, t]
            )
            cp.start()
            loads.append(cp)

    def clear(ref, zs, ys):
        shape = (zs[1] - zs[0], ref.shape[-3], ys[1] - ys[0], LN)
        if len(ref.shape) == 5:
            for k in range(ref.shape[0]):
                ref[k, zs[0]:zs[1], :, ys[0]:ys[1], :] = jnp.zeros(shape, F32)
        else:
            ref[zs[0]:zs[1], :, ys[0]:ys[1], :] = jnp.zeros(shape, F32)

    for ref, h, z, y, reach in ((sb0, H0, 8, 32, 1), (vb, H0, 8, 32, 1), (b1, H1, 4, 16, 2), (s1, H1, 4, 16, 2),
                                (sub2, H2, 2, 8, 2)):
        top, rows = 2 * h + z, 2 * h + y

        @pl.when(gz < reach)
        def _(ref=ref, h=h, rows=rows):
            clear(ref, (0, h), (0, rows))

        @pl.when(gz >= ng - reach)
        def _(ref=ref, h=h, z=z, top=top, rows=rows):
            clear(ref, (h + z, top), (0, rows))

        @pl.when(xy == 0)
        def _(ref=ref, h=h, top=top):
            clear(ref, (0, top), (0, h))

        @pl.when(xy == nw - 1)
        def _(ref=ref, h=h, y=y, top=top, rows=rows):
            clear(ref, (0, top), (h + y, rows))

    @pl.when(xy < 3)
    def _():
        clear(s3, (0, ng), (0, Y3))

    @pl.when(xy >= nw - 3)
    def _():
        clear(s3, (0, ng), (Y3 + 4, 32))

    for ref in (e3a, e3b):
        clear(ref, (0, 3), (0, 32))
        clear(ref, (3 + ng, 6 + ng), (0, 32))

    def inside(a, b):
        conds = []
        if a:
            conds += [gz + a >= 0, gz + a < ng]
        if b:
            conds += [xy + b >= 0, xy + b < nw]
        return functools.reduce(jnp.logical_and, conds)

    barrier = pltpu.get_barrier_semaphore()

    def reach(start):
        def body(k, c):
            for b in range(-3, 4):
                ok = jnp.logical_and(xy + b >= 0, xy + b < nw)
                if b == 0:
                    ok = jnp.logical_and(ok, k != gz)
                pl.when(ok)(functools.partial(start, k, b))
            return c

        lax.fori_loop(0, ng, body, 0)

    greeted = 0
    for a in (-4, -2, -1, 0, 1, 2, 4):
        for b in (-1, 0, 1):
            if (a, b) != (0, 0):
                ok = inside(a, b)

                @pl.when(ok)
                def _(a=a, b=b):
                    pl.semaphore_signal(barrier, inc=1, device_id=(gz + a, xy + b), device_id_type=MESH)

                greeted = greeted + ok.astype(jnp.int32)
    pl.semaphore_wait(barrier, greeted)
    for cp in loads:
        cp.wait()

    used = [0]

    def exchange(moves):
        copies = []
        for a, b, ref, src, dst in moves:
            i = used[0]
            used[0] += 1
            cp = pltpu.make_async_remote_copy(
                src_ref=ref.at[src], dst_ref=ref.at[dst], send_sem=ssem.at[i], recv_sem=rsem.at[i],
                device_id=(gz + a, xy + b), device_id_type=MESH,
            )

            @pl.when(inside(a, b))
            def _(cp=cp):
                cp.start()

            copies.append((a, b, cp))

        def wait_recv():
            for a, b, cp in copies:
                @pl.when(inside(-a, -b))
                def _(cp=cp):
                    cp.wait_recv()

        def wait_send():
            for a, b, cp in copies:
                @pl.when(inside(a, b))
                def _(cp=cp):
                    cp.wait_send()

        return wait_recv, wait_send

    def span(shift, own, h, lo_skip, width):
        if shift == 0:
            return h, h + own
        if shift > 0:
            return max(h - width, h - shift * own), min(h - lo_skip, h - (shift - 1) * own)
        return max(h + own + lo_skip, h - shift * own), min(h + own + width, h + (1 - shift) * own)

    def move(ref, a, b, own, h, wz, wy, lead=(), skip=0):
        z0, z1 = span(a, own[0], h, skip if b == 0 else 0, wz)
        y0, y1 = span(b, own[1], h, skip if a == 0 else 0, wy)
        dst = lead + (pl.ds(z0, z1 - z0), slice(None), pl.ds(y0, y1 - y0), slice(None))
        src = lead + (pl.ds(z0 + a * own[0], z1 - z0), slice(None), pl.ds(y0 + b * own[1], y1 - y0), slice(None))
        return (a, b, ref, src, dst)

    all2 = (slice(None),)
    o0, o1, o2 = (8, 32), (4, 16), (2, 8)
    signs = (-1, 1)
    moves = [move(sb0, a, 0, o0, H0, 3, 0, (1,)) for a in signs]
    moves += [move(sb0, a, 0, o0, H0, 2, 0, (0,)) for a in signs]
    moves += [move(sb0, 0, b, o0, H0, 0, 3, all2) for b in signs]
    moves += [move(sb0, a, b, o0, H0, 2, 2, all2) for a in signs for b in signs]
    got0, sent0 = exchange(moves)

    coarsen(b0, b1, H0, H0, H1, H1, 4, 16, 1.0)
    moves = [move(b1, a, 0, o1, H1, 7, 0) for a in (-1, 1, -2, 2)]
    moves += [move(b1, 0, b, o1, H1, 0, 7) for b in signs]
    moves += [move(b1, a, b, o1, H1, 7, 6) for a in signs for b in signs]
    moves += [move(b1, a, b, o1, H1, 6, 2) for a in (-2, 2) for b in signs]
    gotb1, sentb1 = exchange(moves)
    coarsen(b1, b2, H1, H1, H2, H2, 2, 8, 1.0)
    coarsen(b2, own3.at[1], H2, H2, 0, 0, 1, 4, 1.0)

    got0()
    weights(b0, w0, (1, 13), (1, 37), nx)
    first_sweep(s0, va, w0, (1, 13), (1, 37))
    sweep(va, vb, w0, s0, (3, 11), (2, 36))
    sweep(va, vb, w0, s0, (2, 3), (3, 35))
    sweep(va, vb, w0, s0, (11, 12), (3, 35))
    defect(vb, vc, w0, s0, (3, 11), (3, 35))
    coarsen(vc, s1, H0, H0, H1, H1, 4, 16, 4.0)

    moves = [move(s1, a, 0, o1, H1, 6, 0) for a in (-1, 1, -2, 2)]
    moves += [move(s1, 0, b, o1, H1, 0, 6) for b in signs]
    moves += [move(s1, a, b, o1, H1, 6, 5) for a in signs for b in signs]
    moves += [move(s1, a, b, o1, H1, 5, 1) for a in (-2, 2) for b in signs]
    gots1, sents1 = exchange(moves)

    moves = [move(vb, a, 0, o0, H0, 3, 0, skip=1) for a in signs]
    moves += [move(vb, 0, b, o0, H0, 0, 3, skip=1) for b in signs]
    moves += [move(vb, a, b, o0, H0, 2, 2) for a in signs for b in signs]
    gotu0, sentu0 = exchange(moves)
    sent0()
    sentb1()
    gotb1()
    weights(b1, w1, (1, 17), (1, 29), nx // 2)
    coarsen(b1, b2, 1, 1, 1, 1, 8, 14, 1.0)
    weights(b2, w2, (2, 8), (2, 14), nx // 4)

    gots1()

    first_sweep(s1, v1a, w1, (1, 17), (1, 29))
    sweep(v1a, v1b, w1, s1, (2, 16), (2, 28))
    defect(v1b, v1c, w1, s1, (3, 15), (3, 27))
    coarsen(v1c, s2, 3, 3, 2, 2, 6, 12, 4.0)
    first_sweep(s2, v2a, w2, (2, 8), (2, 14))
    sweep(v2a, v2b, w2, s2, (3, 7), (3, 13))
    defect(v2b, v2c, w2, s2, (4, 6), (4, 12))
    coarsen(v2c, own3.at[0], H2, H2, 0, 0, 1, 4, 4.0)

    mine = own3[0, 0, 0]
    own3[2, 0, 0] = jnp.where(lane_of(mine) < LN // 2, mine, pltpu.roll(own3[1, 0, 0], LN // 2, axis=1))
    s3[gz, :, pl.ds(Y3, 4), :] = own3[2, 0]
    sides = (0, 1, -1, 2, -2, 3, -3)

    def send3(k, b):
        pltpu.make_async_remote_copy(
            src_ref=own3.at[2, 0], dst_ref=s3.at[gz, :, pl.ds(Y3 - 4 * b, 4), :], send_sem=gsem.at[b + 3],
            recv_sem=grsem.at[b + 3], device_id=(k, xy + b), device_id_type=MESH,
        ).start()

    reach(send3)

    def wait3(sems, sign):
        for b in sides:
            part = s3.at[pl.ds(0, ng - 1 if b == 0 else ng), :, pl.ds(Y3 - 4 * b, 4), :]

            @pl.when(jnp.logical_and(xy + sign * b >= 0, xy + sign * b < nw))
            def _(b=b, part=part):
                pltpu.make_async_copy(part, part, sems.at[b + 3]).wait()

    gots3, sents3 = lambda: wait3(grsem, -1), lambda: wait3(gsem, 1)

    for i, ref in enumerate((b2, s2, v2b)):
        sub2[i, pl.ds(H2, 2), :, pl.ds(H2, 8), :] = ref[pl.ds(H2, 2), :, pl.ds(H2, 8), :]
    moves = [move(sub2, a, b, o2, H2, 4, 4, all2) for a in range(-2, 3) for b in (-1, 0, 1) if (a, b) != (0, 0)]
    gotsub, sentsub = exchange(moves)

    sents1()
    sentu0()
    sents3()
    gots3()
    v = s3[:, 0, pl.ds(0, 28), :]
    low = lane_of(v) < LN // 2
    b3[:, 0, pl.ds(0, 28), :] = jnp.where(low, pltpu.roll(v, LN // 2, axis=2), 0.0)
    s3[:, 0, pl.ds(0, 28), :] = jnp.where(low, v, 0.0)
    R = (2, 26)
    n = R[1] - R[0]
    v = b3[:, 0, pl.ds(R[0], n), :]
    x = lane_of(v)
    zero = jnp.zeros((1, n, LN), F32)
    up = jnp.where(x >= nx // 8 - 1, 0.0, pltpu.roll(v, LN - 1, axis=2))
    down = jnp.where(x == 0, 0.0, pltpu.roll(v, 1, axis=2))
    above = jnp.concatenate([v[1:], zero], axis=0)
    below = jnp.concatenate([zero, v[:-1]], axis=0)
    north, south = b3[:, 0, pl.ds(R[0] + 1, n), :], b3[:, 0, pl.ds(R[0] - 1, n), :]
    w3a[:, pl.ds(R[0], n), :] = jnp.where(x >= nx // 8 - 1, 0.0, 0.5 * (v + up))
    w3b[:, pl.ds(R[0], n), :] = 0.5 * (v + north)
    w3e[:, pl.ds(R[0], n), :] = 0.5 * (v + south)
    w3c[pl.ds(1, ng), pl.ds(R[0], n), :] = 0.5 * (v + above)
    w3c[pl.ds(0, 1), pl.ds(R[0], n), :] = zero
    total = 3.0 * v + 0.5 * ((up + down) + (north + south) + (above + below))
    w3d[:, pl.ds(R[0], n), :] = jnp.where(v > 0.0, 0.8 / total, 0.0)
    e3a[pl.ds(3, ng), 0, pl.ds(R[0], n), :] = w3d[:, pl.ds(R[0], n), :] * s3[:, 0, pl.ds(R[0], n), :]
    a, out = e3a, e3b
    for lo, n in ((3, 22), (3, 22), (6, 16), (6, 16), (6, 16), (6, 16), (10, 8)):
        rows = pl.ds(lo, n)
        v = a[pl.ds(3, ng), 0, rows, :]
        wx = w3a[:, rows, :]
        acc = wx * pltpu.roll(v, LN - 1, axis=2) + pltpu.roll(wx * v, 1, axis=2)
        acc += w3b[:, rows, :] * a[pl.ds(3, ng), 0, pl.ds(lo + 1, n), :]
        acc += w3e[:, rows, :] * a[pl.ds(3, ng), 0, pl.ds(lo - 1, n), :]
        acc += w3c[pl.ds(1, ng), rows, :] * a[pl.ds(4, ng), 0, rows, :]
        acc += w3c[pl.ds(0, ng), rows, :] * a[pl.ds(2, ng), 0, rows, :]
        out[pl.ds(3, ng), 0, rows, :] = 0.2 * v + w3d[:, rows, :] * (s3[:, 0, rows, :] + acc)
        a, out = out, a

    gotsub()
    weights(sub2.at[0], w2, (1, 9), (1, 15), nx // 4)
    spread(a, pe2, gz + 1, 10, 0, 0, 5, 8, 1)
    add_spread(sub2.at[2], pe2, v2a, 0, 10, (0, 16))
    sweep(v2a, v2b, w2, sub2.at[1], (1, 9), (1, 15))
    sweep(v2b, v2a, w2, sub2.at[1], (2, 8), (2, 14))

    spread(v2a, pe1, 2, 2, 0, 3, 6, 12, 2)
    add_spread(v1b, pe1, v1a, 3, 12, (3, 27))
    sweep(v1a, v1c, w1, s1, (4, 14), (4, 26))
    sweep(v1c, v1a, w1, s1, (5, 13), (5, 25))

    spread(v1a, pe0, 5, 5, 0, 0, 8, 20, 4)
    gotu0()

    def add0(fine):
        def body(k):
            todo = []
            for y in windows(0, 38):
                p = pe0[k, :, pl.ds(y + 1, 8), :]
                for i in fine:
                    at = (2 * k + i, slice(None), pl.ds(y, 8), slice(None))
                    todo.append((va, at, vb[at] + p))
            return todo

        return body

    planes((0, 1), add0((0,)), 4)
    planes((1, 7), add0((-1, 0)), 4)
    planes((7, 8), add0((-1,)), 4)
    sweep(va, vc, w0, s0, (1, 13), (1, 37))
    sweep(vc, va, w0, s0, (2, 12), (2, 36))

    def keep(z):
        own = (slice(None), pl.ds(H0, 32), slice(None))
        return [(p_out, (z - H0,), va[(z,) + own])]

    planes((H0, H0 + 8), keep, 4)
    defect(va, r_out, w0, s0, (3, 11), (3, 35), H0)
    sentsub()


def solution(mesh):
    ng, nw = mesh.shape["gz"], mesh.shape["xy"]

    def block(rhs, den):
        nx = rhs.shape[2]
        f0 = pltpu.VMEM((14, 4, 40, LN), F32)
        f1 = pltpu.VMEM((18, 2, 32, LN), F32)
        f2 = pltpu.VMEM((10, 1, 16, LN), F32)
        g3 = pltpu.VMEM((ng, 1, 32, LN), F32)
        w3 = pltpu.VMEM((ng, 32, LN), F32)
        out = pl.pallas_call(
            functools.partial(kernel, ng, nw, nx),
            out_shape=[jax.ShapeDtypeStruct((8, 4, 32, LN), F32)] * 2,
            in_specs=[pl.BlockSpec(memory_space=pl.ANY)] * 2,
            out_specs=[pl.BlockSpec(memory_space=pltpu.VMEM)] * 2,
            scratch_shapes=[pltpu.VMEM((2, 14, 4, 40, LN), F32)] + [f0] * 8 + [pltpu.VMEM((8, 4, 48, LN), F32)]
            + [f1] * 10 + [pltpu.VMEM((6, 2, 32, LN), F32)]
            + [pltpu.VMEM((3, 10, 1, 16, LN), F32)] + [f2] * 10 + [pltpu.VMEM((5, 1, 24, LN), F32)]
            + [pltpu.VMEM((3, 1, 1, 4, LN), F32), g3, g3, w3, w3, pltpu.VMEM((ng + 1, 32, LN), F32), w3, w3]
            + [pltpu.VMEM((ng + 6, 1, 32, LN), F32)] * 2
            + [pltpu.SemaphoreType.DMA((2, 4))]
            + [pltpu.SemaphoreType.DMA((64,))] * 2
            + [pltpu.SemaphoreType.DMA((7,))] * 2,
            compiler_params=pltpu.CompilerParams(
                collective_id=0, has_side_effects=True, vmem_limit_bytes=50 * 2**20
            ),
        )(*(pltpu.with_memory_space_constraint(x, pltpu.HBM) for x in (rhs, den)))

        def place(p_ref, r_ref, p_hbm, r_hbm, sem):
            copies = [
                pltpu.make_async_copy(src.at[:, t], dst.at[:, :, pl.ds(LN * t, LN)], sem.at[k, t])
                for k, (src, dst) in enumerate(((p_ref, p_hbm), (r_ref, r_hbm)))
                for t in range(4)
            ]
            for cp in copies:
                cp.start()
            for cp in copies:
                cp.wait()

        return pl.pallas_call(
            place,
            out_shape=[jax.ShapeDtypeStruct(rhs.shape, F32)] * 2,
            in_specs=[pl.BlockSpec(memory_space=pltpu.VMEM)] * 2,
            out_specs=[pl.BlockSpec(memory_space=pl.ANY)] * 2,
            scratch_shapes=[pltpu.SemaphoreType.DMA((2, 4))],
            compiler_params=pltpu.CompilerParams(vmem_limit_bytes=8 * 2**20),
        )(*out)

    spec = P("gz", "xy", None)
    return jax.shard_map(block, mesh=mesh, in_specs=(spec, spec), out_specs=(spec, spec), check_vma=False)
```

```python
import functools

import jax
import jax.numpy as jnp
from jax import lax
from jax.experimental import pallas as pl
from jax.experimental.pallas import tpu as pltpu
from jax.sharding import PartitionSpec as P

MESH = pl.DeviceIdType.MESH
F32 = jnp.float32
LN = 128


def windows(lo, hi, rows=8):
    starts = list(range(lo, hi - rows + 1, rows))
    if starts[-1] + rows < hi:
        starts.append(hi - rows)
    return starts


def lane_of(v):
    return lax.broadcasted_iota(jnp.int32, v.shape, v.ndim - 1)


def next_x(v):
    r = pltpu.roll(v, LN - 1, axis=2)
    if v.shape[0] == 1:
        return r
    carry = jnp.concatenate([r[1:], r[:1]], axis=0)
    return jnp.where(lane_of(v) == LN - 1, carry, r)


def prev_x(v):
    r = pltpu.roll(v, 1, axis=2)
    if v.shape[0] == 1:
        return r
    carry = jnp.concatenate([r[-1:], r[:-1]], axis=0)
    return jnp.where(lane_of(v) == 0, carry, r)


def x_index(v):
    tile = lax.broadcasted_iota(jnp.int32, v.shape, 0)
    return tile * LN + lane_of(v)


def neighbour_sum(a, w, z, y, n):
    wx, wy, wz = w[0], w[1], w[2]
    ys = pl.ds(y, n)
    v = a[z, :, ys, :]
    wxc = wx[z, :, ys, :]
    acc = wxc * next_x(v) + prev_x(wxc * v)
    acc += wy[z, :, ys, :] * a[z, :, pl.ds(y + 1, n), :]
    acc += wy[z, :, pl.ds(y - 1, n), :] * a[z, :, pl.ds(y - 1, n), :]
    acc += wz[z, :, ys, :] * a[z + 1, :, ys, :]
    acc += wz[z - 1, :, ys, :] * a[z - 1, :, ys, :]
    return v, acc


PLANES = {4: 14, 2: 16, 1: 16}


def planes(zs, body, tiles):
    n = zs[1] - zs[0]
    u = max(u for u in range(1, PLANES[tiles] + 1) if n % u == 0)

    def run(z0, k):
        todo = []
        for i in range(k):
            todo += body(z0 + i)
        for ref, index, value in todo:
            ref[index] = value

    if n // u > 1:
        def step(k, c):
            run(zs[0] + k * u, u)
            return c

        lax.fori_loop(0, n // u, step, 0)
    else:
        run(zs[0], u)


def sweep(a, out, w, s, zs, yr):
    def body(z):
        todo = []
        for y in windows(*yr):
            v, acc = neighbour_sum(a, w, z, y, 8)
            at = (z, slice(None), pl.ds(y, 8), slice(None))
            todo.append((out, at, 0.2 * v + w[3][at] * (s[at] + acc)))
        return todo

    planes(zs, body, a.shape[1])


def defect(a, out, w, s, zs, yr, shift=0):
    def body(z):
        todo = []
        for y in windows(*yr):
            v, acc = neighbour_sum(a, w, z, y, 8)
            at = (z, slice(None), pl.ds(y, 8), slice(None))
            to = (z - shift, slice(None), pl.ds(y - shift, 8), slice(None))
            todo.append((out, to, s[at] + (acc - w[4][at] * v)))
        return todo

    planes(zs, body, a.shape[1])


def weights(b, w, zs, yr, nx):
    wx, wy, wz, d, tot = w

    def body(z):
        todo = []
        for y in windows(yr[0] - 1, yr[1]):
            at = (z, slice(None), pl.ds(y, 8), slice(None))
            todo.append((wy, at, 0.5 * (b[at] + b[z, :, pl.ds(y + 1, 8), :])))
        for y in windows(*yr):
            ys = pl.ds(y, 8)
            at = (z, slice(None), ys, slice(None))
            v = b[at]
            x = x_index(v)
            up = jnp.where(x >= nx - 1, 0.0, next_x(v))
            down = jnp.where(x == 0, 0.0, prev_x(v))
            above = b[z + 1, :, ys, :]
            todo.append((wx, at, jnp.where(x >= nx - 1, 0.0, 0.5 * (v + up))))
            todo.append((wz, at, 0.5 * (v + above)))
            beside = b[z, :, pl.ds(y + 1, 8), :] + b[z, :, pl.ds(y - 1, 8), :]
            total = 3.0 * v + 0.5 * ((up + down) + beside + (above + b[z - 1, :, ys, :]))
            todo.append((tot, at, total))
            todo.append((d, at, jnp.where(v > 0.0, 0.8 / total, 0.0)))
        return todo

    planes(zs, body, b.shape[1])
    z = zs[0] - 1
    for y in windows(*yr):
        ys = pl.ds(y, 8)
        wz[z, :, ys, :] = 0.5 * (b[z, :, ys, :] + b[z + 1, :, ys, :])


def first_sweep(s, out, w, zs, yr):
    def body(z):
        todo = []
        for y in windows(*yr):
            at = (z, slice(None), pl.ds(y, 8), slice(None))
            todo.append((out, at, w[3][at] * s[at]))
        return todo

    planes(zs, body, s.shape[1])


def take(v, index):
    flat = v.reshape(-1, LN)
    return jnp.take_along_axis(flat, index(lax.broadcasted_iota(jnp.int32, flat.shape, 1)), axis=1).reshape(v.shape)


def coarsen(f, out, z_f, y_f, z_c, y_c, nz, ny, scale):
    rows = min(ny, 8)

    def body(k):
        todo = []
        for y in windows(0, ny, rows):
            even = pl.ds(y_f + 2 * y, rows, stride=2)
            odd = pl.ds(y_f + 2 * y + 1, rows, stride=2)
            z = z_f + 2 * k
            v = (f[z, :, even, :] + f[z, :, odd, :]) + (f[z + 1, :, even, :] + f[z + 1, :, odd, :])
            if scale != 1.0:
                v = v * scale
            v = v + pltpu.roll(v, LN - 1, axis=2)
            g = take(v, lambda j: lax.rem(2 * j, LN))
            low = lax.broadcasted_iota(jnp.int32, (rows, LN), 1) < LN // 2
            tiles = v.shape[0]
            for t in range(max(1, tiles // 2)):
                high = g[2 * t + 1] if tiles > 1 else jnp.zeros((rows, LN), F32)
                todo.append((out, (z_c + k, t, pl.ds(y_c + y, rows), slice(None)), jnp.where(low, g[2 * t], high)))
        return todo

    planes((0, nz), body, max(1, f.shape[1] // 2))


def spread(e, out, z_c, y_c, z_o, y_o, nz, ny, tiles):
    def body(k):
        todo = []
        for y in windows(0, ny):
            v = e[z_c + k, :, pl.ds(y_c + y, 8), :]
            parts = [take(v, lambda j: j // 2)]
            if tiles > 1:
                parts.append(take(v, lambda j: LN // 2 + j // 2))
            for t in range(tiles):
                for i in range(2):
                    at = (z_o + k, t, pl.ds(y_o + 2 * y + i, 8, stride=2), slice(None))
                    todo.append((out, at, parts[t % 2][t // 2]))
        return todo

    planes((0, nz), body, max(1, tiles // 2))


def add_spread(u, pe, out, z0, nz, yr):
    def body(k):
        todo = []
        for y in windows(*yr):
            ys = pl.ds(y, 8)
            p = pe[k, :, ys, :]
            for i in range(2):
                at = (z0 + 2 * k + i, slice(None), ys, slice(None))
                todo.append((out, at, u[at] + p))
        return todo

    planes((0, nz // 2), body, u.shape[1])


def kernel(ng, nw, nx, rhs, den, p_out, r_out,
           sb0, w0a, w0b, w0c, w0d, w0e, va, vb, vc, pe0,
           b1, s1, w1a, w1b, w1c, w1d, w1e, v1a, v1b, v1c, pe1,
           sub2, b2, s2, w2a, w2b, w2c, w2d, w2e, v2a, v2b, v2c, pe2,
           own3, b3, s3, w3a, w3b, w3c, w3d, w3e, e3a, e3b,
           in_sem, ssem, rsem, gsem, grsem):
    gz, xy = lax.axis_index("gz"), lax.axis_index("xy")
    w0 = (w0a, w0b, w0c, w0d, w0e)
    w1 = (w1a, w1b, w1c, w1d, w1e)
    w2 = (w2a, w2b, w2c, w2d, w2e)
    w3 = (w3a, w3b, w3c, w3d, w3e)
    b0, s0 = sb0.at[1], sb0.at[0]
    H0, H1, H2, Y3 = 3, 7, 4, 12

    loads = []
    for t in range(4):
        for i, (src, dst) in enumerate(((den, b0), (rhs, s0))):
            cp = pltpu.make_async_copy(
                src.at[:, :, pl.ds(LN * t, LN)], dst.at[pl.ds(H0, 8), t, pl.ds(H0, 32), :], in_sem.at[i, t]
            )
            cp.start()
            loads.append(cp)

    def clear(ref, zs, ys):
        shape = (zs[1] - zs[0], ref.shape[-3], ys[1] - ys[0], LN)
        if len(ref.shape) == 5:
            for k in range(ref.shape[0]):
                ref[k, zs[0]:zs[1], :, ys[0]:ys[1], :] = jnp.zeros(shape, F32)
        else:
            ref[zs[0]:zs[1], :, ys[0]:ys[1], :] = jnp.zeros(shape, F32)

    for ref, h, z, y, reach in ((sb0, H0, 8, 32, 1), (vb, H0, 8, 32, 1), (b1, H1, 4, 16, 2), (s1, H1, 4, 16, 2),
                                (sub2, H2, 2, 8, 2)):
        top, rows = 2 * h + z, 2 * h + y

        @pl.when(gz < reach)
        def _(ref=ref, h=h, rows=rows):
            clear(ref, (0, h), (0, rows))

        @pl.when(gz >= ng - reach)
        def _(ref=ref, h=h, z=z, top=top, rows=rows):
            clear(ref, (h + z, top), (0, rows))

        @pl.when(xy == 0)
        def _(ref=ref, h=h, top=top):
            clear(ref, (0, top), (0, h))

        @pl.when(xy == nw - 1)
        def _(ref=ref, h=h, y=y, top=top, rows=rows):
            clear(ref, (0, top), (h + y, rows))

    @pl.when(xy < 3)
    def _():
        clear(s3, (0, ng), (0, Y3))

    @pl.when(xy >= nw - 3)
    def _():
        clear(s3, (0, ng), (Y3 + 4, 32))

    for ref in (e3a, e3b):
        clear(ref, (0, 3), (0, 32))
        clear(ref, (3 + ng, 6 + ng), (0, 32))

    def inside(a, b):
        conds = []
        if a:
            conds += [gz + a >= 0, gz + a < ng]
        if b:
            conds += [xy + b >= 0, xy + b < nw]
        return functools.reduce(jnp.logical_and, conds)

    barrier = pltpu.get_barrier_semaphore()

    def reach(start):
        def body(k, c):
            for b in range(-3, 4):
                ok = jnp.logical_and(xy + b >= 0, xy + b < nw)
                if b == 0:
                    ok = jnp.logical_and(ok, k != gz)
                pl.when(ok)(functools.partial(start, k, b))
            return c

        lax.fori_loop(0, ng, body, 0)

    greeted = 0
    for a in (-4, -2, -1, 0, 1, 2, 4):
        for b in (-1, 0, 1):
            if (a, b) != (0, 0):
                ok = inside(a, b)

                @pl.when(ok)
                def _(a=a, b=b):
                    pl.semaphore_signal(barrier, inc=1, device_id=(gz + a, xy + b), device_id_type=MESH)

                greeted = greeted + ok.astype(jnp.int32)
    pl.semaphore_wait(barrier, greeted)
    for cp in loads:
        cp.wait()

    used = [0]

    def exchange(moves):
        copies = []
        for a, b, ref, src, dst in moves:
            i = used[0]
            used[0] += 1
            cp = pltpu.make_async_remote_copy(
                src_ref=ref.at[src], dst_ref=ref.at[dst], send_sem=ssem.at[i], recv_sem=rsem.at[i],
                device_id=(gz + a, xy + b), device_id_type=MESH,
            )

            @pl.when(inside(a, b))
            def _(cp=cp):
                cp.start()

            copies.append((a, b, cp))

        def wait_recv():
            for a, b, cp in copies:
                @pl.when(inside(-a, -b))
                def _(cp=cp):
                    cp.wait_recv()

        def wait_send():
            for a, b, cp in copies:
                @pl.when(inside(a, b))
                def _(cp=cp):
                    cp.wait_send()

        return wait_recv, wait_send

    def span(shift, own, h, lo_skip, width):
        if shift == 0:
            return h, h + own
        if shift > 0:
            return max(h - width, h - shift * own), min(h - lo_skip, h - (shift - 1) * own)
        return max(h + own + lo_skip, h - shift * own), min(h + own + width, h + (1 - shift) * own)

    def move(ref, a, b, own, h, wz, wy, lead=(), skip=0):
        z0, z1 = span(a, own[0], h, skip if b == 0 else 0, wz)
        y0, y1 = span(b, own[1], h, skip if a == 0 else 0, wy)
        dst = lead + (pl.ds(z0, z1 - z0), slice(None), pl.ds(y0, y1 - y0), slice(None))
        src = lead + (pl.ds(z0 + a * own[0], z1 - z0), slice(None), pl.ds(y0 + b * own[1], y1 - y0), slice(None))
        return (a, b, ref, src, dst)

    all2 = (slice(None),)
    o0, o1, o2 = (8, 32), (4, 16), (2, 8)
    signs = (-1, 1)
    moves = [move(sb0, a, 0, o0, H0, 3, 0, (1,)) for a in signs]
    moves += [move(sb0, 0, b, o0, H0, 0, 3, all2) for b in signs]
    moves += [move(sb0, a, b, o0, H0, 2, 2, all2) for a in signs for b in signs]
    got0, sent0 = exchange(moves)
    gots0, sents0 = exchange([move(sb0, a, 0, o0, H0, 2, 0, (0,)) for a in signs])

    coarsen(b0, b1, H0, H0, H1, H1, 4, 16, 1.0)
    moves = [move(b1, a, 0, o1, H1, 7, 0) for a in (-1, 1, -2, 2)]
    moves += [move(b1, 0, b, o1, H1, 0, 7) for b in signs]
    moves += [move(b1, a, b, o1, H1, 7, 6) for a in signs for b in signs]
    moves += [move(b1, a, b, o1, H1, 6, 2) for a in (-2, 2) for b in signs]
    gotb1, sentb1 = exchange(moves)
    coarsen(b1, b2, H1, H1, H2, H2, 2, 8, 1.0)
    coarsen(b2, own3.at[1], H2, H2, 0, 0, 1, 4, 1.0)

    got0()
    weights(b0, w0, (1, 13), (1, 37), nx)
    gots0()
    first_sweep(s0, va, w0, (1, 13), (1, 37))
    sweep(va, vb, w0, s0, (3, 11), (2, 36))
    sweep(va, vb, w0, s0, (2, 3), (3, 35))
    sweep(va, vb, w0, s0, (11, 12), (3, 35))
    defect(vb, vc, w0, s0, (3, 11), (3, 35))
    coarsen(vc, s1, H0, H0, H1, H1, 4, 16, 4.0)

    moves = [move(s1, a, 0, o1, H1, 6, 0) for a in (-1, 1, -2, 2)]
    moves += [move(s1, 0, b, o1, H1, 0, 6) for b in signs]
    moves += [move(s1, a, b, o1, H1, 6, 5) for a in signs for b in signs]
    moves += [move(s1, a, b, o1, H1, 5, 1) for a in (-2, 2) for b in signs]
    gots1, sents1 = exchange(moves)

    moves = [move(vb, a, 0, o0, H0, 3, 0, skip=1) for a in signs]
    moves += [move(vb, 0, b, o0, H0, 0, 3, skip=1) for b in signs]
    moves += [move(vb, a, b, o0, H0, 2, 2) for a in signs for b in signs]
    gotu0, sentu0 = exchange(moves)
    sent0()
    sents0()
    sentb1()
    gotb1()
    weights(b1, w1, (1, 17), (1, 29), nx // 2)
    coarsen(b1, b2, 1, 1, 1, 1, 8, 14, 1.0)
    weights(b2, w2, (2, 8), (2, 14), nx // 4)

    gots1()

    first_sweep(s1, v1a, w1, (1, 17), (1, 29))
    sweep(v1a, v1b, w1, s1, (2, 16), (2, 28))
    defect(v1b, v1c, w1, s1, (3, 15), (3, 27))
    coarsen(v1c, s2, 3, 3, 2, 2, 6, 12, 4.0)
    first_sweep(s2, v2a, w2, (2, 8), (2, 14))
    sweep(v2a, v2b, w2, s2, (3, 7), (3, 13))
    defect(v2b, v2c, w2, s2, (4, 6), (4, 12))
    coarsen(v2c, own3.at[0], H2, H2, 0, 0, 1, 4, 4.0)

    mine = own3[0, 0, 0]
    own3[2, 0, 0] = jnp.where(lane_of(mine) < LN // 2, mine, pltpu.roll(own3[1, 0, 0], LN // 2, axis=1))
    s3[gz, :, pl.ds(Y3, 4), :] = own3[2, 0]
    sides = (0, 1, -1, 2, -2, 3, -3)

    def send3(k, b):
        pltpu.make_async_remote_copy(
            src_ref=own3.at[2, 0], dst_ref=s3.at[gz, :, pl.ds(Y3 - 4 * b, 4), :], send_sem=gsem.at[b + 3],
            recv_sem=grsem.at[b + 3], device_id=(k, xy + b), device_id_type=MESH,
        ).start()

    reach(send3)

    def wait3(sems, sign):
        for b in sides:
            part = s3.at[pl.ds(0, ng - 1 if b == 0 else ng), :, pl.ds(Y3 - 4 * b, 4), :]

            @pl.when(jnp.logical_and(xy + sign * b >= 0, xy + sign * b < nw))
            def _(b=b, part=part):
                pltpu.make_async_copy(part, part, sems.at[b + 3]).wait()

    gots3, sents3 = lambda: wait3(grsem, -1), lambda: wait3(gsem, 1)

    for i, ref in enumerate((b2, s2, v2b)):
        sub2[i, pl.ds(H2, 2), :, pl.ds(H2, 8), :] = ref[pl.ds(H2, 2), :, pl.ds(H2, 8), :]
    moves = [move(sub2, a, b, o2, H2, 4, 4, all2) for a in range(-2, 3) for b in (-1, 0, 1) if (a, b) != (0, 0)]
    gotsub, sentsub = exchange(moves)

    sents1()
    sentu0()
    sents3()
    gots3()
    v = s3[:, 0, pl.ds(0, 28), :]
    low = lane_of(v) < LN // 2
    b3[:, 0, pl.ds(0, 28), :] = jnp.where(low, pltpu.roll(v, LN // 2, axis=2), 0.0)
    s3[:, 0, pl.ds(0, 28), :] = jnp.where(low, v, 0.0)
    R = (2, 26)
    n = R[1] - R[0]
    v = b3[:, 0, pl.ds(R[0], n), :]
    x = lane_of(v)
    zero = jnp.zeros((1, n, LN), F32)
    up = jnp.where(x >= nx // 8 - 1, 0.0, pltpu.roll(v, LN - 1, axis=2))
    down = jnp.where(x == 0, 0.0, pltpu.roll(v, 1, axis=2))
    above = jnp.concatenate([v[1:], zero], axis=0)
    below = jnp.concatenate([zero, v[:-1]], axis=0)
    north, south = b3[:, 0, pl.ds(R[0] + 1, n), :], b3[:, 0, pl.ds(R[0] - 1, n), :]
    w3a[:, pl.ds(R[0], n), :] = jnp.where(x >= nx // 8 - 1, 0.0, 0.5 * (v + up))
    w3b[:, pl.ds(R[0], n), :] = 0.5 * (v + north)
    w3e[:, pl.ds(R[0], n), :] = 0.5 * (v + south)
    w3c[pl.ds(1, ng), pl.ds(R[0], n), :] = 0.5 * (v + above)
    w3c[pl.ds(0, 1), pl.ds(R[0], n), :] = zero
    total = 3.0 * v + 0.5 * ((up + down) + (north + south) + (above + below))
    w3d[:, pl.ds(R[0], n), :] = jnp.where(v > 0.0, 0.8 / total, 0.0)
    e3a[pl.ds(3, ng), 0, pl.ds(R[0], n), :] = w3d[:, pl.ds(R[0], n), :] * s3[:, 0, pl.ds(R[0], n), :]
    a, out = e3a, e3b
    for lo, n in ((3, 22), (3, 22), (6, 16), (6, 16), (6, 16), (6, 16), (10, 8)):
        rows = pl.ds(lo, n)
        v = a[pl.ds(3, ng), 0, rows, :]
        wx = w3a[:, rows, :]
        acc = wx * pltpu.roll(v, LN - 1, axis=2) + pltpu.roll(wx * v, 1, axis=2)
        acc += w3b[:, rows, :] * a[pl.ds(3, ng), 0, pl.ds(lo + 1, n), :]
        acc += w3e[:, rows, :] * a[pl.ds(3, ng), 0, pl.ds(lo - 1, n), :]
        acc += w3c[pl.ds(1, ng), rows, :] * a[pl.ds(4, ng), 0, rows, :]
        acc += w3c[pl.ds(0, ng), rows, :] * a[pl.ds(2, ng), 0, rows, :]
        out[pl.ds(3, ng), 0, rows, :] = 0.2 * v + w3d[:, rows, :] * (s3[:, 0, rows, :] + acc)
        a, out = out, a

    gotsub()
    weights(sub2.at[0], w2, (1, 9), (1, 15), nx // 4)
    spread(a, pe2, gz + 1, 10, 0, 0, 5, 8, 1)
    add_spread(sub2.at[2], pe2, v2a, 0, 10, (0, 16))
    sweep(v2a, v2b, w2, sub2.at[1], (1, 9), (1, 15))
    sweep(v2b, v2a, w2, sub2.at[1], (2, 8), (2, 14))

    spread(v2a, pe1, 2, 2, 0, 3, 6, 12, 2)
    add_spread(v1b, pe1, v1a, 3, 12, (3, 27))
    sweep(v1a, v1c, w1, s1, (4, 14), (4, 26))
    sweep(v1c, v1a, w1, s1, (5, 13), (5, 25))

    spread(v1a, pe0, 5, 5, 0, 0, 8, 20, 4)
    gotu0()

    def add0(fine):
        def body(k):
            todo = []
            for y in windows(0, 38):
                p = pe0[k, :, pl.ds(y + 1, 8), :]
                for i in fine:
                    at = (2 * k + i, slice(None), pl.ds(y, 8), slice(None))
                    todo.append((va, at, vb[at] + p))
            return todo

        return body

    planes((0, 1), add0((0,)), 4)
    planes((1, 7), add0((-1, 0)), 4)
    planes((7, 8), add0((-1,)), 4)
    sweep(va, vc, w0, s0, (1, 13), (1, 37))
    sweep(vc, va, w0, s0, (2, 12), (2, 36))

    def keep(z):
        own = (slice(None), pl.ds(H0, 32), slice(None))
        return [(p_out, (z - H0,), va[(z,) + own])]

    planes((H0, H0 + 8), keep, 4)
    defect(va, r_out, w0, s0, (3, 11), (3, 35), H0)
    sentsub()


def solution(mesh):
    ng, nw = mesh.shape["gz"], mesh.shape["xy"]

    def block(rhs, den):
        nx = rhs.shape[2]
        f0 = pltpu.VMEM((14, 4, 40, LN), F32)
        f1 = pltpu.VMEM((18, 2, 32, LN), F32)
        f2 = pltpu.VMEM((10, 1, 16, LN), F32)
        g3 = pltpu.VMEM((ng, 1, 32, LN), F32)
        w3 = pltpu.VMEM((ng, 32, LN), F32)
        out = pl.pallas_call(
            functools.partial(kernel, ng, nw, nx),
            out_shape=[jax.ShapeDtypeStruct((8, 4, 32, LN), F32)] * 2,
            in_specs=[pl.BlockSpec(memory_space=pl.ANY)] * 2,
            out_specs=[pl.BlockSpec(memory_space=pltpu.VMEM)] * 2,
            scratch_shapes=[pltpu.VMEM((2, 14, 4, 40, LN), F32)] + [f0] * 8 + [pltpu.VMEM((8, 4, 48, LN), F32)]
            + [f1] * 10 + [pltpu.VMEM((6, 2, 32, LN), F32)]
            + [pltpu.VMEM((3, 10, 1, 16, LN), F32)] + [f2] * 10 + [pltpu.VMEM((5, 1, 24, LN), F32)]
            + [pltpu.VMEM((3, 1, 1, 4, LN), F32), g3, g3, w3, w3, pltpu.VMEM((ng + 1, 32, LN), F32), w3, w3]
            + [pltpu.VMEM((ng + 6, 1, 32, LN), F32)] * 2
            + [pltpu.SemaphoreType.DMA((2, 4))]
            + [pltpu.SemaphoreType.DMA((64,))] * 2
            + [pltpu.SemaphoreType.DMA((7,))] * 2,
            compiler_params=pltpu.CompilerParams(
                collective_id=0, has_side_effects=True, vmem_limit_bytes=50 * 2**20
            ),
        )(*(pltpu.with_memory_space_constraint(x, pltpu.HBM) for x in (rhs, den)))

        def place(p_ref, r_ref, p_hbm, r_hbm, sem):
            copies = [
                pltpu.make_async_copy(src.at[:, t], dst.at[:, :, pl.ds(LN * t, LN)], sem.at[k, t])
                for k, (src, dst) in enumerate(((p_ref, p_hbm), (r_ref, r_hbm)))
                for t in range(4)
            ]
            for cp in copies:
                cp.start()
            for cp in copies:
                cp.wait()

        return pl.pallas_call(
            place,
            out_shape=[jax.ShapeDtypeStruct(rhs.shape, F32)] * 2,
            in_specs=[pl.BlockSpec(memory_space=pltpu.VMEM)] * 2,
            out_specs=[pl.BlockSpec(memory_space=pl.ANY)] * 2,
            scratch_shapes=[pltpu.SemaphoreType.DMA((2, 4))],
            compiler_params=pltpu.CompilerParams(vmem_limit_bytes=8 * 2**20),
        )(*out)

    spec = P("gz", "xy", None)
    return jax.shard_map(block, mesh=mesh, in_specs=(spec, spec), out_specs=(spec, spec), check_vma=False)
```

```python
import functools

import jax
import jax.numpy as jnp
from jax import lax
from jax.experimental import pallas as pl
from jax.experimental.pallas import tpu as pltpu
from jax.sharding import PartitionSpec as P

MESH = pl.DeviceIdType.MESH
F32 = jnp.float32
LN = 128


def windows(lo, hi, rows=8):
    starts = list(range(lo, hi - rows + 1, rows))
    if starts[-1] + rows < hi:
        starts.append(hi - rows)
    return starts


def lane_of(v):
    return lax.broadcasted_iota(jnp.int32, v.shape, v.ndim - 1)


def next_x(v):
    r = pltpu.roll(v, LN - 1, axis=2)
    if v.shape[0] == 1:
        return r
    carry = jnp.concatenate([r[1:], r[:1]], axis=0)
    return jnp.where(lane_of(v) == LN - 1, carry, r)


def prev_x(v):
    r = pltpu.roll(v, 1, axis=2)
    if v.shape[0] == 1:
        return r
    carry = jnp.concatenate([r[-1:], r[:-1]], axis=0)
    return jnp.where(lane_of(v) == 0, carry, r)


def x_index(v):
    tile = lax.broadcasted_iota(jnp.int32, v.shape, 0)
    return tile * LN + lane_of(v)


def neighbour_sum(a, w, z, y, n):
    wx, wy, wz = w[0], w[1], w[2]
    ys = pl.ds(y, n)
    v = a[z, :, ys, :]
    wxc = wx[z, :, ys, :]
    acc = wxc * next_x(v) + prev_x(wxc * v)
    acc += wy[z, :, ys, :] * a[z, :, pl.ds(y + 1, n), :]
    acc += wy[z, :, pl.ds(y - 1, n), :] * a[z, :, pl.ds(y - 1, n), :]
    acc += wz[z, :, ys, :] * a[z + 1, :, ys, :]
    acc += wz[z - 1, :, ys, :] * a[z - 1, :, ys, :]
    return v, acc


PLANES = {4: 14, 2: 16, 1: 16}


def planes(zs, body, tiles):
    n = zs[1] - zs[0]
    u = max(u for u in range(1, PLANES[tiles] + 1) if n % u == 0)

    def run(z0, k):
        todo = []
        for i in range(k):
            todo += body(z0 + i)
        for ref, index, value in todo:
            ref[index] = value

    if n // u > 1:
        def step(k, c):
            run(zs[0] + k * u, u)
            return c

        lax.fori_loop(0, n // u, step, 0)
    else:
        run(zs[0], u)


def sweep(a, out, w, s, zs, yr):
    def body(z):
        todo = []
        for y in windows(*yr):
            v, acc = neighbour_sum(a, w, z, y, 8)
            at = (z, slice(None), pl.ds(y, 8), slice(None))
            todo.append((out, at, 0.2 * v + w[3][at] * (s[at] + acc)))
        return todo

    planes(zs, body, a.shape[1])


def defect(a, out, w, s, zs, yr, shift=0):
    def body(z):
        todo = []
        for y in windows(*yr):
            v, acc = neighbour_sum(a, w, z, y, 8)
            at = (z, slice(None), pl.ds(y, 8), slice(None))
            to = (z - shift, slice(None), pl.ds(y - shift, 8), slice(None))
            todo.append((out, to, s[at] + (acc - w[4][at] * v)))
        return todo

    planes(zs, body, a.shape[1])


def weights(b, w, zs, yr, nx):
    wx, wy, wz, d, tot = w

    def body(z):
        todo = []
        for y in windows(yr[0] - 1, yr[1]):
            at = (z, slice(None), pl.ds(y, 8), slice(None))
            todo.append((wy, at, 0.5 * (b[at] + b[z, :, pl.ds(y + 1, 8), :])))
        for y in windows(*yr):
            ys = pl.ds(y, 8)
            at = (z, slice(None), ys, slice(None))
            v = b[at]
            x = x_index(v)
            up = jnp.where(x >= nx - 1, 0.0, next_x(v))
            down = jnp.where(x == 0, 0.0, prev_x(v))
            above = b[z + 1, :, ys, :]
            todo.append((wx, at, jnp.where(x >= nx - 1, 0.0, 0.5 * (v + up))))
            todo.append((wz, at, 0.5 * (v + above)))
            beside = b[z, :, pl.ds(y + 1, 8), :] + b[z, :, pl.ds(y - 1, 8), :]
            total = 3.0 * v + 0.5 * ((up + down) + beside + (above + b[z - 1, :, ys, :]))
            todo.append((tot, at, total))
            todo.append((d, at, jnp.where(v > 0.0, 0.8 / total, 0.0)))
        return todo

    planes(zs, body, b.shape[1])
    z = zs[0] - 1
    for y in windows(*yr):
        ys = pl.ds(y, 8)
        wz[z, :, ys, :] = 0.5 * (b[z, :, ys, :] + b[z + 1, :, ys, :])


def first_sweep(s, out, w, zs, yr):
    def body(z):
        todo = []
        for y in windows(*yr):
            at = (z, slice(None), pl.ds(y, 8), slice(None))
            todo.append((out, at, w[3][at] * s[at]))
        return todo

    planes(zs, body, s.shape[1])


def take(v, index):
    flat = v.reshape(-1, LN)
    return jnp.take_along_axis(flat, index(lax.broadcasted_iota(jnp.int32, flat.shape, 1)), axis=1).reshape(v.shape)


def coarsen(f, out, z_f, y_f, z_c, y_c, nz, ny, scale):
    rows = min(ny, 8)

    def body(k):
        todo = []
        for y in windows(0, ny, rows):
            even = pl.ds(y_f + 2 * y, rows, stride=2)
            odd = pl.ds(y_f + 2 * y + 1, rows, stride=2)
            z = z_f + 2 * k
            v = (f[z, :, even, :] + f[z, :, odd, :]) + (f[z + 1, :, even, :] + f[z + 1, :, odd, :])
            if scale != 1.0:
                v = v * scale
            v = v + pltpu.roll(v, LN - 1, axis=2)
            g = take(v, lambda j: lax.rem(2 * j, LN))
            low = lax.broadcasted_iota(jnp.int32, (rows, LN), 1) < LN // 2
            tiles = v.shape[0]
            for t in range(max(1, tiles // 2)):
                high = g[2 * t + 1] if tiles > 1 else jnp.zeros((rows, LN), F32)
                todo.append((out, (z_c + k, t, pl.ds(y_c + y, rows), slice(None)), jnp.where(low, g[2 * t], high)))
        return todo

    planes((0, nz), body, max(1, f.shape[1] // 2))


def spread(e, out, z_c, y_c, z_o, y_o, nz, ny, tiles):
    def body(k):
        todo = []
        for y in windows(0, ny):
            v = e[z_c + k, :, pl.ds(y_c + y, 8), :]
            parts = [take(v, lambda j: j // 2)]
            if tiles > 1:
                parts.append(take(v, lambda j: LN // 2 + j // 2))
            for t in range(tiles):
                for i in range(2):
                    at = (z_o + k, t, pl.ds(y_o + 2 * y + i, 8, stride=2), slice(None))
                    todo.append((out, at, parts[t % 2][t // 2]))
        return todo

    planes((0, nz), body, max(1, tiles // 2))


def add_spread(u, pe, out, z0, nz, yr):
    def body(k):
        todo = []
        for y in windows(*yr):
            ys = pl.ds(y, 8)
            p = pe[k, :, ys, :]
            for i in range(2):
                at = (z0 + 2 * k + i, slice(None), ys, slice(None))
                todo.append((out, at, u[at] + p))
        return todo

    planes((0, nz // 2), body, u.shape[1])


def kernel(ng, nw, nx, rhs, den, p_out, r_out,
           sb0, w0a, w0b, w0c, w0d, w0e, va, vb, vc, pe0,
           b1, s1, w1a, w1b, w1c, w1d, w1e, v1a, v1b, v1c, pe1,
           sub2, b2, s2, w2a, w2b, w2c, w2d, w2e, v2a, v2b, v2c, pe2,
           own3, b3, s3, w3a, w3b, w3c, w3d, w3e, e3a, e3b,
           in_sem, ssem, rsem, gsem, grsem):
    gz, xy = lax.axis_index("gz"), lax.axis_index("xy")
    w0 = (w0a, w0b, w0c, w0d, w0e)
    w1 = (w1a, w1b, w1c, w1d, w1e)
    w2 = (w2a, w2b, w2c, w2d, w2e)
    w3 = (w3a, w3b, w3c, w3d, w3e)
    b0, s0 = sb0.at[1], sb0.at[0]
    H0, H1, H2, Y3 = 3, 7, 4, 12

    loads = []
    for t in range(4):
        for i, (src, dst) in enumerate(((den, b0), (rhs, s0))):
            cp = pltpu.make_async_copy(
                src.at[:, :, pl.ds(LN * t, LN)], dst.at[pl.ds(H0, 8), t, pl.ds(H0, 32), :], in_sem.at[i, t]
            )
            cp.start()
            loads.append(cp)

    def clear(ref, zs, ys):
        shape = (zs[1] - zs[0], ref.shape[-3], ys[1] - ys[0], LN)
        if len(ref.shape) == 5:
            for k in range(ref.shape[0]):
                ref[k, zs[0]:zs[1], :, ys[0]:ys[1], :] = jnp.zeros(shape, F32)
        else:
            ref[zs[0]:zs[1], :, ys[0]:ys[1], :] = jnp.zeros(shape, F32)

    for ref, h, z, y, reach in ((sb0, H0, 8, 32, 1), (vb, H0, 8, 32, 1), (b1, H1, 4, 16, 2), (s1, H1, 4, 16, 2),
                                (sub2, H2, 2, 8, 2)):
        top, rows = 2 * h + z, 2 * h + y

        @pl.when(gz < reach)
        def _(ref=ref, h=h, rows=rows):
            clear(ref, (0, h), (0, rows))

        @pl.when(gz >= ng - reach)
        def _(ref=ref, h=h, z=z, top=top, rows=rows):
            clear(ref, (h + z, top), (0, rows))

        @pl.when(xy == 0)
        def _(ref=ref, h=h, top=top):
            clear(ref, (0, top), (0, h))

        @pl.when(xy == nw - 1)
        def _(ref=ref, h=h, y=y, top=top, rows=rows):
            clear(ref, (0, top), (h + y, rows))

    @pl.when(xy < 3)
    def _():
        clear(s3, (0, ng), (0, Y3))

    @pl.when(xy >= nw - 3)
    def _():
        clear(s3, (0, ng), (Y3 + 4, 32))

    for ref in (e3a, e3b):
        clear(ref, (0, 3), (0, 32))
        clear(ref, (3 + ng, 6 + ng), (0, 32))

    def inside(a, b):
        conds = []
        if a:
            conds += [gz + a >= 0, gz + a < ng]
        if b:
            conds += [xy + b >= 0, xy + b < nw]
        return functools.reduce(jnp.logical_and, conds)

    barrier = pltpu.get_barrier_semaphore()

    def reach(start):
        def body(k, c):
            for b in range(-3, 4):
                ok = jnp.logical_and(xy + b >= 0, xy + b < nw)
                if b == 0:
                    ok = jnp.logical_and(ok, k != gz)
                pl.when(ok)(functools.partial(start, k, b))
            return c

        lax.fori_loop(0, ng, body, 0)

    greeted = 0
    for a in (-4, -2, -1, 0, 1, 2, 4):
        for b in (-1, 0, 1):
            if (a, b) != (0, 0):
                ok = inside(a, b)

                @pl.when(ok)
                def _(a=a, b=b):
                    pl.semaphore_signal(barrier, inc=1, device_id=(gz + a, xy + b), device_id_type=MESH)

                greeted = greeted + ok.astype(jnp.int32)
    pl.semaphore_wait(barrier, greeted)
    for cp in loads:
        cp.wait()

    used = [0]

    def exchange(moves):
        copies = []
        for a, b, ref, src, dst in moves:
            i = used[0]
            used[0] += 1
            cp = pltpu.make_async_remote_copy(
                src_ref=ref.at[src], dst_ref=ref.at[dst], send_sem=ssem.at[i], recv_sem=rsem.at[i],
                device_id=(gz + a, xy + b), device_id_type=MESH,
            )

            @pl.when(inside(a, b))
            def _(cp=cp):
                cp.start()

            copies.append((a, b, cp))

        def wait_recv():
            for a, b, cp in copies:
                @pl.when(inside(-a, -b))
                def _(cp=cp):
                    cp.wait_recv()

        def wait_send():
            for a, b, cp in copies:
                @pl.when(inside(a, b))
                def _(cp=cp):
                    cp.wait_send()

        return wait_recv, wait_send

    def span(shift, own, h, lo_skip, width):
        if shift == 0:
            return h, h + own
        if shift > 0:
            return max(h - width, h - shift * own), min(h - lo_skip, h - (shift - 1) * own)
        return max(h + own + lo_skip, h - shift * own), min(h + own + width, h + (1 - shift) * own)

    def move(ref, a, b, own, h, wz, wy, lead=(), skip=0):
        z0, z1 = span(a, own[0], h, skip if b == 0 else 0, wz)
        y0, y1 = span(b, own[1], h, skip if a == 0 else 0, wy)
        dst = lead + (pl.ds(z0, z1 - z0), slice(None), pl.ds(y0, y1 - y0), slice(None))
        src = lead + (pl.ds(z0 + a * own[0], z1 - z0), slice(None), pl.ds(y0 + b * own[1], y1 - y0), slice(None))
        return (a, b, ref, src, dst)

    all2 = (slice(None),)
    o0, o1, o2 = (8, 32), (4, 16), (2, 8)
    signs = (-1, 1)
    moves = [move(sb0, a, 0, o0, H0, 3, 0, (1,)) for a in signs]
    moves += [move(sb0, 0, b, o0, H0, 0, 3, all2) for b in signs]
    moves += [move(sb0, a, b, o0, H0, 2, 2, all2) for a in signs for b in signs]
    got0, sent0 = exchange(moves)
    gots0, sents0 = exchange([move(sb0, a, 0, o0, H0, 2, 0, (0,)) for a in signs])

    coarsen(b0, b1, H0, H0, H1, H1, 4, 16, 1.0)
    moves = [move(b1, 0, b, o1, H1, 0, 7) for b in signs]
    moves += [move(b1, a, b, o1, H1, 7, 6) for a in signs for b in signs]
    moves += [move(b1, a, b, o1, H1, 6, 2) for a in (-2, 2) for b in signs]
    gotb1, sentb1 = exchange(moves)
    coarsen(b1, b2, H1, H1, H2, H2, 2, 8, 1.0)
    coarsen(b2, own3.at[1], H2, H2, 0, 0, 1, 4, 1.0)

    got0()
    weights(b0, w0, (1, 13), (1, 37), nx)
    gots0()
    gotz1, sentz1 = exchange([move(b1, a, 0, o1, H1, 7, 0) for a in (-1, 1, -2, 2)])
    first_sweep(s0, va, w0, (1, 13), (1, 37))
    sweep(va, vb, w0, s0, (3, 11), (2, 36))
    sweep(va, vb, w0, s0, (2, 3), (3, 35))
    sweep(va, vb, w0, s0, (11, 12), (3, 35))
    defect(vb, vc, w0, s0, (3, 11), (3, 35))
    coarsen(vc, s1, H0, H0, H1, H1, 4, 16, 4.0)

    moves = [move(s1, a, 0, o1, H1, 6, 0) for a in (-1, 1)]
    moves += [move(s1, a, b, o1, H1, 6, 5) for a in signs for b in signs]
    moves += [move(s1, a, b, o1, H1, 5, 1) for a in (-2, 2) for b in signs]
    moves += [move(s1, a, 0, o1, H1, 6, 0) for a in (-2, 2)]
    moves += [move(s1, 0, b, o1, H1, 0, 6) for b in signs]
    gots1, sents1 = exchange(moves)

    moves = [move(vb, a, 0, o0, H0, 3, 0, skip=1) for a in signs]
    moves += [move(vb, 0, b, o0, H0, 0, 3, skip=1) for b in signs]
    moves += [move(vb, a, b, o0, H0, 2, 2) for a in signs for b in signs]
    gotu0, sentu0 = exchange(moves)
    sent0()
    sents0()
    sentb1()
    sentz1()
    gotb1()
    gotz1()
    weights(b1, w1, (1, 17), (1, 29), nx // 2)
    coarsen(b1, b2, 1, 1, 1, 1, 8, 14, 1.0)
    weights(b2, w2, (2, 8), (2, 14), nx // 4)

    gots1()

    first_sweep(s1, v1a, w1, (1, 17), (1, 29))
    sweep(v1a, v1b, w1, s1, (2, 16), (2, 28))
    defect(v1b, v1c, w1, s1, (3, 15), (3, 27))
    coarsen(v1c, s2, 3, 3, 2, 2, 6, 12, 4.0)
    first_sweep(s2, v2a, w2, (2, 8), (2, 14))
    sweep(v2a, v2b, w2, s2, (3, 7), (3, 13))
    defect(v2b, v2c, w2, s2, (4, 6), (4, 12))
    coarsen(v2c, own3.at[0], H2, H2, 0, 0, 1, 4, 4.0)

    mine = own3[0, 0, 0]
    own3[2, 0, 0] = jnp.where(lane_of(mine) < LN // 2, mine, pltpu.roll(own3[1, 0, 0], LN // 2, axis=1))
    s3[gz, :, pl.ds(Y3, 4), :] = own3[2, 0]
    sides = (0, 1, -1, 2, -2, 3, -3)

    def send3(k, b):
        pltpu.make_async_remote_copy(
            src_ref=own3.at[2, 0], dst_ref=s3.at[gz, :, pl.ds(Y3 - 4 * b, 4), :], send_sem=gsem.at[b + 3],
            recv_sem=grsem.at[b + 3], device_id=(k, xy + b), device_id_type=MESH,
        ).start()

    reach(send3)

    def wait3(sems, sign):
        for b in sides:
            part = s3.at[pl.ds(0, ng - 1 if b == 0 else ng), :, pl.ds(Y3 - 4 * b, 4), :]

            @pl.when(jnp.logical_and(xy + sign * b >= 0, xy + sign * b < nw))
            def _(b=b, part=part):
                pltpu.make_async_copy(part, part, sems.at[b + 3]).wait()

    gots3, sents3 = lambda: wait3(grsem, -1), lambda: wait3(gsem, 1)

    for i, ref in enumerate((b2, s2, v2b)):
        sub2[i, pl.ds(H2, 2), :, pl.ds(H2, 8), :] = ref[pl.ds(H2, 2), :, pl.ds(H2, 8), :]
    moves = [move(sub2, a, b, o2, H2, 4, 4, all2) for a in range(-2, 3) for b in (-1, 0, 1) if (a, b) != (0, 0)]
    gotsub, sentsub = exchange(moves)

    sents1()
    sentu0()
    sents3()
    gots3()
    v = s3[:, 0, pl.ds(0, 28), :]
    low = lane_of(v) < LN // 2
    b3[:, 0, pl.ds(0, 28), :] = jnp.where(low, pltpu.roll(v, LN // 2, axis=2), 0.0)
    s3[:, 0, pl.ds(0, 28), :] = jnp.where(low, v, 0.0)
    R = (2, 26)
    n = R[1] - R[0]
    v = b3[:, 0, pl.ds(R[0], n), :]
    x = lane_of(v)
    zero = jnp.zeros((1, n, LN), F32)
    up = jnp.where(x >= nx // 8 - 1, 0.0, pltpu.roll(v, LN - 1, axis=2))
    down = jnp.where(x == 0, 0.0, pltpu.roll(v, 1, axis=2))
    above = jnp.concatenate([v[1:], zero], axis=0)
    below = jnp.concatenate([zero, v[:-1]], axis=0)
    north, south = b3[:, 0, pl.ds(R[0] + 1, n), :], b3[:, 0, pl.ds(R[0] - 1, n), :]
    w3a[:, pl.ds(R[0], n), :] = jnp.where(x >= nx // 8 - 1, 0.0, 0.5 * (v + up))
    w3b[:, pl.ds(R[0], n), :] = 0.5 * (v + north)
    w3e[:, pl.ds(R[0], n), :] = 0.5 * (v + south)
    w3c[pl.ds(1, ng), pl.ds(R[0], n), :] = 0.5 * (v + above)
    w3c[pl.ds(0, 1), pl.ds(R[0], n), :] = zero
    total = 3.0 * v + 0.5 * ((up + down) + (north + south) + (above + below))
    w3d[:, pl.ds(R[0], n), :] = jnp.where(v > 0.0, 0.8 / total, 0.0)
    e3a[pl.ds(3, ng), 0, pl.ds(R[0], n), :] = w3d[:, pl.ds(R[0], n), :] * s3[:, 0, pl.ds(R[0], n), :]
    a, out = e3a, e3b
    for lo, n in ((3, 22), (3, 22), (6, 16), (6, 16), (6, 16), (6, 16), (10, 8)):
        rows = pl.ds(lo, n)
        v = a[pl.ds(3, ng), 0, rows, :]
        wx = w3a[:, rows, :]
        acc = wx * pltpu.roll(v, LN - 1, axis=2) + pltpu.roll(wx * v, 1, axis=2)
        acc += w3b[:, rows, :] * a[pl.ds(3, ng), 0, pl.ds(lo + 1, n), :]
        acc += w3e[:, rows, :] * a[pl.ds(3, ng), 0, pl.ds(lo - 1, n), :]
        acc += w3c[pl.ds(1, ng), rows, :] * a[pl.ds(4, ng), 0, rows, :]
        acc += w3c[pl.ds(0, ng), rows, :] * a[pl.ds(2, ng), 0, rows, :]
        out[pl.ds(3, ng), 0, rows, :] = 0.2 * v + w3d[:, rows, :] * (s3[:, 0, rows, :] + acc)
        a, out = out, a

    gotsub()
    weights(sub2.at[0], w2, (1, 9), (1, 15), nx // 4)
    spread(a, pe2, gz + 1, 10, 0, 0, 5, 8, 1)
    add_spread(sub2.at[2], pe2, v2a, 0, 10, (0, 16))
    sweep(v2a, v2b, w2, sub2.at[1], (1, 9), (1, 15))
    sweep(v2b, v2a, w2, sub2.at[1], (2, 8), (2, 14))

    spread(v2a, pe1, 2, 2, 0, 3, 6, 12, 2)
    add_spread(v1b, pe1, v1a, 3, 12, (3, 27))
    sweep(v1a, v1c, w1, s1, (4, 14), (4, 26))
    sweep(v1c, v1a, w1, s1, (5, 13), (5, 25))

    spread(v1a, pe0, 5, 5, 0, 0, 8, 20, 4)
    gotu0()

    def add0(fine):
        def body(k):
            todo = []
            for y in windows(0, 38):
                p = pe0[k, :, pl.ds(y + 1, 8), :]
                for i in fine:
                    at = (2 * k + i, slice(None), pl.ds(y, 8), slice(None))
                    todo.append((va, at, vb[at] + p))
            return todo

        return body

    planes((0, 1), add0((0,)), 4)
    planes((1, 7), add0((-1, 0)), 4)
    planes((7, 8), add0((-1,)), 4)
    sweep(va, vc, w0, s0, (1, 13), (1, 37))
    sweep(vc, va, w0, s0, (2, 12), (2, 36))

    def keep(z):
        own = (slice(None), pl.ds(H0, 32), slice(None))
        return [(p_out, (z - H0,), va[(z,) + own])]

    planes((H0, H0 + 8), keep, 4)
    defect(va, r_out, w0, s0, (3, 11), (3, 35), H0)
    sentsub()


def solution(mesh):
    ng, nw = mesh.shape["gz"], mesh.shape["xy"]

    def block(rhs, den):
        nx = rhs.shape[2]
        f0 = pltpu.VMEM((14, 4, 40, LN), F32)
        f1 = pltpu.VMEM((18, 2, 32, LN), F32)
        f2 = pltpu.VMEM((10, 1, 16, LN), F32)
        g3 = pltpu.VMEM((ng, 1, 32, LN), F32)
        w3 = pltpu.VMEM((ng, 32, LN), F32)
        out = pl.pallas_call(
            functools.partial(kernel, ng, nw, nx),
            out_shape=[jax.ShapeDtypeStruct((8, 4, 32, LN), F32)] * 2,
            in_specs=[pl.BlockSpec(memory_space=pl.ANY)] * 2,
            out_specs=[pl.BlockSpec(memory_space=pltpu.VMEM)] * 2,
            scratch_shapes=[pltpu.VMEM((2, 14, 4, 40, LN), F32)] + [f0] * 8 + [pltpu.VMEM((8, 4, 48, LN), F32)]
            + [f1] * 10 + [pltpu.VMEM((6, 2, 32, LN), F32)]
            + [pltpu.VMEM((3, 10, 1, 16, LN), F32)] + [f2] * 10 + [pltpu.VMEM((5, 1, 24, LN), F32)]
            + [pltpu.VMEM((3, 1, 1, 4, LN), F32), g3, g3, w3, w3, pltpu.VMEM((ng + 1, 32, LN), F32), w3, w3]
            + [pltpu.VMEM((ng + 6, 1, 32, LN), F32)] * 2
            + [pltpu.SemaphoreType.DMA((2, 4))]
            + [pltpu.SemaphoreType.DMA((64,))] * 2
            + [pltpu.SemaphoreType.DMA((7,))] * 2,
            compiler_params=pltpu.CompilerParams(
                collective_id=0, has_side_effects=True, vmem_limit_bytes=50 * 2**20
            ),
        )(*(pltpu.with_memory_space_constraint(x, pltpu.HBM) for x in (rhs, den)))

        def place(p_ref, r_ref, p_hbm, r_hbm, sem):
            copies = [
                pltpu.make_async_copy(src.at[:, t], dst.at[:, :, pl.ds(LN * t, LN)], sem.at[k, t])
                for k, (src, dst) in enumerate(((p_ref, p_hbm), (r_ref, r_hbm)))
                for t in range(4)
            ]
            for cp in copies:
                cp.start()
            for cp in copies:
                cp.wait()

        return pl.pallas_call(
            place,
            out_shape=[jax.ShapeDtypeStruct(rhs.shape, F32)] * 2,
            in_specs=[pl.BlockSpec(memory_space=pltpu.VMEM)] * 2,
            out_specs=[pl.BlockSpec(memory_space=pl.ANY)] * 2,
            scratch_shapes=[pltpu.SemaphoreType.DMA((2, 4))],
            compiler_params=pltpu.CompilerParams(vmem_limit_bytes=8 * 2**20),
        )(*out)

    spec = P("gz", "xy", None)
    return jax.shard_map(block, mesh=mesh, in_specs=(spec, spec), out_specs=(spec, spec), check_vma=False)
```

```python
import functools

import jax
import jax.numpy as jnp
from jax import lax
from jax.experimental import pallas as pl
from jax.experimental.pallas import tpu as pltpu
from jax.sharding import PartitionSpec as P

MESH = pl.DeviceIdType.MESH
F32 = jnp.float32
LN = 128


def windows(lo, hi, rows=8):
    starts = list(range(lo, hi - rows + 1, rows))
    if starts[-1] + rows < hi:
        starts.append(hi - rows)
    return starts


def lane_of(v):
    return lax.broadcasted_iota(jnp.int32, v.shape, v.ndim - 1)


def next_x(v):
    r = pltpu.roll(v, LN - 1, axis=2)
    if v.shape[0] == 1:
        return r
    carry = jnp.concatenate([r[1:], r[:1]], axis=0)
    return jnp.where(lane_of(v) == LN - 1, carry, r)


def prev_x(v):
    r = pltpu.roll(v, 1, axis=2)
    if v.shape[0] == 1:
        return r
    carry = jnp.concatenate([r[-1:], r[:-1]], axis=0)
    return jnp.where(lane_of(v) == 0, carry, r)


def x_index(v):
    tile = lax.broadcasted_iota(jnp.int32, v.shape, 0)
    return tile * LN + lane_of(v)


def neighbour_sum(a, w, z, y, n):
    wx, wy, wz = w[0], w[1], w[2]
    ys = pl.ds(y, n)
    v = a[z, :, ys, :]
    wxc = wx[z, :, ys, :]
    acc = wxc * next_x(v) + prev_x(wxc * v)
    acc += wy[z, :, ys, :] * a[z, :, pl.ds(y + 1, n), :]
    acc += wy[z, :, pl.ds(y - 1, n), :] * a[z, :, pl.ds(y - 1, n), :]
    acc += wz[z, :, ys, :] * a[z + 1, :, ys, :]
    acc += wz[z - 1, :, ys, :] * a[z - 1, :, ys, :]
    return v, acc


PLANES = {4: 14, 2: 16, 1: 16}


def planes(zs, body, tiles):
    n = zs[1] - zs[0]
    u = max(u for u in range(1, PLANES[tiles] + 1) if n % u == 0)

    def run(z0, k):
        todo = []
        for i in range(k):
            todo += body(z0 + i)
        for ref, index, value in todo:
            ref[index] = value

    if n // u > 1:
        def step(k, c):
            run(zs[0] + k * u, u)
            return c

        lax.fori_loop(0, n // u, step, 0)
    else:
        run(zs[0], u)


def sweep(a, out, w, s, zs, yr):
    def body(z):
        todo = []
        for y in windows(*yr):
            v, acc = neighbour_sum(a, w, z, y, 8)
            at = (z, slice(None), pl.ds(y, 8), slice(None))
            todo.append((out, at, 0.2 * v + w[3][at] * (s[at] + acc)))
        return todo

    planes(zs, body, a.shape[1])


def defect(a, out, w, s, zs, yr, shift=0):
    def body(z):
        todo = []
        for y in windows(*yr):
            v, acc = neighbour_sum(a, w, z, y, 8)
            at = (z, slice(None), pl.ds(y, 8), slice(None))
            to = (z - shift, slice(None), pl.ds(y - shift, 8), slice(None))
            todo.append((out, to, s[at] + (acc - w[4][at] * v)))
        return todo

    planes(zs, body, a.shape[1])


def weights(b, w, zs, yr, nx):
    wx, wy, wz, d, tot = w

    def body(z):
        todo = []
        for y in windows(yr[0] - 1, yr[1]):
            at = (z, slice(None), pl.ds(y, 8), slice(None))
            todo.append((wy, at, 0.5 * (b[at] + b[z, :, pl.ds(y + 1, 8), :])))
        for y in windows(*yr):
            ys = pl.ds(y, 8)
            at = (z, slice(None), ys, slice(None))
            v = b[at]
            x = x_index(v)
            up = jnp.where(x >= nx - 1, 0.0, next_x(v))
            down = jnp.where(x == 0, 0.0, prev_x(v))
            above = b[z + 1, :, ys, :]
            todo.append((wx, at, jnp.where(x >= nx - 1, 0.0, 0.5 * (v + up))))
            todo.append((wz, at, 0.5 * (v + above)))
            beside = b[z, :, pl.ds(y + 1, 8), :] + b[z, :, pl.ds(y - 1, 8), :]
            total = 3.0 * v + 0.5 * ((up + down) + beside + (above + b[z - 1, :, ys, :]))
            todo.append((tot, at, total))
            todo.append((d, at, jnp.where(v > 0.0, 0.8 / total, 0.0)))
        return todo

    planes(zs, body, b.shape[1])
    z = zs[0] - 1
    for y in windows(*yr):
        ys = pl.ds(y, 8)
        wz[z, :, ys, :] = 0.5 * (b[z, :, ys, :] + b[z + 1, :, ys, :])


def first_sweep(s, out, w, zs, yr):
    def body(z):
        todo = []
        for y in windows(*yr):
            at = (z, slice(None), pl.ds(y, 8), slice(None))
            todo.append((out, at, w[3][at] * s[at]))
        return todo

    planes(zs, body, s.shape[1])


def take(v, index):
    flat = v.reshape(-1, LN)
    return jnp.take_along_axis(flat, index(lax.broadcasted_iota(jnp.int32, flat.shape, 1)), axis=1).reshape(v.shape)


def coarsen(f, out, z_f, y_f, z_c, y_c, nz, ny, scale):
    rows = min(ny, 8)

    def body(k):
        todo = []
        for y in windows(0, ny, rows):
            even = pl.ds(y_f + 2 * y, rows, stride=2)
            odd = pl.ds(y_f + 2 * y + 1, rows, stride=2)
            z = z_f + 2 * k
            v = (f[z, :, even, :] + f[z, :, odd, :]) + (f[z + 1, :, even, :] + f[z + 1, :, odd, :])
            if scale != 1.0:
                v = v * scale
            v = v + pltpu.roll(v, LN - 1, axis=2)
            g = take(v, lambda j: lax.rem(2 * j, LN))
            low = lax.broadcasted_iota(jnp.int32, (rows, LN), 1) < LN // 2
            tiles = v.shape[0]
            for t in range(max(1, tiles // 2)):
                high = g[2 * t + 1] if tiles > 1 else jnp.zeros((rows, LN), F32)
                todo.append((out, (z_c + k, t, pl.ds(y_c + y, rows), slice(None)), jnp.where(low, g[2 * t], high)))
        return todo

    planes((0, nz), body, max(1, f.shape[1] // 2))


def spread(e, out, z_c, y_c, z_o, y_o, nz, ny, tiles):
    def body(k):
        todo = []
        for y in windows(0, ny):
            v = e[z_c + k, :, pl.ds(y_c + y, 8), :]
            parts = [take(v, lambda j: j // 2)]
            if tiles > 1:
                parts.append(take(v, lambda j: LN // 2 + j // 2))
            for t in range(tiles):
                for i in range(2):
                    at = (z_o + k, t, pl.ds(y_o + 2 * y + i, 8, stride=2), slice(None))
                    todo.append((out, at, parts[t % 2][t // 2]))
        return todo

    planes((0, nz), body, max(1, tiles // 2))


def add_spread(u, pe, out, z0, nz, yr):
    def body(k):
        todo = []
        for y in windows(*yr):
            ys = pl.ds(y, 8)
            p = pe[k, :, ys, :]
            for i in range(2):
                at = (z0 + 2 * k + i, slice(None), ys, slice(None))
                todo.append((out, at, u[at] + p))
        return todo

    planes((0, nz // 2), body, u.shape[1])


def kernel(ng, nw, nx, rhs, den, p_out, r_out,
           sb0, w0a, w0b, w0c, w0d, w0e, va, vb, vc, pe0,
           b1, s1, w1a, w1b, w1c, w1d, w1e, v1a, v1b, v1c, pe1,
           sub2, b2, s2, w2a, w2b, w2c, w2d, w2e, v2a, v2b, v2c, pe2,
           own3, b3, s3, w3a, w3b, w3c, w3d, w3e, e3a, e3b,
           in_sem, ssem, rsem, gsem, grsem):
    gz, xy = lax.axis_index("gz"), lax.axis_index("xy")
    w0 = (w0a, w0b, w0c, w0d, w0e)
    w1 = (w1a, w1b, w1c, w1d, w1e)
    w2 = (w2a, w2b, w2c, w2d, w2e)
    w3 = (w3a, w3b, w3c, w3d, w3e)
    b0, s0 = sb0.at[1], sb0.at[0]
    H0, H1, H2, Y3 = 3, 7, 4, 12

    loads = []
    for t in range(4):
        for i, (src, dst) in enumerate(((den, b0), (rhs, s0))):
            cp = pltpu.make_async_copy(
                src.at[:, :, pl.ds(LN * t, LN)], dst.at[pl.ds(H0, 8), t, pl.ds(H0, 32), :], in_sem.at[i, t]
            )
            cp.start()
            loads.append(cp)

    def clear(ref, zs, ys):
        shape = (zs[1] - zs[0], ref.shape[-3], ys[1] - ys[0], LN)
        if len(ref.shape) == 5:
            for k in range(ref.shape[0]):
                ref[k, zs[0]:zs[1], :, ys[0]:ys[1], :] = jnp.zeros(shape, F32)
        else:
            ref[zs[0]:zs[1], :, ys[0]:ys[1], :] = jnp.zeros(shape, F32)

    for ref, h, z, y, reach in ((sb0, H0, 8, 32, 1), (vb, H0, 8, 32, 1), (b1, H1, 4, 16, 2), (s1, H1, 4, 16, 2),
                                (sub2, H2, 2, 8, 2)):
        top, rows = 2 * h + z, 2 * h + y

        @pl.when(gz < reach)
        def _(ref=ref, h=h, rows=rows):
            clear(ref, (0, h), (0, rows))

        @pl.when(gz >= ng - reach)
        def _(ref=ref, h=h, z=z, top=top, rows=rows):
            clear(ref, (h + z, top), (0, rows))

        @pl.when(xy == 0)
        def _(ref=ref, h=h, top=top):
            clear(ref, (0, top), (0, h))

        @pl.when(xy == nw - 1)
        def _(ref=ref, h=h, y=y, top=top, rows=rows):
            clear(ref, (0, top), (h + y, rows))

    @pl.when(xy < 3)
    def _():
        clear(s3, (0, ng), (0, Y3))

    @pl.when(xy >= nw - 3)
    def _():
        clear(s3, (0, ng), (Y3 + 4, 32))

    for ref in (e3a, e3b):
        clear(ref, (0, 3), (0, 32))
        clear(ref, (3 + ng, 6 + ng), (0, 32))

    def inside(a, b):
        conds = []
        if a:
            conds += [gz + a >= 0, gz + a < ng]
        if b:
            conds += [xy + b >= 0, xy + b < nw]
        return functools.reduce(jnp.logical_and, conds)

    barrier = pltpu.get_barrier_semaphore()

    def reach(start):
        def body(k, c):
            for b in range(-3, 4):
                ok = jnp.logical_and(xy + b >= 0, xy + b < nw)
                if b == 0:
                    ok = jnp.logical_and(ok, k != gz)
                pl.when(ok)(functools.partial(start, k, b))
            return c

        lax.fori_loop(0, ng, body, 0)

    greeted = 0
    for a in (-4, -2, -1, 0, 1, 2, 4):
        for b in (-1, 0, 1):
            if (a, b) != (0, 0):
                ok = inside(a, b)

                @pl.when(ok)
                def _(a=a, b=b):
                    pl.semaphore_signal(barrier, inc=1, device_id=(gz + a, xy + b), device_id_type=MESH)

                greeted = greeted + ok.astype(jnp.int32)
    pl.semaphore_wait(barrier, greeted)
    for cp in loads:
        cp.wait()

    used = [0]

    def exchange(moves):
        copies = []
        for a, b, ref, src, dst in moves:
            i = used[0]
            used[0] += 1
            cp = pltpu.make_async_remote_copy(
                src_ref=ref.at[src], dst_ref=ref.at[dst], send_sem=ssem.at[i], recv_sem=rsem.at[i],
                device_id=(gz + a, xy + b), device_id_type=MESH,
            )

            @pl.when(inside(a, b))
            def _(cp=cp):
                cp.start()

            copies.append((a, b, cp))

        def wait_recv():
            for a, b, cp in copies:
                @pl.when(inside(-a, -b))
                def _(cp=cp):
                    cp.wait_recv()

        def wait_send():
            for a, b, cp in copies:
                @pl.when(inside(a, b))
                def _(cp=cp):
                    cp.wait_send()

        return wait_recv, wait_send

    def span(shift, own, h, lo_skip, width):
        if shift == 0:
            return h, h + own
        if shift > 0:
            return max(h - width, h - shift * own), min(h - lo_skip, h - (shift - 1) * own)
        return max(h + own + lo_skip, h - shift * own), min(h + own + width, h + (1 - shift) * own)

    def move(ref, a, b, own, h, wz, wy, lead=(), skip=0):
        z0, z1 = span(a, own[0], h, skip if b == 0 else 0, wz)
        y0, y1 = span(b, own[1], h, skip if a == 0 else 0, wy)
        dst = lead + (pl.ds(z0, z1 - z0), slice(None), pl.ds(y0, y1 - y0), slice(None))
        src = lead + (pl.ds(z0 + a * own[0], z1 - z0), slice(None), pl.ds(y0 + b * own[1], y1 - y0), slice(None))
        return (a, b, ref, src, dst)

    all2 = (slice(None),)
    o0, o1, o2 = (8, 32), (4, 16), (2, 8)
    signs = (-1, 1)
    moves = [move(sb0, a, 0, o0, H0, 3, 0, (1,)) for a in signs]
    moves += [move(sb0, a, b, o0, H0, 2, 2, all2) for a in signs for b in signs]
    moves += [move(sb0, 0, b, o0, H0, 0, 3, all2) for b in signs]
    got0, sent0 = exchange(moves)
    gots0, sents0 = exchange([move(sb0, a, 0, o0, H0, 2, 0, (0,)) for a in signs])

    coarsen(b0, b1, H0, H0, H1, H1, 4, 16, 1.0)
    moves = [move(b1, 0, b, o1, H1, 0, 7) for b in signs]
    moves += [move(b1, a, b, o1, H1, 7, 6) for a in signs for b in signs]
    moves += [move(b1, a, b, o1, H1, 6, 2) for a in (-2, 2) for b in signs]
    gotb1, sentb1 = exchange(moves)
    coarsen(b1, b2, H1, H1, H2, H2, 2, 8, 1.0)
    coarsen(b2, own3.at[1], H2, H2, 0, 0, 1, 4, 1.0)

    got0()
    weights(b0, w0, (1, 13), (1, 37), nx)
    gots0()
    gotz1, sentz1 = exchange([move(b1, a, 0, o1, H1, 7, 0) for a in (-1, 1, -2, 2)])
    first_sweep(s0, va, w0, (1, 13), (1, 37))
    sweep(va, vb, w0, s0, (3, 11), (2, 36))
    sweep(va, vb, w0, s0, (2, 3), (3, 35))
    sweep(va, vb, w0, s0, (11, 12), (3, 35))
    defect(vb, vc, w0, s0, (3, 11), (3, 35))
    coarsen(vc, s1, H0, H0, H1, H1, 4, 16, 4.0)

    moves = [move(s1, a, 0, o1, H1, 6, 0) for a in (-1, 1)]
    moves += [move(s1, a, b, o1, H1, 6, 5) for a in signs for b in signs]
    moves += [move(s1, a, b, o1, H1, 5, 1) for a in (-2, 2) for b in signs]
    moves += [move(s1, a, 0, o1, H1, 6, 0) for a in (-2, 2)]
    moves += [move(s1, 0, b, o1, H1, 0, 6) for b in signs]
    gots1, sents1 = exchange(moves)

    sent0()
    sents0()
    sentb1()
    sentz1()
    gotb1()
    gotz1()
    weights(b1, w1, (1, 17), (1, 29), nx // 2)
    coarsen(b1, b2, 1, 1, 1, 1, 8, 14, 1.0)
    weights(b2, w2, (2, 8), (2, 14), nx // 4)

    moves = [move(vb, a, 0, o0, H0, 3, 0, skip=1) for a in signs]
    moves += [move(vb, 0, b, o0, H0, 0, 3, skip=1) for b in signs]
    moves += [move(vb, a, b, o0, H0, 2, 2) for a in signs for b in signs]
    gotu0, sentu0 = exchange(moves)
    gots1()

    first_sweep(s1, v1a, w1, (1, 17), (1, 29))
    sweep(v1a, v1b, w1, s1, (2, 16), (2, 28))
    defect(v1b, v1c, w1, s1, (3, 15), (3, 27))
    coarsen(v1c, s2, 3, 3, 2, 2, 6, 12, 4.0)
    first_sweep(s2, v2a, w2, (2, 8), (2, 14))
    sweep(v2a, v2b, w2, s2, (3, 7), (3, 13))
    defect(v2b, v2c, w2, s2, (4, 6), (4, 12))
    coarsen(v2c, own3.at[0], H2, H2, 0, 0, 1, 4, 4.0)

    mine = own3[0, 0, 0]
    own3[2, 0, 0] = jnp.where(lane_of(mine) < LN // 2, mine, pltpu.roll(own3[1, 0, 0], LN // 2, axis=1))
    s3[gz, :, pl.ds(Y3, 4), :] = own3[2, 0]
    sides = (0, 1, -1, 2, -2, 3, -3)

    def send3(k, b):
        pltpu.make_async_remote_copy(
            src_ref=own3.at[2, 0], dst_ref=s3.at[gz, :, pl.ds(Y3 - 4 * b, 4), :], send_sem=gsem.at[b + 3],
            recv_sem=grsem.at[b + 3], device_id=(k, xy + b), device_id_type=MESH,
        ).start()

    reach(send3)

    def wait3(sems, sign):
        for b in sides:
            part = s3.at[pl.ds(0, ng - 1 if b == 0 else ng), :, pl.ds(Y3 - 4 * b, 4), :]

            @pl.when(jnp.logical_and(xy + sign * b >= 0, xy + sign * b < nw))
            def _(b=b, part=part):
                pltpu.make_async_copy(part, part, sems.at[b + 3]).wait()

    gots3, sents3 = lambda: wait3(grsem, -1), lambda: wait3(gsem, 1)

    for i, ref in enumerate((b2, s2, v2b)):
        sub2[i, pl.ds(H2, 2), :, pl.ds(H2, 8), :] = ref[pl.ds(H2, 2), :, pl.ds(H2, 8), :]
    moves = [move(sub2, a, b, o2, H2, 4, 4, all2) for a in range(-2, 3) for b in (-1, 0, 1) if (a, b) != (0, 0)]
    gotsub, sentsub = exchange(moves)

    sents1()
    sentu0()
    sents3()
    gots3()
    v = s3[:, 0, pl.ds(0, 28), :]
    low = lane_of(v) < LN // 2
    b3[:, 0, pl.ds(0, 28), :] = jnp.where(low, pltpu.roll(v, LN // 2, axis=2), 0.0)
    s3[:, 0, pl.ds(0, 28), :] = jnp.where(low, v, 0.0)
    R = (2, 26)
    n = R[1] - R[0]
    v = b3[:, 0, pl.ds(R[0], n), :]
    x = lane_of(v)
    zero = jnp.zeros((1, n, LN), F32)
    up = jnp.where(x >= nx // 8 - 1, 0.0, pltpu.roll(v, LN - 1, axis=2))
    down = jnp.where(x == 0, 0.0, pltpu.roll(v, 1, axis=2))
    above = jnp.concatenate([v[1:], zero], axis=0)
    below = jnp.concatenate([zero, v[:-1]], axis=0)
    north, south = b3[:, 0, pl.ds(R[0] + 1, n), :], b3[:, 0, pl.ds(R[0] - 1, n), :]
    w3a[:, pl.ds(R[0], n), :] = jnp.where(x >= nx // 8 - 1, 0.0, 0.5 * (v + up))
    w3b[:, pl.ds(R[0], n), :] = 0.5 * (v + north)
    w3e[:, pl.ds(R[0], n), :] = 0.5 * (v + south)
    w3c[pl.ds(1, ng), pl.ds(R[0], n), :] = 0.5 * (v + above)
    w3c[pl.ds(0, 1), pl.ds(R[0], n), :] = zero
    total = 3.0 * v + 0.5 * ((up + down) + (north + south) + (above + below))
    w3d[:, pl.ds(R[0], n), :] = jnp.where(v > 0.0, 0.8 / total, 0.0)
    e3a[pl.ds(3, ng), 0, pl.ds(R[0], n), :] = w3d[:, pl.ds(R[0], n), :] * s3[:, 0, pl.ds(R[0], n), :]
    a, out = e3a, e3b
    for lo, n in ((3, 22), (3, 22), (6, 16), (6, 16), (6, 16), (6, 16), (10, 8)):
        rows = pl.ds(lo, n)
        v = a[pl.ds(3, ng), 0, rows, :]
        wx = w3a[:, rows, :]
        acc = wx * pltpu.roll(v, LN - 1, axis=2) + pltpu.roll(wx * v, 1, axis=2)
        acc += w3b[:, rows, :] * a[pl.ds(3, ng), 0, pl.ds(lo + 1, n), :]
        acc += w3e[:, rows, :] * a[pl.ds(3, ng), 0, pl.ds(lo - 1, n), :]
        acc += w3c[pl.ds(1, ng), rows, :] * a[pl.ds(4, ng), 0, rows, :]
        acc += w3c[pl.ds(0, ng), rows, :] * a[pl.ds(2, ng), 0, rows, :]
        out[pl.ds(3, ng), 0, rows, :] = 0.2 * v + w3d[:, rows, :] * (s3[:, 0, rows, :] + acc)
        a, out = out, a

    gotsub()
    weights(sub2.at[0], w2, (1, 9), (1, 15), nx // 4)
    spread(a, pe2, gz + 1, 10, 0, 0, 5, 8, 1)
    add_spread(sub2.at[2], pe2, v2a, 0, 10, (0, 16))
    sweep(v2a, v2b, w2, sub2.at[1], (1, 9), (1, 15))
    sweep(v2b, v2a, w2, sub2.at[1], (2, 8), (2, 14))

    spread(v2a, pe1, 2, 2, 0, 3, 6, 12, 2)
    add_spread(v1b, pe1, v1a, 3, 12, (3, 27))
    sweep(v1a, v1c, w1, s1, (4, 14), (4, 26))
    sweep(v1c, v1a, w1, s1, (5, 13), (5, 25))

    spread(v1a, pe0, 5, 5, 0, 0, 8, 20, 4)
    gotu0()

    def add0(fine):
        def body(k):
            todo = []
            for y in windows(0, 38):
                p = pe0[k, :, pl.ds(y + 1, 8), :]
                for i in fine:
                    at = (2 * k + i, slice(None), pl.ds(y, 8), slice(None))
                    todo.append((va, at, vb[at] + p))
            return todo

        return body

    planes((0, 1), add0((0,)), 4)
    planes((1, 7), add0((-1, 0)), 4)
    planes((7, 8), add0((-1,)), 4)
    sweep(va, vc, w0, s0, (1, 13), (1, 37))
    sweep(vc, va, w0, s0, (2, 12), (2, 36))

    def keep(z):
        own = (slice(None), pl.ds(H0, 32), slice(None))
        return [(p_out, (z - H0,), va[(z,) + own])]

    planes((H0, H0 + 8), keep, 4)
    defect(va, r_out, w0, s0, (3, 11), (3, 35), H0)
    sentsub()


def solution(mesh):
    ng, nw = mesh.shape["gz"], mesh.shape["xy"]

    def block(rhs, den):
        nx = rhs.shape[2]
        f0 = pltpu.VMEM((14, 4, 40, LN), F32)
        f1 = pltpu.VMEM((18, 2, 32, LN), F32)
        f2 = pltpu.VMEM((10, 1, 16, LN), F32)
        g3 = pltpu.VMEM((ng, 1, 32, LN), F32)
        w3 = pltpu.VMEM((ng, 32, LN), F32)
        out = pl.pallas_call(
            functools.partial(kernel, ng, nw, nx),
            out_shape=[jax.ShapeDtypeStruct((8, 4, 32, LN), F32)] * 2,
            in_specs=[pl.BlockSpec(memory_space=pl.ANY)] * 2,
            out_specs=[pl.BlockSpec(memory_space=pltpu.VMEM)] * 2,
            scratch_shapes=[pltpu.VMEM((2, 14, 4, 40, LN), F32)] + [f0] * 8 + [pltpu.VMEM((8, 4, 48, LN), F32)]
            + [f1] * 10 + [pltpu.VMEM((6, 2, 32, LN), F32)]
            + [pltpu.VMEM((3, 10, 1, 16, LN), F32)] + [f2] * 10 + [pltpu.VMEM((5, 1, 24, LN), F32)]
            + [pltpu.VMEM((3, 1, 1, 4, LN), F32), g3, g3, w3, w3, pltpu.VMEM((ng + 1, 32, LN), F32), w3, w3]
            + [pltpu.VMEM((ng + 6, 1, 32, LN), F32)] * 2
            + [pltpu.SemaphoreType.DMA((2, 4))]
            + [pltpu.SemaphoreType.DMA((64,))] * 2
            + [pltpu.SemaphoreType.DMA((7,))] * 2,
            compiler_params=pltpu.CompilerParams(
                collective_id=0, has_side_effects=True, vmem_limit_bytes=50 * 2**20
            ),
        )(*(pltpu.with_memory_space_constraint(x, pltpu.HBM) for x in (rhs, den)))

        def place(p_ref, r_ref, p_hbm, r_hbm, sem):
            copies = [
                pltpu.make_async_copy(src.at[:, t], dst.at[:, :, pl.ds(LN * t, LN)], sem.at[k, t])
                for k, (src, dst) in enumerate(((p_ref, p_hbm), (r_ref, r_hbm)))
                for t in range(4)
            ]
            for cp in copies:
                cp.start()
            for cp in copies:
                cp.wait()

        return pl.pallas_call(
            place,
            out_shape=[jax.ShapeDtypeStruct(rhs.shape, F32)] * 2,
            in_specs=[pl.BlockSpec(memory_space=pltpu.VMEM)] * 2,
            out_specs=[pl.BlockSpec(memory_space=pl.ANY)] * 2,
            scratch_shapes=[pltpu.SemaphoreType.DMA((2, 4))],
            compiler_params=pltpu.CompilerParams(vmem_limit_bytes=8 * 2**20),
        )(*out)

    spec = P("gz", "xy", None)
    return jax.shard_map(block, mesh=mesh, in_specs=(spec, spec), out_specs=(spec, spec), check_vma=False)
```
